32 devices in a mesh: batch: 8 (over z, x), tm: 4 (over y, core).
Axes of the slice: x: 2, y: 2, z: 4, core: 2. Of those that a mesh axis runs over, the one named last changes fastest.
Arguments:
- inputs: bfloat16 [96, 256, 25, 128], P('batch', 'tm'), may hold values from -6 to 6
- cotangent: bfloat16 [96, 128, 25, 256], P('batch', 'tm'), may hold values from -6 to 6
- lengths: int32 [96], P('batch'), may hold values from 64 to 256, as said below
- frame_mask: int32 [96, 256], P('batch', 'tm'), may hold values 0 or 1
- subsets: int32 [25, 25], replicated, may hold values from 0 to 3, as said below
- graph_weight: float32 [128, 768], replicated, may hold values from -0.5 to 0.5
- graph_moment: float32 [128, 768], replicated, may hold values from -0.00030517578 to 0.00030517578
- graph_square: float32 [128, 768], replicated, may hold values from 2.0768907e-10 to 8.307563e-10
- graph_average: float32 [128, 768], replicated, may hold values from -0.5 to 0.5
- temporal_weight: float32 [9, 256, 256], replicated, may hold values from -0.125 to 0.125
- temporal_moment: float32 [9, 256, 256], replicated, may hold values from -0.0008544922 to 0.0008544922
- temporal_square: float32 [9, 256, 256], replicated, may hold values from 1.695421e-09 to 6.781684e-09
- temporal_average: float32 [9, 256, 256], replicated, may hold values from -0.125 to 0.125
- shortcut_weight: float32 [128, 256], replicated, may hold values from -0.5 to 0.5
- shortcut_moment: float32 [128, 256], replicated, may hold values from -0.0007324219 to 0.0007324219
- shortcut_square: float32 [128, 256], replicated, may hold values from 1.373291e-09 to 5.493164e-09
- shortcut_average: float32 [128, 256], replicated, may hold values from -0.5 to 0.5
- edge_weight: float32 [3, 25, 25], replicated, may hold values from 0.25 to 1.75
- edge_moment: float32 [3, 25, 25], replicated, may hold values from -0.0012207031 to 0.0012207031
- edge_square: float32 [3, 25, 25], replicated, may hold values from 3.390842e-09 to 1.3563368e-08
- edge_average: float32 [3, 25, 25], replicated, may hold values from 0.25 to 1.75
- norm_params: float32 [6, 256], replicated, may hold values from 0.25 to 1.75
- norm_moment: float32 [6, 256], replicated, may hold values from -0.0007324219 to 0.0007324219
- norm_square: float32 [6, 256], replicated, may hold values from 1.373291e-09 to 5.493164e-09
- norm_average: float32 [6, 256], replicated, may hold values from 0.25 to 1.75
Outputs:
- outputs: bfloat16 [96, 128, 25, 256], P('batch', 'tm')
- input_grad: bfloat16 [96, 256, 25, 128], P('batch', 'tm')
- grad_norm: float32 [1], replicated
- graph_weight_new: float32 [128, 768], replicated
- graph_moment_new: float32 [128, 768], replicated
- graph_square_new: float32 [128, 768], replicated
- graph_average_new: float32 [128, 768], replicated
- temporal_weight_new: float32 [9, 256, 256], replicated
- temporal_moment_new: float32 [9, 256, 256], replicated
- temporal_square_new: float32 [9, 256, 256], replicated
- temporal_average_new: float32 [9, 256, 256], replicated
- shortcut_weight_new: float32 [128, 256], replicated
- shortcut_moment_new: float32 [128, 256], replicated
- shortcut_square_new: float32 [128, 256], replicated
- shortcut_average_new: float32 [128, 256], replicated
- edge_weight_new: float32 [3, 25, 25], replicated
- edge_moment_new: float32 [3, 25, 25], replicated
- edge_square_new: float32 [3, 25, 25], replicated
- edge_average_new: float32 [3, 25, 25], replicated
- norm_params_new: float32 [6, 256], replicated
- norm_moment_new: float32 [6, 256], replicated
- norm_square_new: float32 [6, 256], replicated
- norm_average_new: float32 [6, 256], replicated
The draws below stay inside these ranges and needn't reach their ends.
Inputs may be any that keep to these rules, and one draw needn't show every extreme that they name: `lengths`: clips at even positions have all 256 frames; each other clip has at most 129. `subsets`: A synthetic graph, not a real skeleton: label 1 on the diagonal only; joints whose numbers differ by one are linked, and further pairs are linked at random; a link from v to w has label 2 where w < v and 3 where w > v; 0 means no link; the pattern of links is symmetric.
All inputs are finite; a program needn't handle non-finite values. No bound on the sum of `frame_mask` on one device may be relied on, other than what follows from the above.
Results may differ from the reference program's by a relative error of at most 0.0076.
Values may be sent and summed in bfloat16 or wider, within the bound.
A program may use at most 384 MiB of HBM per device.

```python
import math
import jax
import jax.numpy as jnp
from jax import lax

C_IN = 128
C_OUT = 256
JOINTS = 25
SUBSETS = 3
TAPS = 9
CLIPS_DEV = 12
CLIPS = 96
TOTAL_FRAMES = 256
OUT_FRAMES = 128
N_BATCH = 8


def draw_lengths(key, part):
    shorter = jax.random.randint(key, (CLIPS,), TOTAL_FRAMES // 4, TOTAL_FRAMES // 2 + 2)
    parity = jnp.arange(CLIPS, dtype=jnp.int32) % 2
    return jnp.where(parity == 0, TOTAL_FRAMES, shorter).astype(jnp.int32)


def draw_subsets(key, part):
    rows = jnp.arange(JOINTS, dtype=jnp.int32)[:, None]
    cols = jnp.arange(JOINTS, dtype=jnp.int32)[None, :]
    picks = jax.random.randint(key, (JOINTS, JOINTS), 0, 8)
    picks = jnp.minimum(picks, picks.T)
    linked = (picks < 1) | (jnp.abs(rows - cols) == 1)
    corner = (rows == 0) & (cols == JOINTS - 1) | (rows == JOINTS - 1) & (cols == 0)
    linked = linked & jnp.logical_not(corner)
    labels = jnp.where(cols > rows, 3, 2)
    labels = jnp.where(linked, labels, 0)
    labels = jnp.where(rows == cols, 1, labels)
    return labels.astype(jnp.int32)


def place_ends(entries, key, least, largest):
    shape = entries.shape
    index_at = [jax.random.randint(jax.random.fold_in(key, axis), (), 0, shape[axis]) for axis in range(len(shape))]
    entries = entries.at[tuple(index_at)].set(least)
    longest = shape.index(max(shape))
    index_at[longest] = (index_at[longest] + 1) % shape[longest]
    return entries.at[tuple(index_at)].set(largest)


def steps_of(key, dims, cuts, least, top_value):
    def one(axis_at, blocks):
        draws = jax.random.uniform(jax.random.fold_in(jax.random.fold_in(key, 6), axis_at), (blocks,), jnp.float32, least / len(cuts), top_value / len(cuts))
        return jnp.repeat(jnp.exp(draws), dims[axis_at] // blocks).reshape((-1,) + (1,) * (len(dims) - axis_at - 1))

    level = one(*cuts[0])
    for cut in cuts[1:]:
        level = level * one(*cut)
    return level


def centred(stream_key, extent, width, most, pieces=(), kind=jnp.bfloat16):
    array = width * jax.random.normal(stream_key, extent, jnp.float32)
    if pieces:
        array = array * steps_of(stream_key, extent, pieces, -0.22, 0.18)
    return jnp.clip(array, -most, most).astype(kind)


def setup_inputs(seed: int = 0) -> dict:
    seeds = jax.random.split(jax.random.key(seed), 26)
    return {
        "inputs": centred(seeds[0], (CLIPS, TOTAL_FRAMES, JOINTS, C_IN), 1.0, 6.0, ((0, 8), (1, 4))),
        "cotangent": centred(seeds[1], (CLIPS, OUT_FRAMES, JOINTS, C_OUT), 1.0, 6.0, ((0, 8), (1, 4))),
        "lengths": draw_lengths(jax.random.fold_in(seeds[25], 71), 0),
        "frame_mask": place_ends((jax.random.randint(seeds[3], (CLIPS, TOTAL_FRAMES), 0, 16) < 15).astype(jnp.int32), jax.random.fold_in(seeds[3], 1), 0, 1),
        "subsets": draw_subsets(jax.random.fold_in(seeds[25], 71), 0),
        "graph_weight": centred(seeds[5], (C_IN, SUBSETS * C_OUT), C_IN ** -0.5, 0.5, (), jnp.float32),
        "graph_moment": centred(seeds[6], (C_IN, SUBSETS * C_OUT), (0.11 * 0.35 * (TAPS * C_OUT * C_OUT) ** -0.5), 0.00030517578, (), jnp.float32),
        "graph_square": jnp.clip(jnp.exp(jax.random.uniform(seeds[7], (C_IN, SUBSETS * C_OUT), jnp.float32, math.log(2.0768907427193284e-10), math.log(8.307562970877314e-10))), 2.0768907427193284e-10, 8.307562970877314e-10),
        "graph_average": centred(seeds[8], (C_IN, SUBSETS * C_OUT), C_IN ** -0.5, 0.5, (), jnp.float32),
        "temporal_weight": centred(seeds[9], (TAPS, C_OUT, C_OUT), (TAPS * C_OUT) ** -0.5, 0.125, (), jnp.float32),
        "temporal_moment": centred(seeds[10], (TAPS, C_OUT, C_OUT), (0.11 * (TAPS * C_OUT * C_OUT) ** -0.5), 0.0008544922, (), jnp.float32),
        "temporal_square": jnp.clip(jnp.exp(jax.random.uniform(seeds[11], (TAPS, C_OUT, C_OUT), jnp.float32, math.log(1.6954210257935642e-09), math.log(6.781684103174257e-09))), 1.6954210257935642e-09, 6.781684103174257e-09),
        "temporal_average": centred(seeds[12], (TAPS, C_OUT, C_OUT), (TAPS * C_OUT) ** -0.5, 0.125, (), jnp.float32),
        "shortcut_weight": centred(seeds[13], (C_IN, C_OUT), C_IN ** -0.5, 0.5, (), jnp.float32),
        "shortcut_moment": centred(seeds[14], (C_IN, C_OUT), (0.11 * 0.9 * (TAPS * C_OUT * C_OUT) ** -0.5), 0.0007324219, (), jnp.float32),
        "shortcut_square": jnp.clip(jnp.exp(jax.random.uniform(seeds[15], (C_IN, C_OUT), jnp.float32, math.log(1.3732910364439022e-09), math.log(5.493164145775609e-09))), 1.3732910364439022e-09, 5.493164145775609e-09),
        "shortcut_average": centred(seeds[16], (C_IN, C_OUT), C_IN ** -0.5, 0.5, (), jnp.float32),
        "edge_weight": jnp.clip(1.0 + 0.15 * jax.random.normal(seeds[17], (SUBSETS, JOINTS, JOINTS), jnp.float32), 0.25, 1.75),
        "edge_moment": centred(seeds[18], (SUBSETS, JOINTS, JOINTS), (0.11 * 1.4 * (TAPS * C_OUT * C_OUT) ** -0.5), 0.0012207031, (), jnp.float32),
        "edge_square": jnp.clip(jnp.exp(jax.random.uniform(seeds[19], (SUBSETS, JOINTS, JOINTS), jnp.float32, math.log(3.3908420515871285e-09), math.log(1.3563368206348514e-08))), 3.3908420515871285e-09, 1.3563368206348514e-08),
        "edge_average": jnp.clip(1.0 + 0.15 * jax.random.normal(seeds[20], (SUBSETS, JOINTS, JOINTS), jnp.float32), 0.25, 1.75),
        "norm_params": jnp.clip(1.0 + 0.15 * jax.random.normal(seeds[21], (6, C_OUT), jnp.float32), 0.25, 1.75),
        "norm_moment": centred(seeds[22], (6, C_OUT), (0.11 * 0.9 * (TAPS * C_OUT * C_OUT) ** -0.5), 0.0007324219, (), jnp.float32),
        "norm_square": jnp.clip(jnp.exp(jax.random.uniform(seeds[23], (6, C_OUT), jnp.float32, math.log(1.3732910364439022e-09), math.log(5.493164145775609e-09))), 1.3732910364439022e-09, 5.493164145775609e-09),
        "norm_average": jnp.clip(1.0 + 0.15 * jax.random.normal(seeds[24], (6, C_OUT), jnp.float32), 0.25, 1.75),
    }


@jax.custom_vjp
def low(v):
    return lax.optimization_barrier(v.astype(jnp.bfloat16)).astype(jnp.float32)

@jax.custom_vjp
def low_back(v):
    return v

def low_keep(v):
    return (low(v), None)

def low_pass(kept, grad):
    return (grad,)

def back_keep(v):
    return (v, None)

def back_low(kept, grad):
    return (low(grad),)
low.defvjp(low_keep, low_pass)
low_back.defvjp(back_keep, back_low)
top_precision = lax.Precision.HIGHEST
norm_epsilon = 1e-05
beta_first = 0.9
beta_second = 0.999
adam_epsilon = 1e-08
clip_limit = 1.0
average_decay = 0.9
rate_matrix = 0.05
rate_small = 0.3
decay_matrix = 0.01
steps_taken = 3.0

def adjacency(subsets):
    linked = (subsets > 0).astype(jnp.float32)
    degree = lax.optimization_barrier(jnp.sum(linked, axis=0))
    labels = jnp.arange(SUBSETS, dtype=jnp.int32) + 1
    chosen = (subsets[None, :, :] == labels[:, None, None]).astype(jnp.float32)
    return chosen / degree[None, None, :]

def batch_norm(values, weight_mask, total_count, scale_gain, bias_shift):
    mean_value = lax.optimization_barrier(jnp.sum(values * weight_mask, axis=(0, 1, 2))) / total_count
    centered = (values - mean_value) * weight_mask
    variance = lax.optimization_barrier(jnp.sum(centered * centered, axis=(0, 1, 2))) / total_count
    normed = (values - mean_value) * lax.rsqrt(variance + norm_epsilon)
    return scale_gain * normed + bias_shift

def forward(inputs_f, graph_w, temporal_w, shortcut_w, edge_w, norm_p, graph_mask, mask_in, mask_out):
    graph_low = low(graph_mask * edge_w)
    weight_low = low(graph_w)

    def graph_part(clip_block):
        mixed_rows = jnp.dot(clip_block.reshape(-1, C_IN), weight_low, preferred_element_type=jnp.float32, precision=top_precision)
        mixed_rows = low_back(low(mixed_rows)).reshape(clip_block.shape[0], clip_block.shape[1], JOINTS, SUBSETS, C_OUT)
        joined = jnp.einsum('ntvkc,kvw->ntwc', mixed_rows, graph_low, precision=top_precision)
        return low_back(joined)
    blocks = inputs_f.reshape(N_BATCH, CLIPS_DEV, TOTAL_FRAMES, JOINTS, C_IN)
    hidden = lax.map(jax.checkpoint(graph_part), blocks).reshape(CLIPS, TOTAL_FRAMES, JOINTS, C_OUT)
    count_in = JOINTS * jnp.sum(mask_in)
    wide_in = mask_in[:, :, None, None]
    first_norm = batch_norm(hidden, wide_in, count_in, norm_p[0], norm_p[1])
    active = low(jax.nn.silu(first_norm) * wide_in)
    padded = jnp.pad(active, ((0, 0), (4, 4), (0, 0), (0, 0)))
    taps_low = low(temporal_w)

    def temporal_part(clip_block):
        running = jnp.zeros((clip_block.shape[0] * OUT_FRAMES * JOINTS, C_OUT), jnp.float32)
        for tap_index in range(TAPS):
            window = clip_block[:, tap_index:tap_index + 2 * OUT_FRAMES:2]
            running = running + jnp.dot(window.reshape(-1, C_OUT), taps_low[tap_index], preferred_element_type=jnp.float32, precision=top_precision)
        return low_back(running).reshape(clip_block.shape[0], OUT_FRAMES, JOINTS, C_OUT)
    padded_blocks = padded.reshape(N_BATCH, CLIPS_DEV, TOTAL_FRAMES + 8, JOINTS, C_OUT)
    conv_out = lax.map(jax.checkpoint(temporal_part), padded_blocks).reshape(CLIPS, OUT_FRAMES, JOINTS, C_OUT)
    short_low = low(shortcut_w)
    even_inputs = inputs_f[:, ::2].reshape(-1, C_IN)
    short_out = low_back(jnp.dot(even_inputs, short_low, preferred_element_type=jnp.float32, precision=top_precision))
    short_out = short_out.reshape(CLIPS, OUT_FRAMES, JOINTS, C_OUT)
    count_out = JOINTS * jnp.sum(mask_out)
    wide_out = mask_out[:, :, None, None]
    summed = batch_norm(conv_out, wide_out, count_out, norm_p[2], norm_p[3]) + batch_norm(short_out, wide_out, count_out, norm_p[4], norm_p[5])
    return jax.nn.silu(summed) * wide_out

def adam_update(weight, moment, square, average, gradient, factor, rate, decay, fix_first, fix_second):
    clipped = gradient * factor
    moment_new = beta_first * moment + (1.0 - beta_first) * clipped
    square_new = beta_second * square + (1.0 - beta_second) * clipped * clipped
    stepped = moment_new / fix_first / (jnp.sqrt(square_new / fix_second) + adam_epsilon)
    weight_new = weight - rate * (stepped + decay * weight)
    average_new = average_decay * average + (1.0 - average_decay) * weight_new
    return (weight_new, moment_new, square_new, average_new)

def reference(inputs, cotangent, lengths, frame_mask, subsets, graph_weight, graph_moment, graph_square, graph_average, temporal_weight, temporal_moment, temporal_square, temporal_average, shortcut_weight, shortcut_moment, shortcut_square, shortcut_average, edge_weight, edge_moment, edge_square, edge_average, norm_params, norm_moment, norm_square, norm_average):
    frame_ids = jnp.arange(TOTAL_FRAMES, dtype=jnp.int32)
    mask_in = ((frame_ids[None, :] < lengths[:, None]) & (frame_mask > 0)).astype(jnp.float32)
    mask_out = mask_in[:, ::2]
    graph_mask = adjacency(subsets)

    def closed(inputs_f, graph_w, temporal_w, shortcut_w, edge_w, norm_p):
        return forward(inputs_f, graph_w, temporal_w, shortcut_w, edge_w, norm_p, graph_mask, mask_in, mask_out)
    result, pullback = jax.vjp(closed, inputs.astype(jnp.float32), graph_weight, temporal_weight, shortcut_weight, edge_weight, norm_params)
    gradients = pullback(cotangent.astype(jnp.float32))
    weight_grads = gradients[1:]
    squares_total = sum((jnp.sum(gradient * gradient) for gradient in weight_grads))
    norm_total = jnp.sqrt(squares_total)
    factor = jnp.minimum(1.0, clip_limit / (norm_total + 1e-06))
    fix_first = 1.0 - beta_first ** steps_taken
    fix_second = 1.0 - beta_second ** steps_taken
    graph_new = adam_update(graph_weight, graph_moment, graph_square, graph_average, weight_grads[0], factor, rate_matrix, decay_matrix, fix_first, fix_second)
    temporal_new = adam_update(temporal_weight, temporal_moment, temporal_square, temporal_average, weight_grads[1], factor, rate_matrix, decay_matrix, fix_first, fix_second)
    shortcut_new = adam_update(shortcut_weight, shortcut_moment, shortcut_square, shortcut_average, weight_grads[2], factor, rate_matrix, decay_matrix, fix_first, fix_second)
    edge_new = adam_update(edge_weight, edge_moment, edge_square, edge_average, weight_grads[3], factor, rate_small, 0.0, fix_first, fix_second)
    norm_new = adam_update(norm_params, norm_moment, norm_square, norm_average, weight_grads[4], factor, rate_small, 0.0, fix_first, fix_second)
    return (result.astype(jnp.bfloat16), gradients[0].astype(jnp.bfloat16), jnp.reshape(norm_total, (1,)), graph_new[0], graph_new[1], graph_new[2], graph_new[3], temporal_new[0], temporal_new[1], temporal_new[2], temporal_new[3], shortcut_new[0], shortcut_new[1], shortcut_new[2], shortcut_new[3], edge_new[0], edge_new[1], edge_new[2], edge_new[3], norm_new[0], norm_new[1], norm_new[2], norm_new[3])
```

```python
import functools

import jax
import jax.numpy as jnp
from jax import lax
from jax.experimental import pallas as pl
from jax.experimental.pallas import tpu as pltpu
from jax.sharding import PartitionSpec as P

C_IN = 128
C_OUT = 256
JOINTS = 25
SUBSETS = 3
TAPS = 9
GROUP = 8
PHASES = 8
UNITS = 2 * JOINTS
ROWS = UNITS * GROUP
HALF_ROWS = JOINTS * GROUP
HALF = C_IN
CUT = 5

f32 = jnp.float32
bf16 = jnp.bfloat16

norm_epsilon = 1e-05
beta_first = 0.9
beta_second = 0.999
adam_epsilon = 1e-08
clip_limit = 1.0
average_decay = 0.9
rate_matrix = 0.05
rate_small = 0.3
decay_matrix = 0.01
steps_taken = 3.0


def params(**more):
    return pltpu.CompilerParams(
        vmem_limit_bytes=60 * 2**20, dimension_semantics=("arbitrary",), **more
    )


def adjacency(subsets):
    linked = (subsets > 0).astype(f32)
    degree = jnp.sum(linked, axis=0)
    labels = jnp.arange(SUBSETS, dtype=jnp.int32) + 1
    chosen = (subsets[None, :, :] == labels[:, None, None]).astype(f32)
    return chosen / degree[None, None, :]


def adam_update(weight, moment, square, average, gradient, factor, rate, decay):
    fix_first = 1.0 - beta_first**steps_taken
    fix_second = 1.0 - beta_second**steps_taken
    clipped = gradient * factor
    moment_new = beta_first * moment + (1.0 - beta_first) * clipped
    square_new = beta_second * square + (1.0 - beta_second) * clipped * clipped
    stepped = moment_new / fix_first / (jnp.sqrt(square_new / fix_second) + adam_epsilon)
    weight_new = weight - rate * (stepped + decay * weight)
    average_new = average_decay * average + (1.0 - average_decay) * weight_new
    return (weight_new, moment_new, square_new, average_new)


def dot(a, b):
    return jnp.dot(a, b, preferred_element_type=f32)


def dot_nt(a, b):
    return lax.dot_general(a, b, (((1,), (1,)), ((), ())), preferred_element_type=f32)


def dot_tn(a, b):
    return lax.dot_general(a, b, (((0,), (0,)), ((), ())), preferred_element_type=f32)


def fold(values):
    return jnp.sum(values.reshape(-1, GROUP, values.shape[-1]), axis=0)


def first_moments(stats, norm):
    count_in = stats[4:5]
    mean = stats[0:1] / count_in
    rstd = lax.rsqrt(stats[1:2] / count_in - mean * mean + norm_epsilon)
    return mean, rstd, norm[0:1] * rstd, norm[1:2] - norm[0:1] * rstd * mean


def mix_rows(parts, scales, kron_ref, pad_ref):
    wide = jnp.concatenate([part.reshape(HALF_ROWS, C_IN) for part in parts], axis=1)
    pad_ref[0:HALF_ROWS, :] = wide.astype(bf16)
    mixed = dot(kron_ref[...], pad_ref[...])
    sides = []
    for side in range(2):
        lanes = slice(side * HALF, (side + 1) * HALF)
        sides.append(
            jnp.concatenate(
                [
                    parts[side] * scales,
                    mixed[0:HALF_ROWS, lanes].reshape(JOINTS, GROUP, C_IN),
                    mixed[HALF_ROWS : 2 * HALF_ROWS, lanes].reshape(JOINTS, GROUP, C_IN),
                ],
                axis=2,
            )
        )
    return jnp.concatenate(sides, axis=1).reshape(ROWS, SUBSETS * C_IN).astype(bf16)


def graph_forward(
    x_ref, m_ref, kron_ref, own_ref, wg_ref, ws_ref,
    xg_ref, xq_ref, xe_ref, h_ref, st_ref,
    xs, sums, counts,
):
    step = pl.program_id(0)

    @pl.when(step == 0)
    def _():
        sums[...] = jnp.zeros_like(sums)
        counts[...] = jnp.zeros_like(counts)

    for side in range(2):
        for joint in range(JOINTS):
            xs[side, joint] = x_ref[side, joint].astype(f32)
    own = own_ref[...]
    for c in range(PHASES):
        mask = m_ref[0, c]
        parts = [
            xs[side, :, pl.ds(c, GROUP, stride=PHASES), :]
            * mask[side * GROUP : (side + 1) * GROUP][None]
            for side in range(2)
        ]
        xq_ref[0, c, HALF_ROWS:, :] = jnp.zeros((C_OUT - HALF_ROWS, C_OUT), bf16)
        xg = mix_rows(parts, own, kron_ref, xq_ref.at[0, c])
        xg_ref[0, c] = xg
        hidden = dot(xg, wg_ref[...])
        h_ref[0, c] = hidden.astype(bf16)
        sums[0] += fold(hidden)
        sums[1] += fold(hidden * hidden)
        counts[0] += mask
        if c % 2 == 0:
            counts[1] += mask
            even = jnp.concatenate(parts, axis=1).reshape(ROWS, C_IN).astype(bf16)
            xe_ref[0, c // 2] = even
            short = dot(even, ws_ref[...])
            sums[2] += fold(short)
            sums[3] += fold(short * short)

    @pl.when(step == pl.num_programs(0) - 1)
    def _():
        rows = [jnp.sum(sums[k], axis=0, keepdims=True) for k in range(4)]
        for k in range(2):
            total = JOINTS * jnp.sum(counts[k], axis=0, keepdims=True)
            rows.append(jnp.concatenate([total, total], axis=1))
        rows.append(jnp.zeros((2, C_OUT), f32))
        st_ref[...] = jnp.concatenate(rows, axis=0)


def insert_and_roll(tiles, fill, side):
    sub = lax.broadcasted_iota(jnp.int32, tiles.shape, 1)
    joined = jnp.where(sub == side, fill, tiles)
    return pltpu.roll(joined, 1 if side == 7 else GROUP - 1, 1)


def conv_forward(
    h_ref, xh_ref, m_ref, mh_ref, st_ref, norm_ref, kron_ref, own_ref, wg_ref, taps_ref,
    a_ref, conv_ref, out_ref,
    pad, rims, fills, sums,
):
    step = pl.program_id(0)

    @pl.when(step == 0)
    def _():
        sums[...] = jnp.zeros_like(sums)
        pad[...] = jnp.zeros_like(pad)

    _, _, scale, shift = first_moments(st_ref[...], norm_ref[...])
    scale, shift = 0.5 * scale, 0.5 * shift

    def activate(values, mask):
        half = values * scale + shift
        return (half + half * jnp.tanh(half)).reshape(-1, 2 * GROUP, C_OUT) * mask

    def wide(mask):
        return jnp.concatenate([mask, mask], axis=1)[None]

    rim_mask = mh_ref[0]
    parts = [
        xh_ref[side] * rim_mask[side * GROUP : (side + 1) * GROUP][None] for side in range(2)
    ]
    rim_hidden = dot(mix_rows(parts, own_ref[...], kron_ref, pad), wg_ref[...])
    rim_active = activate(rim_hidden, wide(rim_mask)).reshape(ROWS, C_OUT)
    for lane in range(2):
        rims[lane] = rim_active[:, lane * HALF : (lane + 1) * HALF]
    for p in range(2):
        for q in range(2):
            for lane in range(2):
                fills[2 * p + q, lane, pl.ds(7, UNITS, stride=GROUP), :] = rims[
                    lane, pl.ds(2 * q + p, UNITS, stride=GROUP), :
                ]
                fills[2 * p + q, lane, pl.ds(0, UNITS, stride=GROUP), :] = rims[
                    lane, pl.ds(4 + 2 * q + p, UNITS, stride=GROUP), :
                ]

    for c in range(PHASES):
        p, q = c % 2, c // 2
        mask = wide(m_ref[0, c])
        for start in range(0, JOINTS, CUT):
            rows = slice(start * 2 * GROUP, (start + CUT) * 2 * GROUP)
            active = activate(h_ref[0, c, rows, :].astype(f32), mask)
            a_ref[0, p, q + 2, rows, :] = active.reshape(-1, C_OUT).astype(bf16)
            if p == 1 and q == 1:
                continue
            tiles = active.reshape(-1, GROUP, C_OUT)
            fill = jnp.concatenate(
                [fills[2 * p + q % 2, lane, rows, :] for lane in range(2)], axis=1
            ).reshape(-1, GROUP, C_OUT)
            moved = insert_and_roll(tiles, fill, 7 if q >= 2 else 0)
            at = q - 2 if q >= 2 else q + 6
            a_ref[0, p, at, rows, :] = moved.reshape(-1, C_OUT).astype(bf16)

    total = None
    for j in range(TAPS):
        window = a_ref[0, j % 2, j // 2 : j // 2 + 4].reshape(4 * ROWS, C_OUT)
        part = dot(window, taps_ref[j])
        total = part if total is None else total + part
    conv_ref[0] = total.reshape(4, ROWS, C_OUT)
    for q in range(4):
        block = total[q * ROWS : (q + 1) * ROWS].reshape(JOINTS, 2 * GROUP, C_OUT)
        live = block * wide(m_ref[0, 2 * q])
        sums[0] += fold(live)
        sums[1] += fold(live * block)

    @pl.when(step == pl.num_programs(0) - 1)
    def _():
        rows = [jnp.sum(sums[k], axis=0, keepdims=True) for k in range(2)]
        rows.append(jnp.zeros((6, C_OUT), f32))
        out_ref[...] = jnp.concatenate(rows, axis=0)


def second_moments(stats, conv_stats):
    count_out = stats[5:6]
    mean_conv = conv_stats[0:1] / count_out
    rstd_conv = lax.rsqrt(conv_stats[1:2] / count_out - mean_conv * mean_conv + norm_epsilon)
    mean_short = stats[2:3] / count_out
    rstd_short = lax.rsqrt(stats[3:4] / count_out - mean_short * mean_short + norm_epsilon)
    return mean_conv, rstd_conv, mean_short, rstd_short


def output_part(
    conv_ref, xe_ref, cot_ref, m_ref, st_ref, cs_ref, norm_ref, ws_ref,
    o_ref, up_ref, out_ref,
    cots, outs, sums,
):
    step = pl.program_id(0)

    @pl.when(step == 0)
    def _():
        sums[...] = jnp.zeros_like(sums)

    norm = norm_ref[...]
    mean_conv, rstd_conv, mean_short, rstd_short = second_moments(st_ref[...], cs_ref[...])
    scale_conv = 0.5 * norm[2:3] * rstd_conv
    scale_short = 0.5 * norm[4:5] * rstd_short
    shift = 0.5 * (norm[3:4] + norm[5:6]) - scale_conv * mean_conv - scale_short * mean_short
    for side in range(2):
        for joint in range(JOINTS):
            for lane in range(2):
                cots[side, lane, joint] = cot_ref[
                    side, joint, :, lane * HALF : (lane + 1) * HALF
                ].astype(f32)
    for q in range(4):
        mask = m_ref[0, 2 * q]
        mask = jnp.concatenate([mask, mask], axis=1)[None]
        short_all = dot(xe_ref[0, q], ws_ref[...])
        for start in range(0, JOINTS, CUT):
            rows = slice(start * 2 * GROUP, (start + CUT) * 2 * GROUP)
            conv = conv_ref[0, q, rows, :]
            short = short_all[rows]
            half = conv * scale_conv + short * scale_short + shift
            turn = jnp.tanh(half)
            grow = (0.5 + 0.5 * turn).reshape(CUT, 2 * GROUP, C_OUT) * mask
            half = half.reshape(CUT, 2 * GROUP, C_OUT)
            turn = turn.reshape(CUT, 2 * GROUP, C_OUT)
            result = (half + half) * grow
            slope = grow + grow * (half - half * turn)
            cot = jnp.concatenate(
                [
                    jnp.concatenate(
                        [
                            cots[side, lane, start : start + CUT, pl.ds(q, GROUP, stride=4), :]
                            for lane in range(2)
                        ],
                        axis=2,
                    )
                    for side in range(2)
                ],
                axis=1,
            )
            for side in range(2):
                for lane in range(2):
                    outs[side, lane, start : start + CUT, pl.ds(q, GROUP, stride=4), :] = result[
                        :, side * GROUP : (side + 1) * GROUP, lane * HALF : (lane + 1) * HALF
                    ]
            up = (cot * slope).reshape(-1, C_OUT)
            up_ref[0, q, rows, :] = up
            sums[0] += fold(up)
            sums[1] += fold(up * conv)
            sums[2] += fold(up * short)
    for side in range(2):
        for joint in range(JOINTS):
            for lane in range(2):
                o_ref[side, joint, :, lane * HALF : (lane + 1) * HALF] = outs[
                    side, lane, joint
                ].astype(bf16)

    @pl.when(step == pl.num_programs(0) - 1)
    def _():
        rows = [jnp.sum(sums[k], axis=0, keepdims=True) for k in range(3)]
        rows.append(jnp.zeros((5, C_OUT), f32))
        out_ref[...] = jnp.concatenate(rows, axis=0)


def back_totals(back, moments):
    mean_conv, rstd_conv, mean_short, rstd_short = moments
    back_sum = back[0:1]
    back_conv = rstd_conv * (back[1:2] - mean_conv * back_sum)
    back_short = rstd_short * (back[2:3] - mean_short * back_sum)
    return back_sum, back_conv, back_short


def weight_part(
    conv_ref, up_ref, xe_ref, a_ref, m_ref, st_ref, cs_ref, bk_ref, norm_ref, ws_ref,
    cg_ref, sg_ref, lo_ref, hi_ref, tg_ref, shg_ref,
    turned, edges,
):
    step = pl.program_id(0)

    @pl.when(step == 0)
    def _():
        tg_ref[...] = jnp.zeros_like(tg_ref)
        shg_ref[...] = jnp.zeros_like(shg_ref)

    norm = norm_ref[...]
    stats = st_ref[...]
    moments = second_moments(stats, cs_ref[...])
    mean_conv, rstd_conv, mean_short, rstd_short = moments
    back_sum, back_conv, back_short = back_totals(bk_ref[...], moments)
    count_out = stats[5:6]

    def terms(gain, mean, rstd, back):
        lead = gain * rstd
        slope = lead * rstd * back / count_out
        return lead, slope, lead * back_sum / count_out - slope * mean

    lead_c, slope_c, shift_c = terms(norm[2:3], mean_conv, rstd_conv, back_conv)
    lead_s, slope_s, shift_s = terms(norm[4:5], mean_short, rstd_short, back_short)
    for q in range(4):
        mask = m_ref[0, 2 * q]
        mask = jnp.concatenate([mask, mask], axis=1)[None]
        short_all = dot(xe_ref[0, q], ws_ref[...])
        for start in range(0, JOINTS, CUT):
            rows = slice(start * 2 * GROUP, (start + CUT) * 2 * GROUP)
            up = up_ref[0, q, rows, :]

            def masked(values):
                return (values.reshape(CUT, 2 * GROUP, C_OUT) * mask).reshape(-1, C_OUT)

            cg = up * lead_c - masked(conv_ref[0, q, rows, :] * slope_c + shift_c)
            cg_ref[0, q, rows, :] = cg.astype(bf16)
            for lane in range(2):
                edges[lane, rows, :] = cg[:, lane * HALF : (lane + 1) * HALF]
            sg = up * lead_s - masked(short_all[rows] * slope_s + shift_s)
            sg_ref[0, q, rows, :] = sg.astype(bf16)
        for lane in range(2):
            at = slice(lane * HALF, (lane + 1) * HALF)
            if q < 2:
                lo_ref[0, q, :, at] = edges[lane, pl.ds(0, UNITS, stride=GROUP), :].astype(bf16)
            else:
                hi_ref[0, q - 2, :, at] = edges[lane, pl.ds(7, UNITS, stride=GROUP), :].astype(bf16)
    turned[...] = cg_ref[0].reshape(4 * ROWS, C_OUT).T
    for j in range(TAPS):
        window = a_ref[0, j % 2, j // 2 : j // 2 + 4].reshape(4 * ROWS, C_OUT)
        tg_ref[j] += dot(turned[...], window)
    shg_ref[...] += dot_tn(
        xe_ref[0].reshape(4 * ROWS, C_IN), sg_ref[0].reshape(4 * ROWS, C_OUT)
    )


def conv_back(
    cg_ref, left_ref, right_ref, taps_ref, h_ref, m_ref, st_ref, norm_ref,
    fg_ref, out_ref,
    fills, ext, sums,
):
    step = pl.program_id(0)

    @pl.when(step == 0)
    def _():
        sums[...] = jnp.zeros_like(sums)

    _, _, scale, shift = first_moments(st_ref[...], norm_ref[...])
    scale, shift = 0.5 * scale, 0.5 * shift
    for q in range(2):
        for lane in range(2):
            at = slice(lane * HALF, (lane + 1) * HALF)
            fills[q, lane, pl.ds(7, UNITS, stride=GROUP), :] = left_ref[0, q, :, at].astype(f32)
            fills[q, lane, pl.ds(0, UNITS, stride=GROUP), :] = right_ref[0, q, :, at].astype(f32)
    for q in range(4):
        ext[q + 2] = cg_ref[0, q]
        for start in range(0, JOINTS, CUT):
            rows = slice(start * 2 * GROUP, (start + CUT) * 2 * GROUP)
            tiles = cg_ref[0, q, rows, :].astype(f32).reshape(-1, GROUP, C_OUT)
            fill = jnp.concatenate([fills[q % 2, lane, rows, :] for lane in range(2)], axis=1)
            fill = fill.reshape(-1, GROUP, C_OUT)
            moved = insert_and_roll(tiles, fill, 7 if q >= 2 else 0)
            at = q - 2 if q >= 2 else q + 6
            ext[at, rows, :] = moved.reshape(-1, C_OUT).astype(bf16)
    for p in range(2):
        total = None
        for i in range(5 - p):
            window = ext[4 - i : 8 - i].reshape(4 * ROWS, C_OUT)
            part = dot_nt(window, taps_ref[2 * i + p])
            total = part if total is None else total + part
        for q in range(4):
            c = 2 * q + p
            mask = 0.5 * m_ref[0, c]
            mask = jnp.concatenate([mask, mask], axis=1)[None]
            for start in range(0, JOINTS, CUT):
                rows = slice(start * 2 * GROUP, (start + CUT) * 2 * GROUP)
                hidden = h_ref[0, c, rows, :].astype(f32)
                half = hidden * scale + shift
                turn = jnp.tanh(half)
                slope = (1.0 + turn) * (1.0 + (half - half * turn))
                slope = (slope.reshape(CUT, 2 * GROUP, C_OUT) * mask).reshape(-1, C_OUT)
                grad = total[q * ROWS + rows.start : q * ROWS + rows.stop] * slope
                fg_ref[0, c, rows, :] = grad
                sums[0] += fold(grad)
                sums[1] += fold(grad * hidden)

    @pl.when(step == pl.num_programs(0) - 1)
    def _():
        rows = [jnp.sum(sums[k], axis=0, keepdims=True) for k in range(2)]
        rows.append(jnp.zeros((6, C_OUT), f32))
        out_ref[...] = jnp.concatenate(rows, axis=0)


def graph_back(
    fg_ref, h_ref, xg_ref, xq_ref, sg_ref, m_ref, st_ref, fs_ref, norm_ref,
    wg_ref, ws_ref, kront_ref, own_ref,
    ig_ref, gg_ref, eg_ref, own_grad_ref,
    hg_all, spread, natural,
):
    step = pl.program_id(0)

    @pl.when(step == 0)
    def _():
        gg_ref[...] = jnp.zeros_like(gg_ref)
        eg_ref[...] = jnp.zeros_like(eg_ref)
        own_grad_ref[...] = jnp.zeros_like(own_grad_ref)
        spread[...] = jnp.zeros_like(spread)

    norm = norm_ref[...]
    stats = st_ref[...]
    mean, rstd, _, _ = first_moments(stats, norm)
    count_in = stats[4:5]
    back_sum = fs_ref[0:1]
    back_norm = rstd * (fs_ref[1:2] - mean * back_sum)
    lead = norm[0:1] * rstd
    slope = lead * rstd * back_norm / count_in
    shift = lead * back_sum / count_in - slope * mean
    own = own_ref[...]
    for c in range(PHASES):
        mask = m_ref[0, c]
        mask = jnp.concatenate([mask, mask], axis=1)[None]
        for start in range(0, JOINTS, CUT):
            rows = slice(start * 2 * GROUP, (start + CUT) * 2 * GROUP)
            hidden = h_ref[0, c, rows, :].astype(f32)
            taken = ((hidden * slope + shift).reshape(CUT, 2 * GROUP, C_OUT) * mask).reshape(
                -1, C_OUT
            )
            hg_all[c, rows, :] = (fg_ref[0, c, rows, :] * lead - taken).astype(bf16)
        back = dot(hg_all[c], wg_ref[...]).reshape(JOINTS, 2 * GROUP, SUBSETS * C_IN)

        def side_by_side(values):
            return jnp.concatenate([values[:, 0:GROUP], values[:, GROUP : 2 * GROUP]], axis=2)

        for k in range(2):
            lanes = slice((k + 1) * C_IN, (k + 2) * C_IN)
            spread[k, 0:HALF_ROWS, :] = (
                side_by_side(back[:, :, lanes]).reshape(HALF_ROWS, 2 * C_IN).astype(bf16)
            )
        direct = side_by_side(back[:, :, 0:C_IN])
        both = spread[...].reshape(2 * C_OUT, C_OUT)
        whole = dot(kront_ref[...], both)
        result = whole.reshape(JOINTS, GROUP, 2 * C_IN) + direct * jnp.concatenate([own, own], axis=2)
        if c % 2 == 0:
            short = dot(sg_ref[0, c // 2], ws_ref[...]).reshape(JOINTS, 2 * GROUP, C_IN)
            result = result + side_by_side(short)
        for side in range(2):
            natural[side, :, pl.ds(c, GROUP, stride=PHASES), :] = result[
                :, :, side * C_IN : (side + 1) * C_IN
            ]
        eg_ref[...] += dot_nt(both, xq_ref[0, c])
        seen = xq_ref[0, c, 0:HALF_ROWS, :].astype(f32).reshape(JOINTS, GROUP, 2 * C_IN)
        own_grad_ref[...] += seen * direct
    for side in range(2):
        for joint in range(JOINTS):
            ig_ref[side, joint] = natural[side, joint].astype(bf16)
    gg_ref[...] += dot_tn(
        xg_ref[0].reshape(PHASES * ROWS, SUBSETS * C_IN), hg_all[...].reshape(PHASES * ROWS, C_OUT)
    )


def whole_spec(shape):
    return pl.BlockSpec(shape, lambda i: (0,) * len(shape))


def lead_spec(shape):
    return pl.BlockSpec(shape, lambda i: (i,) + (0,) * (len(shape) - 1))


def call(body, pairs, ins, outs, scratch, name):
    in_specs = [
        whole_spec(array.shape) if block is None else lead_spec(block) for array, block in ins
    ]
    out_specs = [whole_spec(shape) if block is None else lead_spec(block) for shape, _, block in outs]
    return pl.pallas_call(
        body,
        grid=(pairs,),
        in_specs=in_specs,
        out_specs=out_specs,
        out_shape=[jax.ShapeDtypeStruct(shape, kind) for shape, kind, _ in outs],
        scratch_shapes=scratch,
        compiler_params=params(),
        name=name,
    )(*[array for array, _ in ins])


def shards(
    inputs, cotangent, lengths, frame_mask, subsets,
    graph_weight, graph_moment, graph_square, graph_average,
    temporal_weight, temporal_moment, temporal_square, temporal_average,
    shortcut_weight, shortcut_moment, shortcut_square, shortcut_average,
    edge_weight, edge_moment, edge_square, edge_average,
    norm_params, norm_moment, norm_square, norm_average,
):
    clips = inputs.shape[0]
    frames = inputs.shape[1]
    pairs = clips // 2
    tm_size = lax.axis_size("tm")
    forward = [(i, i + 1) for i in range(tm_size - 1)]
    backward = [(i + 1, i) for i in range(tm_size - 1)]
    first_frame = lax.axis_index("tm") * frames
    frame_ids = first_frame + jnp.arange(frames, dtype=jnp.int32)
    mask_in = ((frame_ids[None, :] < lengths[:, None]) & (frame_mask > 0)).astype(f32)

    natural = jnp.transpose(inputs, (0, 2, 1, 3))
    before = lax.ppermute(natural[:, :, -4:], "tm", forward)
    after = lax.ppermute(natural[:, :, :4], "tm", backward)
    rim_x = jnp.concatenate([before, after], axis=2).astype(f32)
    mask_before = lax.ppermute(mask_in[:, -4:], "tm", forward)
    mask_after = lax.ppermute(mask_in[:, :4], "tm", backward)
    rim_mask = jnp.concatenate([mask_before, mask_after], axis=1).reshape(pairs, 2 * GROUP)
    rim_mask = jnp.broadcast_to(rim_mask[:, :, None], (pairs, 2 * GROUP, 128))
    masks = mask_in.reshape(pairs, 2, GROUP, PHASES).transpose(0, 3, 1, 2)
    masks = jnp.broadcast_to(
        masks.reshape(pairs, PHASES, 2 * GROUP)[..., None], (pairs, PHASES, 2 * GROUP, 128)
    )

    graph_mask = adjacency(subsets)
    graph_low = (graph_mask * edge_weight).astype(bf16)
    same = jnp.eye(GROUP, dtype=bf16)
    kron = graph_low[1:].transpose(0, 2, 1)[:, :, None, :, None] * same[None, None, :, None, :]
    kron = kron.reshape(2 * HALF_ROWS, HALF_ROWS)
    kron = jnp.pad(kron, ((0, 0), (0, C_OUT - HALF_ROWS)))
    kront = graph_low[1:].transpose(1, 0, 2)[:, None, :, :, None] * same[None, :, None, None, :]
    kront = kront.reshape(HALF_ROWS, 2, HALF_ROWS)
    kront = jnp.pad(kront, ((0, 0), (0, 0), (0, C_OUT - HALF_ROWS))).reshape(HALF_ROWS, 2 * C_OUT)
    own = jnp.diagonal(graph_low[0]).astype(f32)
    own = jnp.broadcast_to(own[:, None, None], (JOINTS, GROUP, C_IN))
    wg = graph_weight.astype(bf16).reshape(C_IN, SUBSETS, C_OUT).transpose(1, 0, 2)
    wg = wg.reshape(SUBSETS * C_IN, C_OUT)
    ws = shortcut_weight.astype(bf16)
    taps = temporal_weight.astype(bf16)

    x_block = (2, JOINTS, frames, C_IN)
    mask_block = (1, PHASES, 2 * GROUP, 128)
    wide_block = (1, PHASES, ROWS, C_OUT)
    out_block = (1, 4, ROWS, C_OUT)
    xe_block = (1, 4, ROWS, C_IN)
    a_block = (1, 2, 8, ROWS, C_OUT)
    rim_block = (1, 2, UNITS, C_OUT)
    small = (8, C_OUT)

    def full(block):
        return (pairs,) + block[1:]

    xg_block = (1, PHASES, ROWS, SUBSETS * C_IN)
    xq_block = (1, PHASES, C_OUT, C_OUT)
    xg, xq, xe, hidden, stats = call(
        graph_forward,
        pairs,
        [(natural, x_block), (masks, mask_block), (kron, None), (own, None), (wg, None), (ws, None)],
        [
            (full(xg_block), bf16, xg_block),
            (full(xq_block), bf16, xq_block),
            (full(xe_block), bf16, xe_block),
            (full(wide_block), bf16, wide_block),
            (small, f32, None),
        ],
        [
            pltpu.VMEM((2, JOINTS, frames, C_IN), f32),
            pltpu.VMEM((4, GROUP, C_OUT), f32),
            pltpu.VMEM((2, 2 * GROUP, 128), f32),
        ],
        "graph_forward",
    )
    stats = lax.psum(stats, ("batch", "tm"))

    active, conv, conv_stats = call(
        conv_forward,
        pairs,
        [
            (hidden, wide_block),
            (rim_x, (2, JOINTS, GROUP, C_IN)),
            (masks, mask_block),
            (rim_mask, (1, 2 * GROUP, 128)),
            (stats, None),
            (norm_params, None),
            (kron, None),
            (own, None),
            (wg, None),
            (taps, None),
        ],
        [
            (full(a_block), bf16, a_block),
            (full(out_block), f32, out_block),
            (small, f32, None),
        ],
        [
            pltpu.VMEM((C_OUT, C_OUT), bf16),
            pltpu.VMEM((2, ROWS, HALF), f32),
            pltpu.VMEM((4, 2, ROWS, HALF), f32),
            pltpu.VMEM((2, GROUP, C_OUT), f32),
        ],
        "conv_forward",
    )
    conv_stats = lax.psum(conv_stats, ("batch", "tm"))

    cot = jnp.transpose(cotangent, (0, 2, 1, 3))
    cot_block = (2, JOINTS, frames // 2, C_OUT)
    outputs, upstream, back = call(
        output_part,
        pairs,
        [
            (conv, out_block),
            (xe, xe_block),
            (cot, cot_block),
            (masks, mask_block),
            (stats, None),
            (conv_stats, None),
            (norm_params, None),
            (ws, None),
        ],
        [
            (cot.shape, bf16, cot_block),
            (full(out_block), f32, out_block),
            (small, f32, None),
        ],
        [
            pltpu.VMEM((2, 2, JOINTS, frames // 2, HALF), f32),
            pltpu.VMEM((2, 2, JOINTS, frames // 2, HALF), f32),
            pltpu.VMEM((3, GROUP, C_OUT), f32),
        ],
        "output_part",
    )
    back = lax.psum(back, ("batch", "tm"))

    conv_grad, short_grad, low_rim, high_rim, temporal_turned, shortcut_grad = call(
        weight_part,
        pairs,
        [
            (conv, out_block),
            (upstream, out_block),
            (xe, xe_block),
            (active, a_block),
            (masks, mask_block),
            (stats, None),
            (conv_stats, None),
            (back, None),
            (norm_params, None),
            (ws, None),
        ],
        [
            (full(out_block), bf16, out_block),
            (full(out_block), bf16, out_block),
            (full(rim_block), bf16, rim_block),
            (full(rim_block), bf16, rim_block),
            ((TAPS, C_OUT, C_OUT), f32, None),
            ((C_IN, C_OUT), f32, None),
        ],
        [
            pltpu.VMEM((C_OUT, 4 * ROWS), bf16),
            pltpu.VMEM((2, ROWS, HALF), f32),
        ],
        "weight_part",
    )
    left_rim = lax.ppermute(high_rim, "tm", forward)
    right_rim = lax.ppermute(low_rim, "tm", backward)

    first_grad, first_sums = call(
        conv_back,
        pairs,
        [
            (conv_grad, out_block),
            (left_rim, rim_block),
            (right_rim, rim_block),
            (taps, None),
            (hidden, wide_block),
            (masks, mask_block),
            (stats, None),
            (norm_params, None),
        ],
        [
            (full(wide_block), f32, wide_block),
            (small, f32, None),
        ],
        [
            pltpu.VMEM((2, 2, ROWS, HALF), f32),
            pltpu.VMEM((8, ROWS, C_OUT), bf16),
            pltpu.VMEM((2, GROUP, C_OUT), f32),
        ],
        "conv_back",
    )
    first_sums = lax.psum(first_sums, ("batch", "tm"))

    input_grad, graph_turned, edge_wide, own_wide = call(
        graph_back,
        pairs,
        [
            (first_grad, wide_block),
            (hidden, wide_block),
            (xg, xg_block),
            (xq, xq_block),
            (short_grad, out_block),
            (masks, mask_block),
            (stats, None),
            (first_sums, None),
            (norm_params, None),
            (wg.T, None),
            (ws.T, None),
            (kront, None),
            (own, None),
        ],
        [
            (natural.shape, bf16, x_block),
            ((SUBSETS * C_IN, C_OUT), f32, None),
            ((2 * C_OUT, C_OUT), f32, None),
            ((JOINTS, GROUP, 2 * C_IN), f32, None),
        ],
        [
            pltpu.VMEM((PHASES, ROWS, C_OUT), bf16),
            pltpu.VMEM((2, C_OUT, C_OUT), bf16),
            pltpu.VMEM((2, JOINTS, frames, C_IN), f32),
        ],
        "graph_back",
    )
    temporal_grad = jnp.swapaxes(temporal_turned, 1, 2)
    graph_grad = graph_turned.reshape(SUBSETS, C_IN, C_OUT).transpose(1, 0, 2)
    graph_grad = graph_grad.reshape(C_IN, SUBSETS * C_OUT)
    edge_wide = edge_wide.reshape(2, C_OUT, C_OUT)[:, :HALF_ROWS, :HALF_ROWS]
    edge_wide = edge_wide.reshape(2, JOINTS, GROUP, JOINTS, GROUP)
    edge_off = jnp.einsum("kwrvr->kvw", edge_wide)
    edge_own = jnp.diag(jnp.sum(own_wide, axis=(1, 2)))
    edge_grad = jnp.concatenate([edge_own[None], edge_off], axis=0) * graph_mask
    graph_sum, temporal_sum, shortcut_sum, edge_sum = lax.psum(
        (graph_grad, temporal_grad, shortcut_grad, edge_grad), ("batch", "tm")
    )

    mean, rstd, _, _ = first_moments(stats, norm_params)
    back_first_sum = first_sums[0:1]
    back_first_norm = rstd * (first_sums[1:2] - mean * back_first_sum)
    back_sum, back_conv, back_short = back_totals(back, second_moments(stats, conv_stats))
    norm_grad = jnp.concatenate(
        [back_first_norm, back_first_sum, back_conv, back_sum, back_short, back_sum], axis=0
    )
    squares_total = (
        jnp.sum(graph_sum * graph_sum)
        + jnp.sum(temporal_sum * temporal_sum)
        + jnp.sum(shortcut_sum * shortcut_sum)
        + jnp.sum(edge_sum * edge_sum)
        + jnp.sum(norm_grad * norm_grad)
    )
    norm_total = jnp.sqrt(squares_total)
    factor = jnp.minimum(1.0, clip_limit / (norm_total + 1e-06))
    graph_new = adam_update(
        graph_weight, graph_moment, graph_square, graph_average,
        graph_sum, factor, rate_matrix, decay_matrix,
    )
    temporal_new = adam_update(
        temporal_weight, temporal_moment, temporal_square, temporal_average,
        temporal_sum, factor, rate_matrix, decay_matrix,
    )
    shortcut_new = adam_update(
        shortcut_weight, shortcut_moment, shortcut_square, shortcut_average,
        shortcut_sum, factor, rate_matrix, decay_matrix,
    )
    edge_new = adam_update(
        edge_weight, edge_moment, edge_square, edge_average, edge_sum, factor, rate_small, 0.0
    )
    norm_new = adam_update(
        norm_params, norm_moment, norm_square, norm_average, norm_grad, factor, rate_small, 0.0
    )
    return (
        jnp.transpose(outputs, (0, 2, 1, 3)),
        jnp.transpose(input_grad, (0, 2, 1, 3)),
        jnp.reshape(norm_total, (1,)),
        *graph_new,
        *temporal_new,
        *shortcut_new,
        *edge_new,
        *norm_new,
    )


def solution(mesh):
    rows = P("batch", "tm", None, None)
    in_specs = (rows, rows, P("batch"), P("batch", "tm")) + (P(),) * 21
    out_specs = (rows, rows) + (P(),) * 21
    return jax.shard_map(shards, mesh=mesh, in_specs=in_specs, out_specs=out_specs, check_vma=False)
```

```python
import functools

import jax
import jax.numpy as jnp
from jax import lax
from jax.experimental import pallas as pl
from jax.experimental.pallas import tpu as pltpu
from jax.sharding import PartitionSpec as P

C_IN = 128
C_OUT = 256
JOINTS = 25
SUBSETS = 3
TAPS = 9
GROUP = 8
PHASES = 8
UNITS = 2 * JOINTS
ROWS = UNITS * GROUP
HALF_ROWS = JOINTS * GROUP
HALF = C_IN
CUT = 5

f32 = jnp.float32
bf16 = jnp.bfloat16

norm_epsilon = 1e-05
beta_first = 0.9
beta_second = 0.999
adam_epsilon = 1e-08
clip_limit = 1.0
average_decay = 0.9
rate_matrix = 0.05
rate_small = 0.3
decay_matrix = 0.01
steps_taken = 3.0


def params(**more):
    return pltpu.CompilerParams(
        vmem_limit_bytes=60 * 2**20, dimension_semantics=("arbitrary",), **more
    )


def adjacency(subsets):
    linked = (subsets > 0).astype(f32)
    degree = jnp.sum(linked, axis=0)
    labels = jnp.arange(SUBSETS, dtype=jnp.int32) + 1
    chosen = (subsets[None, :, :] == labels[:, None, None]).astype(f32)
    return chosen / degree[None, None, :]


def adam_update(weight, moment, square, average, gradient, factor, rate, decay):
    fix_first = 1.0 - beta_first**steps_taken
    fix_second = 1.0 - beta_second**steps_taken
    clipped = gradient * factor
    moment_new = beta_first * moment + (1.0 - beta_first) * clipped
    square_new = beta_second * square + (1.0 - beta_second) * clipped * clipped
    stepped = moment_new / fix_first / (jnp.sqrt(square_new / fix_second) + adam_epsilon)
    weight_new = weight - rate * (stepped + decay * weight)
    average_new = average_decay * average + (1.0 - average_decay) * weight_new
    return (weight_new, moment_new, square_new, average_new)


def dot(a, b):
    return jnp.dot(a, b, preferred_element_type=f32)


def dot_nt(a, b):
    return lax.dot_general(a, b, (((1,), (1,)), ((), ())), preferred_element_type=f32)


def dot_tn(a, b):
    return lax.dot_general(a, b, (((0,), (0,)), ((), ())), preferred_element_type=f32)


def fold(values):
    return jnp.sum(values.reshape(-1, GROUP, values.shape[-1]), axis=0)


def first_moments(stats, norm):
    count_in = stats[4:5]
    mean = stats[0:1] / count_in
    rstd = lax.rsqrt(stats[1:2] / count_in - mean * mean + norm_epsilon)
    return mean, rstd, norm[0:1] * rstd, norm[1:2] - norm[0:1] * rstd * mean


def mix_rows(parts, scales, kron_ref, pad_ref):
    wide = jnp.concatenate([part.reshape(HALF_ROWS, C_IN) for part in parts], axis=1)
    pad_ref[0:HALF_ROWS, :] = wide.astype(bf16)
    mixed = dot(kron_ref[...], pad_ref[...])
    sides = []
    for side in range(2):
        lanes = slice(side * HALF, (side + 1) * HALF)
        sides.append(
            jnp.concatenate(
                [
                    parts[side] * scales,
                    mixed[0:HALF_ROWS, lanes].reshape(JOINTS, GROUP, C_IN),
                    mixed[HALF_ROWS : 2 * HALF_ROWS, lanes].reshape(JOINTS, GROUP, C_IN),
                ],
                axis=2,
            )
        )
    return jnp.concatenate(sides, axis=1).reshape(ROWS, SUBSETS * C_IN).astype(bf16)


def graph_forward(
    x_ref, m_ref, kron_ref, own_ref, wg_ref, ws_ref,
    xg_ref, xq_ref, xe_ref, h_ref, st_ref,
    xs, sums, counts, *sum_buffers,
):
    step = pl.program_id(0)

    @pl.when(step == 0)
    def _():
        greet()
        sums[...] = jnp.zeros_like(sums)
        counts[...] = jnp.zeros_like(counts)

    for side in range(2):
        for joint in range(JOINTS):
            xs[side, joint] = x_ref[side, joint].astype(f32)
    own = own_ref[...]
    for c in range(PHASES):
        mask = m_ref[0, c]
        parts = [
            xs[side, :, pl.ds(c, GROUP, stride=PHASES), :]
            * mask[side * GROUP : (side + 1) * GROUP][None]
            for side in range(2)
        ]
        xq_ref[0, c, HALF_ROWS:, :] = jnp.zeros((C_OUT - HALF_ROWS, C_OUT), bf16)
        xg = mix_rows(parts, own, kron_ref, xq_ref.at[0, c])
        xg_ref[0, c] = xg
        hidden = dot(xg, wg_ref[...])
        h_ref[0, c] = hidden.astype(bf16)
        sums[0] += fold(hidden)
        sums[1] += fold(hidden * hidden)
        counts[0] += mask
        if c % 2 == 0:
            counts[1] += mask
            even = jnp.concatenate(parts, axis=1).reshape(ROWS, C_IN).astype(bf16)
            xe_ref[0, c // 2] = even
            short = dot(even, ws_ref[...])
            sums[2] += fold(short)
            sums[3] += fold(short * short)

    @pl.when(step == pl.num_programs(0) - 1)
    def _():
        await_greetings()
        rows = [jnp.sum(sums[k], axis=0, keepdims=True) for k in range(4)]
        for k in range(2):
            total = JOINTS * jnp.sum(counts[k], axis=0, keepdims=True)
            rows.append(jnp.concatenate([total, total], axis=1))
        rows.append(jnp.zeros((2, C_OUT), f32))
        st_ref[...] = sum_all(jnp.concatenate(rows, axis=0), as_buffers(sum_buffers))


def insert_and_roll(tiles, fill, side):
    sub = lax.broadcasted_iota(jnp.int32, tiles.shape, 1)
    joined = jnp.where(sub == side, fill, tiles)
    return pltpu.roll(joined, 1 if side == 7 else GROUP - 1, 1)


def conv_forward(
    h_ref, xh_ref, m_ref, mh_ref, st_ref, norm_ref, kron_ref, own_ref, wg_ref, taps_ref,
    a_ref, conv_ref, out_ref,
    pad, rims, fills, sums, *sum_buffers,
):
    step = pl.program_id(0)

    @pl.when(step == 0)
    def _():
        greet()
        sums[...] = jnp.zeros_like(sums)
        pad[...] = jnp.zeros_like(pad)

    _, _, scale, shift = first_moments(st_ref[...], norm_ref[...])
    scale, shift = 0.5 * scale, 0.5 * shift

    def activate(values, mask):
        half = values * scale + shift
        return (half + half * jnp.tanh(half)).reshape(-1, 2 * GROUP, C_OUT) * mask

    def wide(mask):
        return jnp.concatenate([mask, mask], axis=1)[None]

    rim_mask = mh_ref[0]
    parts = [
        xh_ref[side] * rim_mask[side * GROUP : (side + 1) * GROUP][None] for side in range(2)
    ]
    rim_hidden = dot(mix_rows(parts, own_ref[...], kron_ref, pad), wg_ref[...])
    rim_active = activate(rim_hidden, wide(rim_mask)).reshape(ROWS, C_OUT)
    for lane in range(2):
        rims[lane] = rim_active[:, lane * HALF : (lane + 1) * HALF]
    for p in range(2):
        for q in range(2):
            for lane in range(2):
                fills[2 * p + q, lane, pl.ds(7, UNITS, stride=GROUP), :] = rims[
                    lane, pl.ds(2 * q + p, UNITS, stride=GROUP), :
                ]
                fills[2 * p + q, lane, pl.ds(0, UNITS, stride=GROUP), :] = rims[
                    lane, pl.ds(4 + 2 * q + p, UNITS, stride=GROUP), :
                ]

    for c in range(PHASES):
        p, q = c % 2, c // 2
        mask = wide(m_ref[0, c])
        for start in range(0, JOINTS, CUT):
            rows = slice(start * 2 * GROUP, (start + CUT) * 2 * GROUP)
            active = activate(h_ref[0, c, rows, :].astype(f32), mask)
            a_ref[0, p, q + 2, rows, :] = active.reshape(-1, C_OUT).astype(bf16)
            if p == 1 and q == 1:
                continue
            tiles = active.reshape(-1, GROUP, C_OUT)
            fill = jnp.concatenate(
                [fills[2 * p + q % 2, lane, rows, :] for lane in range(2)], axis=1
            ).reshape(-1, GROUP, C_OUT)
            moved = insert_and_roll(tiles, fill, 7 if q >= 2 else 0)
            at = q - 2 if q >= 2 else q + 6
            a_ref[0, p, at, rows, :] = moved.reshape(-1, C_OUT).astype(bf16)

    total = None
    for j in range(TAPS):
        window = a_ref[0, j % 2, j // 2 : j // 2 + 4].reshape(4 * ROWS, C_OUT)
        part = dot(window, taps_ref[j])
        total = part if total is None else total + part
    conv_ref[0] = total.reshape(4, ROWS, C_OUT)
    for q in range(4):
        block = total[q * ROWS : (q + 1) * ROWS].reshape(JOINTS, 2 * GROUP, C_OUT)
        live = block * wide(m_ref[0, 2 * q])
        sums[0] += fold(live)
        sums[1] += fold(live * block)

    @pl.when(step == pl.num_programs(0) - 1)
    def _():
        await_greetings()
        rows = [jnp.sum(sums[k], axis=0, keepdims=True) for k in range(2)]
        rows.append(jnp.zeros((6, C_OUT), f32))
        out_ref[...] = sum_all(jnp.concatenate(rows, axis=0), as_buffers(sum_buffers))


def second_moments(stats, conv_stats):
    count_out = stats[5:6]
    mean_conv = conv_stats[0:1] / count_out
    rstd_conv = lax.rsqrt(conv_stats[1:2] / count_out - mean_conv * mean_conv + norm_epsilon)
    mean_short = stats[2:3] / count_out
    rstd_short = lax.rsqrt(stats[3:4] / count_out - mean_short * mean_short + norm_epsilon)
    return mean_conv, rstd_conv, mean_short, rstd_short


def output_part(
    conv_ref, xe_ref, cot_ref, m_ref, st_ref, cs_ref, norm_ref, ws_ref,
    o_ref, up_ref, out_ref,
    cots, outs, sums, *sum_buffers,
):
    step = pl.program_id(0)

    @pl.when(step == 0)
    def _():
        greet()
        sums[...] = jnp.zeros_like(sums)

    norm = norm_ref[...]
    mean_conv, rstd_conv, mean_short, rstd_short = second_moments(st_ref[...], cs_ref[...])
    scale_conv = 0.5 * norm[2:3] * rstd_conv
    scale_short = 0.5 * norm[4:5] * rstd_short
    shift = 0.5 * (norm[3:4] + norm[5:6]) - scale_conv * mean_conv - scale_short * mean_short
    for side in range(2):
        for joint in range(JOINTS):
            for lane in range(2):
                cots[side, lane, joint] = cot_ref[
                    side, joint, :, lane * HALF : (lane + 1) * HALF
                ].astype(f32)
    for q in range(4):
        mask = m_ref[0, 2 * q]
        mask = jnp.concatenate([mask, mask], axis=1)[None]
        short_all = dot(xe_ref[0, q], ws_ref[...])
        for start in range(0, JOINTS, CUT):
            rows = slice(start * 2 * GROUP, (start + CUT) * 2 * GROUP)
            conv = conv_ref[0, q, rows, :]
            short = short_all[rows]
            half = conv * scale_conv + short * scale_short + shift
            turn = jnp.tanh(half)
            grow = (0.5 + 0.5 * turn).reshape(CUT, 2 * GROUP, C_OUT) * mask
            half = half.reshape(CUT, 2 * GROUP, C_OUT)
            turn = turn.reshape(CUT, 2 * GROUP, C_OUT)
            result = (half + half) * grow
            slope = grow + grow * (half - half * turn)
            cot = jnp.concatenate(
                [
                    jnp.concatenate(
                        [
                            cots[side, lane, start : start + CUT, pl.ds(q, GROUP, stride=4), :]
                            for lane in range(2)
                        ],
                        axis=2,
                    )
                    for side in range(2)
                ],
                axis=1,
            )
            for side in range(2):
                for lane in range(2):
                    outs[side, lane, start : start + CUT, pl.ds(q, GROUP, stride=4), :] = result[
                        :, side * GROUP : (side + 1) * GROUP, lane * HALF : (lane + 1) * HALF
                    ]
            up = (cot * slope).reshape(-1, C_OUT)
            up_ref[0, q, rows, :] = up
            sums[0] += fold(up)
            sums[1] += fold(up * conv)
            sums[2] += fold(up * short)
    for side in range(2):
        for joint in range(JOINTS):
            for lane in range(2):
                o_ref[side, joint, :, lane * HALF : (lane + 1) * HALF] = outs[
                    side, lane, joint
                ].astype(bf16)

    @pl.when(step == pl.num_programs(0) - 1)
    def _():
        await_greetings()
        rows = [jnp.sum(sums[k], axis=0, keepdims=True) for k in range(3)]
        rows.append(jnp.zeros((5, C_OUT), f32))
        out_ref[...] = sum_all(jnp.concatenate(rows, axis=0), as_buffers(sum_buffers))


def back_totals(back, moments):
    mean_conv, rstd_conv, mean_short, rstd_short = moments
    back_sum = back[0:1]
    back_conv = rstd_conv * (back[1:2] - mean_conv * back_sum)
    back_short = rstd_short * (back[2:3] - mean_short * back_sum)
    return back_sum, back_conv, back_short


def weight_part(
    conv_ref, up_ref, xe_ref, a_ref, m_ref, st_ref, cs_ref, bk_ref, norm_ref, ws_ref,
    cg_ref, sg_ref, lo_ref, hi_ref, tg_ref, shg_ref,
    turned, edges,
):
    step = pl.program_id(0)

    @pl.when(step == 0)
    def _():
        tg_ref[...] = jnp.zeros_like(tg_ref)
        shg_ref[...] = jnp.zeros_like(shg_ref)

    norm = norm_ref[...]
    stats = st_ref[...]
    moments = second_moments(stats, cs_ref[...])
    mean_conv, rstd_conv, mean_short, rstd_short = moments
    back_sum, back_conv, back_short = back_totals(bk_ref[...], moments)
    count_out = stats[5:6]

    def terms(gain, mean, rstd, back):
        lead = gain * rstd
        slope = lead * rstd * back / count_out
        return lead, slope, lead * back_sum / count_out - slope * mean

    lead_c, slope_c, shift_c = terms(norm[2:3], mean_conv, rstd_conv, back_conv)
    lead_s, slope_s, shift_s = terms(norm[4:5], mean_short, rstd_short, back_short)
    for q in range(4):
        mask = m_ref[0, 2 * q]
        mask = jnp.concatenate([mask, mask], axis=1)[None]
        short_all = dot(xe_ref[0, q], ws_ref[...])
        for start in range(0, JOINTS, CUT):
            rows = slice(start * 2 * GROUP, (start + CUT) * 2 * GROUP)
            up = up_ref[0, q, rows, :]

            def masked(values):
                return (values.reshape(CUT, 2 * GROUP, C_OUT) * mask).reshape(-1, C_OUT)

            cg = up * lead_c - masked(conv_ref[0, q, rows, :] * slope_c + shift_c)
            cg_ref[0, q, rows, :] = cg.astype(bf16)
            for lane in range(2):
                edges[lane, rows, :] = cg[:, lane * HALF : (lane + 1) * HALF]
            sg = up * lead_s - masked(short_all[rows] * slope_s + shift_s)
            sg_ref[0, q, rows, :] = sg.astype(bf16)
        for lane in range(2):
            at = slice(lane * HALF, (lane + 1) * HALF)
            if q < 2:
                lo_ref[0, q, :, at] = edges[lane, pl.ds(0, UNITS, stride=GROUP), :].astype(bf16)
            else:
                hi_ref[0, q - 2, :, at] = edges[lane, pl.ds(7, UNITS, stride=GROUP), :].astype(bf16)
    turned[...] = cg_ref[0].reshape(4 * ROWS, C_OUT).T
    for j in range(TAPS):
        window = a_ref[0, j % 2, j // 2 : j // 2 + 4].reshape(4 * ROWS, C_OUT)
        tg_ref[j] += dot(turned[...], window)
    shg_ref[...] += dot_tn(
        xe_ref[0].reshape(4 * ROWS, C_IN), sg_ref[0].reshape(4 * ROWS, C_OUT)
    )


def conv_back(
    cg_ref, left_ref, right_ref, taps_ref, h_ref, m_ref, st_ref, norm_ref,
    fg_ref, out_ref,
    fills, ext, sums, *sum_buffers,
):
    step = pl.program_id(0)

    @pl.when(step == 0)
    def _():
        greet()
        sums[...] = jnp.zeros_like(sums)

    _, _, scale, shift = first_moments(st_ref[...], norm_ref[...])
    scale, shift = 0.5 * scale, 0.5 * shift
    for q in range(2):
        for lane in range(2):
            at = slice(lane * HALF, (lane + 1) * HALF)
            fills[q, lane, pl.ds(7, UNITS, stride=GROUP), :] = left_ref[0, q, :, at].astype(f32)
            fills[q, lane, pl.ds(0, UNITS, stride=GROUP), :] = right_ref[0, q, :, at].astype(f32)
    for q in range(4):
        ext[q + 2] = cg_ref[0, q]
        for start in range(0, JOINTS, CUT):
            rows = slice(start * 2 * GROUP, (start + CUT) * 2 * GROUP)
            tiles = cg_ref[0, q, rows, :].astype(f32).reshape(-1, GROUP, C_OUT)
            fill = jnp.concatenate([fills[q % 2, lane, rows, :] for lane in range(2)], axis=1)
            fill = fill.reshape(-1, GROUP, C_OUT)
            moved = insert_and_roll(tiles, fill, 7 if q >= 2 else 0)
            at = q - 2 if q >= 2 else q + 6
            ext[at, rows, :] = moved.reshape(-1, C_OUT).astype(bf16)
    for p in range(2):
        total = None
        for i in range(5 - p):
            window = ext[4 - i : 8 - i].reshape(4 * ROWS, C_OUT)
            part = dot_nt(window, taps_ref[2 * i + p])
            total = part if total is None else total + part
        for q in range(4):
            c = 2 * q + p
            mask = 0.5 * m_ref[0, c]
            mask = jnp.concatenate([mask, mask], axis=1)[None]
            for start in range(0, JOINTS, CUT):
                rows = slice(start * 2 * GROUP, (start + CUT) * 2 * GROUP)
                hidden = h_ref[0, c, rows, :].astype(f32)
                half = hidden * scale + shift
                turn = jnp.tanh(half)
                slope = (1.0 + turn) * (1.0 + (half - half * turn))
                slope = (slope.reshape(CUT, 2 * GROUP, C_OUT) * mask).reshape(-1, C_OUT)
                grad = total[q * ROWS + rows.start : q * ROWS + rows.stop] * slope
                fg_ref[0, c, rows, :] = grad
                sums[0] += fold(grad)
                sums[1] += fold(grad * hidden)

    @pl.when(step == pl.num_programs(0) - 1)
    def _():
        await_greetings()
        rows = [jnp.sum(sums[k], axis=0, keepdims=True) for k in range(2)]
        rows.append(jnp.zeros((6, C_OUT), f32))
        out_ref[...] = sum_all(jnp.concatenate(rows, axis=0), as_buffers(sum_buffers))


def graph_back(
    fg_ref, h_ref, xg_ref, xq_ref, sg_ref, m_ref, st_ref, fs_ref, norm_ref,
    wg_ref, ws_ref, kront_ref, own_ref,
    ig_ref, gg_ref, eg_ref, own_grad_ref,
    hg_all, spread, natural,
):
    step = pl.program_id(0)

    @pl.when(step == 0)
    def _():
        gg_ref[...] = jnp.zeros_like(gg_ref)
        eg_ref[...] = jnp.zeros_like(eg_ref)
        own_grad_ref[...] = jnp.zeros_like(own_grad_ref)
        spread[...] = jnp.zeros_like(spread)

    norm = norm_ref[...]
    stats = st_ref[...]
    mean, rstd, _, _ = first_moments(stats, norm)
    count_in = stats[4:5]
    back_sum = fs_ref[0:1]
    back_norm = rstd * (fs_ref[1:2] - mean * back_sum)
    lead = norm[0:1] * rstd
    slope = lead * rstd * back_norm / count_in
    shift = lead * back_sum / count_in - slope * mean
    own = own_ref[...]
    for c in range(PHASES):
        mask = m_ref[0, c]
        mask = jnp.concatenate([mask, mask], axis=1)[None]
        for start in range(0, JOINTS, CUT):
            rows = slice(start * 2 * GROUP, (start + CUT) * 2 * GROUP)
            hidden = h_ref[0, c, rows, :].astype(f32)
            taken = ((hidden * slope + shift).reshape(CUT, 2 * GROUP, C_OUT) * mask).reshape(
                -1, C_OUT
            )
            hg_all[c, rows, :] = (fg_ref[0, c, rows, :] * lead - taken).astype(bf16)
        back = dot(hg_all[c], wg_ref[...]).reshape(JOINTS, 2 * GROUP, SUBSETS * C_IN)

        def side_by_side(values):
            return jnp.concatenate([values[:, 0:GROUP], values[:, GROUP : 2 * GROUP]], axis=2)

        for k in range(2):
            lanes = slice((k + 1) * C_IN, (k + 2) * C_IN)
            spread[k, 0:HALF_ROWS, :] = (
                side_by_side(back[:, :, lanes]).reshape(HALF_ROWS, 2 * C_IN).astype(bf16)
            )
        direct = side_by_side(back[:, :, 0:C_IN])
        both = spread[...].reshape(2 * C_OUT, C_OUT)
        whole = dot(kront_ref[...], both)
        result = whole.reshape(JOINTS, GROUP, 2 * C_IN) + direct * jnp.concatenate([own, own], axis=2)
        if c % 2 == 0:
            short = dot(sg_ref[0, c // 2], ws_ref[...]).reshape(JOINTS, 2 * GROUP, C_IN)
            result = result + side_by_side(short)
        for side in range(2):
            natural[side, :, pl.ds(c, GROUP, stride=PHASES), :] = result[
                :, :, side * C_IN : (side + 1) * C_IN
            ]
        eg_ref[...] += dot_nt(both, xq_ref[0, c])
        seen = xq_ref[0, c, 0:HALF_ROWS, :].astype(f32).reshape(JOINTS, GROUP, 2 * C_IN)
        own_grad_ref[...] += seen * direct
    for side in range(2):
        for joint in range(JOINTS):
            ig_ref[side, joint] = natural[side, joint].astype(bf16)
    gg_ref[...] += dot_tn(
        xg_ref[0].reshape(PHASES * ROWS, SUBSETS * C_IN), hg_all[...].reshape(PHASES * ROWS, C_OUT)
    )


MESH = pl.DeviceIdType.MESH


def peers(axis):
    count = lax.axis_size(axis)
    here = lax.axis_index(axis)
    return [(d, {axis: lax.rem(here + d, count)}) for d in range(1, count)]


def greet():
    barrier = pltpu.get_barrier_semaphore()
    for axis in ("tm", "batch"):
        for _, device in peers(axis):
            pl.semaphore_signal(barrier, inc=1, device_id=device, device_id_type=MESH)


def await_greetings():
    count = lax.axis_size("tm") + lax.axis_size("batch") - 2
    pl.semaphore_wait(pltpu.get_barrier_semaphore(), count)


def sum_all(values, buffers):
    copies = []
    for axis, (slots, sent, received) in zip(("tm", "batch"), buffers):
        here = lax.axis_index(axis)
        slots[here] = values
        started = []
        for d, device in peers(axis):
            copy = pltpu.make_async_remote_copy(
                src_ref=slots.at[here],
                dst_ref=slots.at[here],
                send_sem=sent.at[d],
                recv_sem=received.at[d],
                device_id=device,
                device_id_type=MESH,
            )
            copy.start()
            started.append(copy)
        for copy in started:
            copy.wait_recv()
        values = slots[0]
        for k in range(1, lax.axis_size(axis)):
            values = values + slots[k]
        copies += started
    for copy in copies:
        copy.wait_send()
    return values


def as_buffers(refs):
    return [refs[0:3], refs[3:6]]


def sum_scratch(shape=(8, C_OUT)):
    found = []
    for axis in ("tm", "batch"):
        count = lax.axis_size(axis)
        found += [
            pltpu.VMEM((count, *shape), f32),
            pltpu.SemaphoreType.DMA((count,)),
            pltpu.SemaphoreType.DMA((count,)),
        ]
    return found


def whole_spec(shape):
    return pl.BlockSpec(shape, lambda i: (0,) * len(shape))


def lead_spec(shape):
    return pl.BlockSpec(shape, lambda i: (i,) + (0,) * (len(shape) - 1))


def call(body, pairs, ins, outs, scratch, name, **more):
    in_specs = [
        whole_spec(array.shape) if block is None else lead_spec(block) for array, block in ins
    ]
    out_specs = [whole_spec(shape) if block is None else lead_spec(block) for shape, _, block in outs]
    return pl.pallas_call(
        body,
        grid=(pairs,),
        in_specs=in_specs,
        out_specs=out_specs,
        out_shape=[jax.ShapeDtypeStruct(shape, kind) for shape, kind, _ in outs],
        scratch_shapes=scratch,
        compiler_params=params(**more),
        name=name,
    )(*[array for array, _ in ins])


def shards(
    inputs, cotangent, lengths, frame_mask, subsets,
    graph_weight, graph_moment, graph_square, graph_average,
    temporal_weight, temporal_moment, temporal_square, temporal_average,
    shortcut_weight, shortcut_moment, shortcut_square, shortcut_average,
    edge_weight, edge_moment, edge_square, edge_average,
    norm_params, norm_moment, norm_square, norm_average,
):
    clips = inputs.shape[0]
    frames = inputs.shape[1]
    pairs = clips // 2
    tm_size = lax.axis_size("tm")
    forward = [(i, i + 1) for i in range(tm_size - 1)]
    backward = [(i + 1, i) for i in range(tm_size - 1)]
    first_frame = lax.axis_index("tm") * frames
    frame_ids = first_frame + jnp.arange(frames, dtype=jnp.int32)
    mask_in = ((frame_ids[None, :] < lengths[:, None]) & (frame_mask > 0)).astype(f32)

    natural = jnp.transpose(inputs, (0, 2, 1, 3))
    before = lax.ppermute(natural[:, :, -4:], "tm", forward)
    after = lax.ppermute(natural[:, :, :4], "tm", backward)
    rim_x = jnp.concatenate([before, after], axis=2).astype(f32)
    mask_before = lax.ppermute(mask_in[:, -4:], "tm", forward)
    mask_after = lax.ppermute(mask_in[:, :4], "tm", backward)
    rim_mask = jnp.concatenate([mask_before, mask_after], axis=1).reshape(pairs, 2 * GROUP)
    rim_mask = jnp.broadcast_to(rim_mask[:, :, None], (pairs, 2 * GROUP, 128))
    masks = mask_in.reshape(pairs, 2, GROUP, PHASES).transpose(0, 3, 1, 2)
    masks = jnp.broadcast_to(
        masks.reshape(pairs, PHASES, 2 * GROUP)[..., None], (pairs, PHASES, 2 * GROUP, 128)
    )

    graph_mask = adjacency(subsets)
    graph_low = (graph_mask * edge_weight).astype(bf16)
    same = jnp.eye(GROUP, dtype=bf16)
    kron = graph_low[1:].transpose(0, 2, 1)[:, :, None, :, None] * same[None, None, :, None, :]
    kron = kron.reshape(2 * HALF_ROWS, HALF_ROWS)
    kron = jnp.pad(kron, ((0, 0), (0, C_OUT - HALF_ROWS)))
    kront = graph_low[1:].transpose(1, 0, 2)[:, None, :, :, None] * same[None, :, None, None, :]
    kront = kront.reshape(HALF_ROWS, 2, HALF_ROWS)
    kront = jnp.pad(kront, ((0, 0), (0, 0), (0, C_OUT - HALF_ROWS))).reshape(HALF_ROWS, 2 * C_OUT)
    own = jnp.diagonal(graph_low[0]).astype(f32)
    own = jnp.broadcast_to(own[:, None, None], (JOINTS, GROUP, C_IN))
    wg = graph_weight.astype(bf16).reshape(C_IN, SUBSETS, C_OUT).transpose(1, 0, 2)
    wg = wg.reshape(SUBSETS * C_IN, C_OUT)
    ws = shortcut_weight.astype(bf16)
    taps = temporal_weight.astype(bf16)

    x_block = (2, JOINTS, frames, C_IN)
    mask_block = (1, PHASES, 2 * GROUP, 128)
    wide_block = (1, PHASES, ROWS, C_OUT)
    out_block = (1, 4, ROWS, C_OUT)
    xe_block = (1, 4, ROWS, C_IN)
    a_block = (1, 2, 8, ROWS, C_OUT)
    rim_block = (1, 2, UNITS, C_OUT)
    small = (8, C_OUT)

    def full(block):
        return (pairs,) + block[1:]

    xg_block = (1, PHASES, ROWS, SUBSETS * C_IN)
    xq_block = (1, PHASES, C_OUT, C_OUT)
    xg, xq, xe, hidden, stats = call(
        graph_forward,
        pairs,
        [(natural, x_block), (masks, mask_block), (kron, None), (own, None), (wg, None), (ws, None)],
        [
            (full(xg_block), bf16, xg_block),
            (full(xq_block), bf16, xq_block),
            (full(xe_block), bf16, xe_block),
            (full(wide_block), bf16, wide_block),
            (small, f32, None),
        ],
        [
            pltpu.VMEM((2, JOINTS, frames, C_IN), f32),
            pltpu.VMEM((4, GROUP, C_OUT), f32),
            pltpu.VMEM((2, 2 * GROUP, 128), f32),
        ]
        + sum_scratch(),
        "graph_forward",
        collective_id=1,
        has_side_effects=True,
    )

    active, conv, conv_stats = call(
        conv_forward,
        pairs,
        [
            (hidden, wide_block),
            (rim_x, (2, JOINTS, GROUP, C_IN)),
            (masks, mask_block),
            (rim_mask, (1, 2 * GROUP, 128)),
            (stats, None),
            (norm_params, None),
            (kron, None),
            (own, None),
            (wg, None),
            (taps, None),
        ],
        [
            (full(a_block), bf16, a_block),
            (full(out_block), f32, out_block),
            (small, f32, None),
        ],
        [
            pltpu.VMEM((C_OUT, C_OUT), bf16),
            pltpu.VMEM((2, ROWS, HALF), f32),
            pltpu.VMEM((4, 2, ROWS, HALF), f32),
            pltpu.VMEM((2, GROUP, C_OUT), f32),
        ]
        + sum_scratch(),
        "conv_forward",
        collective_id=2,
        has_side_effects=True,
    )

    cot = jnp.transpose(cotangent, (0, 2, 1, 3))
    cot_block = (2, JOINTS, frames // 2, C_OUT)
    outputs, upstream, back = call(
        output_part,
        pairs,
        [
            (conv, out_block),
            (xe, xe_block),
            (cot, cot_block),
            (masks, mask_block),
            (stats, None),
            (conv_stats, None),
            (norm_params, None),
            (ws, None),
        ],
        [
            (cot.shape, bf16, cot_block),
            (full(out_block), f32, out_block),
            (small, f32, None),
        ],
        [
            pltpu.VMEM((2, 2, JOINTS, frames // 2, HALF), f32),
            pltpu.VMEM((2, 2, JOINTS, frames // 2, HALF), f32),
            pltpu.VMEM((3, GROUP, C_OUT), f32),
        ]
        + sum_scratch(),
        "output_part",
        collective_id=3,
        has_side_effects=True,
    )

    conv_grad, short_grad, low_rim, high_rim, temporal_turned, shortcut_grad = call(
        weight_part,
        pairs,
        [
            (conv, out_block),
            (upstream, out_block),
            (xe, xe_block),
            (active, a_block),
            (masks, mask_block),
            (stats, None),
            (conv_stats, None),
            (back, None),
            (norm_params, None),
            (ws, None),
        ],
        [
            (full(out_block), bf16, out_block),
            (full(out_block), bf16, out_block),
            (full(rim_block), bf16, rim_block),
            (full(rim_block), bf16, rim_block),
            ((TAPS, C_OUT, C_OUT), f32, None),
            ((C_IN, C_OUT), f32, None),
        ],
        [
            pltpu.VMEM((C_OUT, 4 * ROWS), bf16),
            pltpu.VMEM((2, ROWS, HALF), f32),
        ],
        "weight_part",
    )
    left_rim = lax.ppermute(high_rim, "tm", forward)
    right_rim = lax.ppermute(low_rim, "tm", backward)

    first_grad, first_sums = call(
        conv_back,
        pairs,
        [
            (conv_grad, out_block),
            (left_rim, rim_block),
            (right_rim, rim_block),
            (taps, None),
            (hidden, wide_block),
            (masks, mask_block),
            (stats, None),
            (norm_params, None),
        ],
        [
            (full(wide_block), f32, wide_block),
            (small, f32, None),
        ],
        [
            pltpu.VMEM((2, 2, ROWS, HALF), f32),
            pltpu.VMEM((8, ROWS, C_OUT), bf16),
            pltpu.VMEM((2, GROUP, C_OUT), f32),
        ]
        + sum_scratch(),
        "conv_back",
        collective_id=4,
        has_side_effects=True,
    )

    input_grad, graph_turned, edge_wide, own_wide = call(
        graph_back,
        pairs,
        [
            (first_grad, wide_block),
            (hidden, wide_block),
            (xg, xg_block),
            (xq, xq_block),
            (short_grad, out_block),
            (masks, mask_block),
            (stats, None),
            (first_sums, None),
            (norm_params, None),
            (wg.T, None),
            (ws.T, None),
            (kront, None),
            (own, None),
        ],
        [
            (natural.shape, bf16, x_block),
            ((SUBSETS * C_IN, C_OUT), f32, None),
            ((2 * C_OUT, C_OUT), f32, None),
            ((JOINTS, GROUP, 2 * C_IN), f32, None),
        ],
        [
            pltpu.VMEM((PHASES, ROWS, C_OUT), bf16),
            pltpu.VMEM((2, C_OUT, C_OUT), bf16),
            pltpu.VMEM((2, JOINTS, frames, C_IN), f32),
        ],
        "graph_back",
    )
    temporal_grad = jnp.swapaxes(temporal_turned, 1, 2)
    graph_grad = graph_turned.reshape(SUBSETS, C_IN, C_OUT).transpose(1, 0, 2)
    graph_grad = graph_grad.reshape(C_IN, SUBSETS * C_OUT)
    edge_wide = edge_wide.reshape(2, C_OUT, C_OUT)[:, :HALF_ROWS, :HALF_ROWS]
    edge_wide = edge_wide.reshape(2, JOINTS, GROUP, JOINTS, GROUP)
    edge_off = jnp.einsum("kwrvr->kvw", edge_wide)
    edge_own = jnp.diag(jnp.sum(own_wide, axis=(1, 2)))
    edge_grad = jnp.concatenate([edge_own[None], edge_off], axis=0) * graph_mask
    graph_sum, temporal_sum, shortcut_sum, edge_sum = lax.psum(
        (graph_grad, temporal_grad, shortcut_grad, edge_grad), ("batch", "tm")
    )

    mean, rstd, _, _ = first_moments(stats, norm_params)
    back_first_sum = first_sums[0:1]
    back_first_norm = rstd * (first_sums[1:2] - mean * back_first_sum)
    back_sum, back_conv, back_short = back_totals(back, second_moments(stats, conv_stats))
    norm_grad = jnp.concatenate(
        [back_first_norm, back_first_sum, back_conv, back_sum, back_short, back_sum], axis=0
    )
    squares_total = (
        jnp.sum(graph_sum * graph_sum)
        + jnp.sum(temporal_sum * temporal_sum)
        + jnp.sum(shortcut_sum * shortcut_sum)
        + jnp.sum(edge_sum * edge_sum)
        + jnp.sum(norm_grad * norm_grad)
    )
    norm_total = jnp.sqrt(squares_total)
    factor = jnp.minimum(1.0, clip_limit / (norm_total + 1e-06))
    graph_new = adam_update(
        graph_weight, graph_moment, graph_square, graph_average,
        graph_sum, factor, rate_matrix, decay_matrix,
    )
    temporal_new = adam_update(
        temporal_weight, temporal_moment, temporal_square, temporal_average,
        temporal_sum, factor, rate_matrix, decay_matrix,
    )
    shortcut_new = adam_update(
        shortcut_weight, shortcut_moment, shortcut_square, shortcut_average,
        shortcut_sum, factor, rate_matrix, decay_matrix,
    )
    edge_new = adam_update(
        edge_weight, edge_moment, edge_square, edge_average, edge_sum, factor, rate_small, 0.0
    )
    norm_new = adam_update(
        norm_params, norm_moment, norm_square, norm_average, norm_grad, factor, rate_small, 0.0
    )
    return (
        jnp.transpose(outputs, (0, 2, 1, 3)),
        jnp.transpose(input_grad, (0, 2, 1, 3)),
        jnp.reshape(norm_total, (1,)),
        *graph_new,
        *temporal_new,
        *shortcut_new,
        *edge_new,
        *norm_new,
    )


def solution(mesh):
    rows = P("batch", "tm", None, None)
    in_specs = (rows, rows, P("batch"), P("batch", "tm")) + (P(),) * 21
    out_specs = (rows, rows) + (P(),) * 21
    return jax.shard_map(shards, mesh=mesh, in_specs=in_specs, out_specs=out_specs, check_vma=False)
```

```python
import functools

import jax
import jax.numpy as jnp
from jax import lax
from jax.experimental import pallas as pl
from jax.experimental.pallas import tpu as pltpu
from jax.sharding import PartitionSpec as P

C_IN = 128
C_OUT = 256
JOINTS = 25
SUBSETS = 3
TAPS = 9
GROUP = 8
PHASES = 8
UNITS = 2 * JOINTS
ROWS = UNITS * GROUP
HALF_ROWS = JOINTS * GROUP
HALF = C_IN
CUT = 5

f32 = jnp.float32
bf16 = jnp.bfloat16

norm_epsilon = 1e-05
beta_first = 0.9
beta_second = 0.999
adam_epsilon = 1e-08
clip_limit = 1.0
average_decay = 0.9
rate_matrix = 0.05
rate_small = 0.3
decay_matrix = 0.01
steps_taken = 3.0


def params(**more):
    return pltpu.CompilerParams(
        vmem_limit_bytes=60 * 2**20, dimension_semantics=("arbitrary",), **more
    )


def adjacency(subsets):
    linked = (subsets > 0).astype(f32)
    degree = jnp.sum(linked, axis=0)
    labels = jnp.arange(SUBSETS, dtype=jnp.int32) + 1
    chosen = (subsets[None, :, :] == labels[:, None, None]).astype(f32)
    return chosen / degree[None, None, :]


def adam_update(weight, moment, square, average, gradient, factor, rate, decay):
    fix_first = 1.0 - beta_first**steps_taken
    fix_second = 1.0 - beta_second**steps_taken
    clipped = gradient * factor
    moment_new = beta_first * moment + (1.0 - beta_first) * clipped
    square_new = beta_second * square + (1.0 - beta_second) * clipped * clipped
    stepped = moment_new / fix_first / (jnp.sqrt(square_new / fix_second) + adam_epsilon)
    weight_new = weight - rate * (stepped + decay * weight)
    average_new = average_decay * average + (1.0 - average_decay) * weight_new
    return (weight_new, moment_new, square_new, average_new)


def dot(a, b):
    return jnp.dot(a, b, preferred_element_type=f32)


def dot_nt(a, b):
    return lax.dot_general(a, b, (((1,), (1,)), ((), ())), preferred_element_type=f32)


def dot_tn(a, b):
    return lax.dot_general(a, b, (((0,), (0,)), ((), ())), preferred_element_type=f32)


def fold(values):
    return jnp.sum(values.reshape(-1, GROUP, values.shape[-1]), axis=0)


MESH = pl.DeviceIdType.MESH


def peers(axis):
    count = lax.axis_size(axis)
    here = lax.axis_index(axis)
    return [(d, {axis: lax.rem(here + d, count)}) for d in range(1, count)]


def greet():
    barrier = pltpu.get_barrier_semaphore()
    for axis in ("tm", "batch"):
        for _, device in peers(axis):
            pl.semaphore_signal(barrier, inc=1, device_id=device, device_id_type=MESH)


def await_greetings():
    count = lax.axis_size("tm") + lax.axis_size("batch") - 2
    pl.semaphore_wait(pltpu.get_barrier_semaphore(), count)


def sum_all(values, buffers):
    copies = []
    for axis, (slots, sent, received) in zip(("tm", "batch"), buffers):
        here = lax.axis_index(axis)
        slots[here] = values
        started = []
        for d, device in peers(axis):
            copy = pltpu.make_async_remote_copy(
                src_ref=slots.at[here],
                dst_ref=slots.at[here],
                send_sem=sent.at[d],
                recv_sem=received.at[d],
                device_id=device,
                device_id_type=MESH,
            )
            copy.start()
            started.append(copy)
        for copy in started:
            copy.wait_recv()
        values = slots[0]
        for k in range(1, lax.axis_size(axis)):
            values = values + slots[k]
        copies += started
    for copy in copies:
        copy.wait_send()
    return values


def as_buffers(refs):
    return [refs[0:3], refs[3:6]]


def sum_scratch(shape=(8, C_OUT)):
    found = []
    for axis in ("tm", "batch"):
        count = lax.axis_size(axis)
        found += [
            pltpu.VMEM((count, *shape), f32),
            pltpu.SemaphoreType.DMA((count,)),
            pltpu.SemaphoreType.DMA((count,)),
        ]
    return found


def remote(source, target, sent, received, device):
    return pltpu.make_async_remote_copy(
        src_ref=source,
        dst_ref=target,
        send_sem=sent,
        recv_sem=received,
        device_id=device,
        device_id_type=MESH,
    )


def with_neighbours(step, low, high, from_left, from_right, sems, act):
    here = lax.axis_index("tm")
    last = lax.axis_size("tm") - 1
    sent_right, got_left, sent_left, got_right = sems

    def rightward():
        return remote(high, from_left, sent_right.at[step], got_left.at[step], {"tm": here + 1})

    def leftward():
        return remote(low, from_right, sent_left.at[step], got_right.at[step], {"tm": here - 1})

    if act == "start":

        @pl.when(here < last)
        def _():
            rightward().start()

        @pl.when(here > 0)
        def _():
            leftward().start()

    else:

        @pl.when(here < last)
        def _():
            rightward().wait_send()
            leftward().wait_recv()

        @pl.when(here > 0)
        def _():
            leftward().wait_send()
            rightward().wait_recv()


def first_moments(stats, norm):
    count_in = stats[4:5]
    mean = stats[0:1] / count_in
    rstd = lax.rsqrt(stats[1:2] / count_in - mean * mean + norm_epsilon)
    return mean, rstd, norm[0:1] * rstd, norm[1:2] - norm[0:1] * rstd * mean


def one_hot_rows(rows, columns):
    row = lax.broadcasted_iota(jnp.int32, (rows, columns), 0)
    col = lax.broadcasted_iota(jnp.int32, (rows, columns), 1)
    return (row // GROUP == col).astype(bf16)


def prepare(
    length_ref, frame_ref, subset_ref, edge_ref, graph_ref, short_ref, taps_ref,
    m_ref, em_ref, kron_ref, kront_ref, own_ref, gm_ref, wg_ref, wgt_ref, ws_ref, wst_ref, low_ref,
):
    clips, frames = frame_ref.shape
    first = lax.axis_index("tm") * frames
    row = lax.broadcasted_iota(jnp.int32, (clips, frames), 0)
    ids = lax.broadcasted_iota(jnp.int32, (clips, frames), 1) + first
    ends = jnp.zeros((clips, frames), jnp.int32)
    for clip in range(clips):
        ends = jnp.where(row == clip, length_ref[clip], ends)
    mask = ((ids < ends) & (frame_ref[...] > 0)).astype(bf16)
    every = jnp.ones((frames, 128), bf16)

    def spread(rows, clip_of, frame_of):
        at = lax.broadcasted_iota(jnp.int32, (rows, clips), 0)
        chosen = (clip_of(at) == lax.broadcasted_iota(jnp.int32, (rows, clips), 1)).astype(bf16)
        lines = dot(chosen, mask)
        at = lax.broadcasted_iota(jnp.int32, (rows, frames), 0)
        kept = frame_of(at) == lax.broadcasted_iota(jnp.int32, (rows, frames), 1)
        return dot(jnp.where(kept, lines, 0.0).astype(bf16), every)

    side = 2 * GROUP
    m_ref[...] = spread(
        clips * frames,
        lambda at: 2 * (at // (PHASES * side)) + at // GROUP % 2,
        lambda at: PHASES * (at % GROUP) + at // side % PHASES,
    )
    em_ref[...] = spread(
        clips * GROUP, lambda at: at // GROUP, lambda at: (at % GROUP + frames - 4) % frames
    )
    subsets = subset_ref[...]
    degree = jnp.sum((subsets > 0).astype(f32), axis=0, keepdims=True)
    lift = one_hot_rows(HALF_ROWS, JOINTS)
    row = lax.broadcasted_iota(jnp.int32, (JOINTS, C_OUT), 0)
    drop = (row == lax.broadcasted_iota(jnp.int32, (JOINTS, C_OUT), 1) // GROUP).astype(bf16)
    row = lax.broadcasted_iota(jnp.int32, (HALF_ROWS, C_OUT), 0)
    same = row % GROUP == lax.broadcasted_iota(jnp.int32, (HALF_ROWS, C_OUT), 1) % GROUP
    for k in range(SUBSETS):
        share = (subsets == k + 1).astype(f32) / degree
        gm_ref[k] = share
        low = (share * edge_ref[k]).astype(bf16)
        if k == 0:
            row = lax.broadcasted_iota(jnp.int32, (JOINTS, JOINTS), 0)
            col = lax.broadcasted_iota(jnp.int32, (JOINTS, JOINTS), 1)
            diagonal = jnp.sum(jnp.where(row == col, low.astype(f32), 0.0), axis=1, keepdims=True)
            wide = jnp.broadcast_to(diagonal, (JOINTS, C_IN)).astype(bf16)
            own_ref[...] = dot(lift, wide).reshape(JOINTS, GROUP, C_IN)
        else:
            ahead = dot(lift, dot_tn(low, drop).astype(bf16))
            rows = slice((k - 1) * HALF_ROWS, k * HALF_ROWS)
            kron_ref[rows, :] = jnp.where(same, ahead, 0.0).astype(bf16)
            behind = dot(lift, dot(low, drop).astype(bf16))
            lanes = slice((k - 1) * C_OUT, k * C_OUT)
            kront_ref[:, lanes] = jnp.where(same, behind, 0.0).astype(bf16)
        block = graph_ref[:, k * C_OUT : (k + 1) * C_OUT]
        wg_ref[k * C_IN : (k + 1) * C_IN, :] = block.astype(bf16)
        wgt_ref[:, k * C_IN : (k + 1) * C_IN] = block.T.astype(bf16)
    ws_ref[...] = short_ref[...].astype(bf16)
    wst_ref[...] = short_ref[...].T.astype(bf16)
    low_ref[...] = taps_ref[...].astype(bf16)


def mix_rows(parts, scales, kron_ref, pad_ref):
    wide = jnp.concatenate([part.reshape(HALF_ROWS, C_IN) for part in parts], axis=1)
    pad_ref[0:HALF_ROWS, :] = wide.astype(bf16)
    mixed = dot(kron_ref[...], pad_ref[...])
    sides = []
    for side in range(2):
        lanes = slice(side * HALF, (side + 1) * HALF)
        sides.append(
            jnp.concatenate(
                [
                    parts[side] * scales,
                    mixed[0:HALF_ROWS, lanes].reshape(JOINTS, GROUP, C_IN),
                    mixed[HALF_ROWS : 2 * HALF_ROWS, lanes].reshape(JOINTS, GROUP, C_IN),
                ],
                axis=2,
            )
        )
    return jnp.concatenate(sides, axis=1).reshape(ROWS, SUBSETS * C_IN).astype(bf16)


def graph_forward(
    x_ref, m_ref, em_ref, kron_ref, own_ref, wg_ref, ws_ref,
    xg_ref, xq_ref, xe_ref, h_ref, st_ref, rim_ref, rim_mask_ref,
    xs, sums, counts, mine, lefts, rights, mask_lefts, mask_rights,
    sent_right, got_left, sent_left, got_right, *sum_buffers,
):
    step = pl.program_id(0)
    last = pl.num_programs(0) - 1
    sems = (sent_right, got_left, sent_left, got_right)

    def rims(at, act):
        with_neighbours(at, mine.at[at], mine.at[at], lefts.at[at], rights.at[at], sems, act)

    def rim_masks(act):
        with_neighbours(last + 1, em_ref, em_ref, mask_lefts, mask_rights, sems, act)

    @pl.when(step == 0)
    def _():
        for ref in (lefts, rights, mask_lefts, mask_rights):
            ref[...] = jnp.zeros_like(ref)
        greet()
        sums[...] = jnp.zeros_like(sums)
        counts[...] = jnp.zeros_like(counts)

    for side in range(2):
        for joint in range(JOINTS):
            xs[side, joint] = x_ref[side, joint].astype(f32)
    tail = x_ref.shape[2] - 4
    ends = [
        jnp.concatenate([xs[side, :, tail:, :], xs[side, :, 0:4, :]], axis=1) for side in range(2)
    ]
    mine[step] = jnp.concatenate(ends, axis=1).astype(bf16)

    @pl.when(step == 0)
    def _():
        await_greetings()
        rim_masks("start")

    rims(step, "start")
    own = own_ref[...]
    for c in range(PHASES):
        mask = m_ref[0, c]
        parts = [
            xs[side, :, pl.ds(c, GROUP, stride=PHASES), :]
            * mask[side * GROUP : (side + 1) * GROUP][None]
            for side in range(2)
        ]
        xq_ref[0, c, HALF_ROWS:, :] = jnp.zeros((C_OUT - HALF_ROWS, C_OUT), bf16)
        xg = mix_rows(parts, own, kron_ref, xq_ref.at[0, c])
        xg_ref[0, c] = xg
        hidden = dot(xg, wg_ref[...])
        h_ref[0, c] = hidden.astype(bf16)
        sums[0] += fold(hidden)
        sums[1] += fold(hidden * hidden)
        counts[0] += mask
        if c % 2 == 0:
            counts[1] += mask
            even = jnp.concatenate(parts, axis=1).reshape(ROWS, C_IN).astype(bf16)
            xe_ref[0, c // 2] = even
            short = dot(even, ws_ref[...])
            sums[2] += fold(short)
            sums[3] += fold(short * short)

    @pl.when(step == last)
    def _():
        rows = [jnp.sum(sums[k], axis=0, keepdims=True) for k in range(4)]
        for k in range(2):
            total = JOINTS * jnp.sum(counts[k], axis=0, keepdims=True)
            rows.append(jnp.concatenate([total, total], axis=1))
        rows.append(jnp.zeros((2, C_OUT), f32))
        st_ref[...] = sum_all(jnp.concatenate(rows, axis=0), as_buffers(sum_buffers))
        rim_masks("wait")
        sub = lax.broadcasted_iota(jnp.int32, mask_lefts.shape, 0) % GROUP
        rim_mask_ref[...] = jnp.where(sub < 4, mask_lefts[...], mask_rights[...])
        for pair in range(lefts.shape[0]):
            rims(pair, "wait")
            sub = lax.broadcasted_iota(jnp.int32, lefts.shape[1:], 1) % GROUP
            both = jnp.where(sub < 4, lefts[pair].astype(f32), rights[pair].astype(f32))
            rim_ref[pair] = both.astype(bf16)


def insert_and_roll(tiles, fill, side):
    sub = lax.broadcasted_iota(jnp.int32, tiles.shape, 1)
    joined = jnp.where(sub == side, fill, tiles)
    return pltpu.roll(joined, 1 if side == 7 else GROUP - 1, 1)


def conv_forward(
    h_ref, xh_ref, m_ref, mh_ref, st_ref, norm_ref, kron_ref, own_ref, wg_ref, taps_ref,
    a_ref, conv_ref, out_ref,
    pad, rims, fills, sums, *sum_buffers,
):
    step = pl.program_id(0)

    @pl.when(step == 0)
    def _():
        greet()
        sums[...] = jnp.zeros_like(sums)
        pad[...] = jnp.zeros_like(pad)

    _, _, scale, shift = first_moments(st_ref[...], norm_ref[...])
    scale, shift = 0.5 * scale, 0.5 * shift

    def activate(values, mask):
        half = values * scale + shift
        return (half + half * jnp.tanh(half)).reshape(-1, 2 * GROUP, C_OUT) * mask

    def wide(mask):
        return jnp.concatenate([mask, mask], axis=1)[None]

    rim_mask = mh_ref[...]
    rim_rows = xh_ref[0].astype(f32) * rim_mask[None]
    parts = [rim_rows[:, side * GROUP : (side + 1) * GROUP] for side in range(2)]
    rim_hidden = dot(mix_rows(parts, own_ref[...], kron_ref, pad), wg_ref[...])
    rim_active = activate(rim_hidden, wide(rim_mask)).reshape(ROWS, C_OUT)
    for lane in range(2):
        rims[lane] = rim_active[:, lane * HALF : (lane + 1) * HALF]
    for p in range(2):
        for q in range(2):
            for lane in range(2):
                fills[2 * p + q, lane, pl.ds(7, UNITS, stride=GROUP), :] = rims[
                    lane, pl.ds(2 * q + p, UNITS, stride=GROUP), :
                ]
                fills[2 * p + q, lane, pl.ds(0, UNITS, stride=GROUP), :] = rims[
                    lane, pl.ds(4 + 2 * q + p, UNITS, stride=GROUP), :
                ]

    for c in range(PHASES):
        p, q = c % 2, c // 2
        mask = wide(m_ref[0, c])
        for start in range(0, JOINTS, CUT):
            rows = slice(start * 2 * GROUP, (start + CUT) * 2 * GROUP)
            active = activate(h_ref[0, c, rows, :].astype(f32), mask)
            a_ref[0, p, q + 2, rows, :] = active.reshape(-1, C_OUT).astype(bf16)
            if p == 1 and q == 1:
                continue
            tiles = active.reshape(-1, GROUP, C_OUT)
            fill = jnp.concatenate(
                [fills[2 * p + q % 2, lane, rows, :] for lane in range(2)], axis=1
            ).reshape(-1, GROUP, C_OUT)
            moved = insert_and_roll(tiles, fill, 7 if q >= 2 else 0)
            at = q - 2 if q >= 2 else q + 6
            a_ref[0, p, at, rows, :] = moved.reshape(-1, C_OUT).astype(bf16)

    total = None
    for j in range(TAPS):
        window = a_ref[0, j % 2, j // 2 : j // 2 + 4].reshape(4 * ROWS, C_OUT)
        part = dot(window, taps_ref[j])
        total = part if total is None else total + part
    conv_ref[0] = total.reshape(4, ROWS, C_OUT)
    for q in range(4):
        block = total[q * ROWS : (q + 1) * ROWS].reshape(JOINTS, 2 * GROUP, C_OUT)
        live = block * wide(m_ref[0, 2 * q])
        sums[0] += fold(live)
        sums[1] += fold(live * block)

    @pl.when(step == pl.num_programs(0) - 1)
    def _():
        await_greetings()
        rows = [jnp.sum(sums[k], axis=0, keepdims=True) for k in range(2)]
        rows.append(jnp.zeros((6, C_OUT), f32))
        out_ref[...] = sum_all(jnp.concatenate(rows, axis=0), as_buffers(sum_buffers))


def second_moments(stats, conv_stats):
    count_out = stats[5:6]
    mean_conv = conv_stats[0:1] / count_out
    rstd_conv = lax.rsqrt(conv_stats[1:2] / count_out - mean_conv * mean_conv + norm_epsilon)
    mean_short = stats[2:3] / count_out
    rstd_short = lax.rsqrt(stats[3:4] / count_out - mean_short * mean_short + norm_epsilon)
    return mean_conv, rstd_conv, mean_short, rstd_short


def output_part(
    conv_ref, xe_ref, cot_ref, m_ref, st_ref, cs_ref, norm_ref, ws_ref,
    o_ref, up_ref, out_ref,
    cots, outs, sums,
):
    step = pl.program_id(0)

    @pl.when(step == 0)
    def _():
        sums[...] = jnp.zeros_like(sums)

    norm = norm_ref[...]
    mean_conv, rstd_conv, mean_short, rstd_short = second_moments(st_ref[...], cs_ref[...])
    scale_conv = 0.5 * norm[2:3] * rstd_conv
    scale_short = 0.5 * norm[4:5] * rstd_short
    shift = 0.5 * (norm[3:4] + norm[5:6]) - scale_conv * mean_conv - scale_short * mean_short
    for side in range(2):
        for joint in range(JOINTS):
            for lane in range(2):
                cots[side, lane, joint] = cot_ref[
                    side, joint, :, lane * HALF : (lane + 1) * HALF
                ].astype(f32)
    for q in range(4):
        mask = m_ref[0, 2 * q]
        mask = jnp.concatenate([mask, mask], axis=1)[None]
        short_all = dot(xe_ref[0, q], ws_ref[...])
        for start in range(0, JOINTS, CUT):
            rows = slice(start * 2 * GROUP, (start + CUT) * 2 * GROUP)
            conv = conv_ref[0, q, rows, :]
            short = short_all[rows]
            half = conv * scale_conv + short * scale_short + shift
            turn = jnp.tanh(half)
            grow = (0.5 + 0.5 * turn).reshape(CUT, 2 * GROUP, C_OUT) * mask
            half = half.reshape(CUT, 2 * GROUP, C_OUT)
            turn = turn.reshape(CUT, 2 * GROUP, C_OUT)
            result = (half + half) * grow
            slope = grow + grow * (half - half * turn)
            cot = jnp.concatenate(
                [
                    jnp.concatenate(
                        [
                            cots[side, lane, start : start + CUT, pl.ds(q, GROUP, stride=4), :]
                            for lane in range(2)
                        ],
                        axis=2,
                    )
                    for side in range(2)
                ],
                axis=1,
            )
            for side in range(2):
                for lane in range(2):
                    outs[side, lane, start : start + CUT, pl.ds(q, GROUP, stride=4), :] = result[
                        :, side * GROUP : (side + 1) * GROUP, lane * HALF : (lane + 1) * HALF
                    ]
            up = (cot * slope).reshape(-1, C_OUT)
            up_ref[0, q, rows, :] = up
            sums[0] += fold(up)
            sums[1] += fold(up * conv)
            sums[2] += fold(up * short)
    for side in range(2):
        for joint in range(JOINTS):
            for lane in range(2):
                o_ref[side, joint, :, lane * HALF : (lane + 1) * HALF] = outs[
                    side, lane, joint
                ].astype(bf16)

    @pl.when(step == pl.num_programs(0) - 1)
    def _():
        rows = [jnp.sum(sums[k], axis=0, keepdims=True) for k in range(3)]
        rows.append(jnp.zeros((5, C_OUT), f32))
        out_ref[...] = jnp.concatenate(rows, axis=0)


def back_totals(back, moments):
    mean_conv, rstd_conv, mean_short, rstd_short = moments
    back_sum = back[0:1]
    back_conv = rstd_conv * (back[1:2] - mean_conv * back_sum)
    back_short = rstd_short * (back[2:3] - mean_short * back_sum)
    return back_sum, back_conv, back_short


def weight_part(
    conv_ref, up_ref, xe_ref, a_ref, m_ref, st_ref, cs_ref, bk_ref, norm_ref, ws_ref,
    cg_ref, sg_ref, left_ref, right_ref, grad_ref, total_ref,
    turned, edges, tg, shg, low_rims, high_rims, lefts, rights,
    sent_right, got_left, sent_left, got_right, *sum_buffers,
):
    step = pl.program_id(0)
    last = pl.num_programs(0) - 1
    sems = (sent_right, got_left, sent_left, got_right)

    def rims(at, act):
        with_neighbours(
            at, low_rims.at[at], high_rims.at[at], lefts.at[at], rights.at[at], sems, act
        )

    @pl.when(step == 0)
    def _():
        lefts[...] = jnp.zeros_like(lefts)
        rights[...] = jnp.zeros_like(rights)
        greet()
        tg[...] = jnp.zeros_like(tg)
        shg[...] = jnp.zeros_like(shg)
        low_rims[...] = jnp.zeros_like(low_rims)
        high_rims[...] = jnp.zeros_like(high_rims)
        await_greetings()
        total_ref[...] = sum_all(bk_ref[...], as_buffers(sum_buffers))

    norm = norm_ref[...]
    stats = st_ref[...]
    moments = second_moments(stats, cs_ref[...])
    mean_conv, rstd_conv, mean_short, rstd_short = moments
    back_sum, back_conv, back_short = back_totals(total_ref[...], moments)
    count_out = stats[5:6]

    def terms(gain, mean, rstd, back):
        lead = gain * rstd
        slope = lead * rstd * back / count_out
        return lead, slope, lead * back_sum / count_out - slope * mean

    lead_c, slope_c, shift_c = terms(norm[2:3], mean_conv, rstd_conv, back_conv)
    lead_s, slope_s, shift_s = terms(norm[4:5], mean_short, rstd_short, back_short)
    for q in range(4):
        mask = m_ref[0, 2 * q]
        mask = jnp.concatenate([mask, mask], axis=1)[None]
        short_all = dot(xe_ref[0, q], ws_ref[...])
        for start in range(0, JOINTS, CUT):
            rows = slice(start * 2 * GROUP, (start + CUT) * 2 * GROUP)
            up = up_ref[0, q, rows, :]

            def masked(values):
                return (values.reshape(CUT, 2 * GROUP, C_OUT) * mask).reshape(-1, C_OUT)

            cg = up * lead_c - masked(conv_ref[0, q, rows, :] * slope_c + shift_c)
            cg_ref[0, q, rows, :] = cg.astype(bf16)
            for lane in range(2):
                edges[lane, rows, :] = cg[:, lane * HALF : (lane + 1) * HALF]
            sg = up * lead_s - masked(short_all[rows] * slope_s + shift_s)
            sg_ref[0, q, rows, :] = sg.astype(bf16)
        for lane in range(2):
            at = slice(lane * HALF, (lane + 1) * HALF)
            target = low_rims if q < 2 else high_rims
            outer = edges[lane, pl.ds(0 if q < 2 else 7, UNITS, stride=GROUP), :]
            target[step, q % 2, 0:UNITS, at] = outer.astype(bf16)
    rims(step, "start")
    turned[...] = cg_ref[0].reshape(4 * ROWS, C_OUT).T
    for j in range(TAPS):
        window = a_ref[0, j % 2, j // 2 : j // 2 + 4].reshape(4 * ROWS, C_OUT)
        tg[j] += dot(turned[...], window)
    shg[...] += dot_tn(
        xe_ref[0].reshape(4 * ROWS, C_IN), sg_ref[0].reshape(4 * ROWS, C_OUT)
    )

    @pl.when(step == last)
    def _():
        for j in range(TAPS):
            grad_ref[j * C_OUT : (j + 1) * C_OUT, :] = tg[j].astype(bf16)
        grad_ref[TAPS * C_OUT : TAPS * C_OUT + C_IN, :] = shg[...].astype(bf16)
        rest = grad_ref.shape[0] - TAPS * C_OUT - C_IN
        if rest:
            grad_ref[TAPS * C_OUT + C_IN :, :] = jnp.zeros((rest, C_OUT), bf16)
        for pair in range(lefts.shape[0]):
            rims(pair, "wait")
        left_ref[...] = lefts[...]
        right_ref[...] = rights[...]


class Sharing:
    def __init__(self, source, refs):
        self.source = source
        self.here, self.up, self.out = refs[0:3]
        self.firsts, self.seconds, self.thirds, self.gathered, self.joined, self.full = refs[3:9]
        self.sems = refs[9:21]
        tm = lax.axis_index("tm")
        self.core = tm % 2
        self.line = tm // 2
        self.lines = lax.axis_size("tm") // 2
        self.batch = lax.axis_index("batch")
        self.batches = lax.axis_size("batch")
        self.half = source.shape[0] // 2
        self.part = self.half // self.lines
        self.piece = self.part // self.batches

    @staticmethod
    def padded(rows):
        unit = 16 * lax.axis_size("tm") * lax.axis_size("batch")
        return (rows + unit - 1) // unit * unit

    @staticmethod
    def scratch(rows):
        lines, batches = lax.axis_size("tm") // 2, lax.axis_size("batch")
        half = rows // 2
        part = half // lines
        piece = part // batches
        found = [
            pltpu.VMEM(shape, bf16)
            for shape in (
                (half, C_OUT),
                (part, C_OUT),
                (piece, C_OUT),
                (half, C_OUT),
                (lines, part, C_OUT),
                (batches, piece, C_OUT),
                (batches, piece, C_OUT),
                (lines, part, C_OUT),
                (2, half, C_OUT),
            )
        ]
        for count in (1, lines, batches, batches, lines, 1):
            found += [pltpu.SemaphoreType.DMA((count,))] * 2
        return found

    def core_peer(self):
        return {"tm": 2 * self.line + 1 - self.core}

    def line_peers(self):
        for d in range(1, self.lines):
            to = lax.rem(self.line + d, self.lines)
            yield d, to, {"tm": 2 * to + self.core}

    def batch_peers(self):
        for d in range(1, self.batches):
            to = lax.rem(self.batch + d, self.batches)
            yield d, to, {"batch": to}

    def rows(self, index, count):
        return pl.ds(pl.multiple_of(index * count, 16), count)

    def copies(self, level):
        sent, got = self.sems[2 * level], self.sems[2 * level + 1]
        if level == 0:
            source = self.source.at[self.rows(1 - self.core, self.half)]
            return [remote(source, self.firsts, sent.at[0], got.at[0], self.core_peer())]
        if level == 1:
            return [
                remote(
                    self.here.at[self.rows(to, self.part)], self.seconds.at[self.line],
                    sent.at[d], got.at[d], device,
                )
                for d, to, device in self.line_peers()
            ]
        if level == 2:
            return [
                remote(
                    self.up.at[self.rows(to, self.piece)], self.thirds.at[self.batch],
                    sent.at[d], got.at[d], device,
                )
                for d, to, device in self.batch_peers()
            ]
        if level == 3:
            slot = self.gathered.at[self.batch]
            return [
                remote(slot, slot, sent.at[d], got.at[d], device)
                for d, _, device in self.batch_peers()
            ]
        if level == 4:
            slot = self.joined.at[self.line]
            return [
                remote(slot, slot, sent.at[d], got.at[d], device)
                for d, _, device in self.line_peers()
            ]
        slot = self.full.at[self.core]
        return [remote(slot, slot, sent.at[0], got.at[0], self.core_peer())]

    def start(self, level):
        if level == 3:
            self.gathered[self.batch] = self.out[...]
        if level == 4:
            self.joined[self.line] = self.gathered[...].reshape(self.part, C_OUT)
        if level == 5:
            self.full[self.core] = self.joined[...].reshape(self.half, C_OUT)
        for copy in self.copies(level):
            copy.start()

    def end(self, level):
        for copy in self.copies(level):
            copy.wait()
        if level == 0:
            own = self.source[self.rows(self.core, self.half), :].astype(f32)
            self.here[...] = (own + self.firsts[...].astype(f32)).astype(bf16)
        if level == 1:
            own = self.here[self.rows(self.line, self.part), :].astype(f32)
            for d in range(1, self.lines):
                own = own + self.seconds[lax.rem(self.line + d, self.lines)].astype(f32)
            self.up[...] = own.astype(bf16)
        if level == 2:
            own = self.up[self.rows(self.batch, self.piece), :].astype(f32)
            for d in range(1, self.batches):
                own = own + self.thirds[lax.rem(self.batch + d, self.batches)].astype(f32)
            self.out[...] = own.astype(bf16)

    def next(self, level):
        self.end(level)
        if level < 5:
            self.start(level + 1)


def conv_back(
    cg_ref, left_ref, right_ref, taps_ref, h_ref, m_ref, st_ref, norm_ref, xg_ref, grad_ref,
    hg_ref, out_ref, sum_ref, gg_ref,
    fills, ext, sums, fg, gg, *buffers,
):
    step = pl.program_id(0)
    pairs = pl.num_programs(0) // 2
    sharing = Sharing(grad_ref, buffers[6:])
    stats = st_ref[...]
    norm = norm_ref[...]
    mean, rstd, scale, shift = first_moments(stats, norm)

    @pl.when(step == 0)
    def _():
        greet()
        sums[...] = jnp.zeros_like(sums)
        gg[...] = jnp.zeros_like(gg)

    @pl.when(step < pairs)
    def _():
        half_scale, half_shift = 0.5 * scale, 0.5 * shift
        for q in range(2):
            for lane in range(2):
                at = slice(lane * HALF, (lane + 1) * HALF)
                fills[q, lane, pl.ds(7, UNITS, stride=GROUP), :] = left_ref[
                    0, q, 0:UNITS, at
                ].astype(f32)
                fills[q, lane, pl.ds(0, UNITS, stride=GROUP), :] = right_ref[
                    0, q, 0:UNITS, at
                ].astype(f32)
        for q in range(4):
            ext[q + 2] = cg_ref[0, q]
            for start in range(0, JOINTS, CUT):
                rows = slice(start * 2 * GROUP, (start + CUT) * 2 * GROUP)
                tiles = cg_ref[0, q, rows, :].astype(f32).reshape(-1, GROUP, C_OUT)
                fill = jnp.concatenate([fills[q % 2, lane, rows, :] for lane in range(2)], axis=1)
                fill = fill.reshape(-1, GROUP, C_OUT)
                moved = insert_and_roll(tiles, fill, 7 if q >= 2 else 0)
                at = q - 2 if q >= 2 else q + 6
                ext[at, rows, :] = moved.reshape(-1, C_OUT).astype(bf16)
        for p in range(2):
            total = None
            for i in range(5 - p):
                window = ext[4 - i : 8 - i].reshape(4 * ROWS, C_OUT)
                part = dot_nt(window, taps_ref[2 * i + p])
                total = part if total is None else total + part
            for q in range(4):
                c = 2 * q + p
                mask = 0.5 * m_ref[0, c]
                mask = jnp.concatenate([mask, mask], axis=1)[None]
                for start in range(0, JOINTS, CUT):
                    rows = slice(start * 2 * GROUP, (start + CUT) * 2 * GROUP)
                    hidden = h_ref[0, c, rows, :].astype(f32)
                    half = hidden * half_scale + half_shift
                    turn = jnp.tanh(half)
                    slope = (1.0 + turn) * (1.0 + (half - half * turn))
                    slope = (slope.reshape(CUT, 2 * GROUP, C_OUT) * mask).reshape(-1, C_OUT)
                    grad = total[q * ROWS + rows.start : q * ROWS + rows.stop] * slope
                    fg[step, c, rows, :] = grad
                    sums[0] += fold(grad)
                    sums[1] += fold(grad * hidden)

    @pl.when(step >= pairs)
    def _():
        pair = step - pairs
        count_in = stats[4:5]
        back_sum = out_ref[0:1]
        back_norm = rstd * (out_ref[1:2] - mean * back_sum)
        lead = norm[0:1] * rstd
        slope = lead * rstd * back_norm / count_in
        offset = lead * back_sum / count_in - slope * mean
        for c in range(PHASES):
            mask = m_ref[0, c]
            mask = jnp.concatenate([mask, mask], axis=1)[None]
            for start in range(0, JOINTS, CUT):
                rows = slice(start * 2 * GROUP, (start + CUT) * 2 * GROUP)
                hidden = h_ref[0, c, rows, :].astype(f32)
                taken = (hidden * slope + offset).reshape(CUT, 2 * GROUP, C_OUT) * mask
                taken = taken.reshape(-1, C_OUT)
                hg_ref[0, c, rows, :] = (fg[pair, c, rows, :] * lead - taken).astype(bf16)
        gg[...] += dot_tn(
            xg_ref[0].reshape(PHASES * ROWS, SUBSETS * C_IN),
            hg_ref[0].reshape(PHASES * ROWS, C_OUT),
        )

    @pl.when(step == 0)
    def _():
        await_greetings()
        sharing.start(0)

    for level, at in ((0, 1), (1, 3)):

        @pl.when(step == at)
        def _(level=level):
            sharing.next(level)

    @pl.when(step == pairs - 1)
    def _():
        rows = [jnp.sum(sums[k], axis=0, keepdims=True) for k in range(2)]
        rows.append(jnp.zeros((6, C_OUT), f32))
        sharing.end(2)
        out_ref[...] = sum_all(jnp.concatenate(rows, axis=0), as_buffers(buffers[0:6]))
        sharing.start(3)

    for level, at in ((3, pairs + 1), (4, pairs + 3)):

        @pl.when(step == at)
        def _(level=level):
            sharing.next(level)

    @pl.when(step == 2 * pairs - 1)
    def _():
        gg_ref[0 : SUBSETS * C_IN, :] = gg[...].astype(bf16)
        rest = gg_ref.shape[0] - SUBSETS * C_IN
        if rest:
            gg_ref[SUBSETS * C_IN :, :] = jnp.zeros((rest, C_OUT), bf16)
        sharing.end(5)
        sum_ref[...] = sharing.full[...].reshape(sum_ref.shape)


def graph_back(
    hg_ref, xq_ref, sg_ref, wgt_ref, wst_ref, kront_ref, own_ref, grad_ref,
    ig_ref, sum_ref, edge_ref,
    spread, natural, eg, own_grad, *buffers,
):
    step = pl.program_id(0)
    last = pl.num_programs(0) - 1
    sharing = Sharing(grad_ref, buffers[6:])

    @pl.when(step == 0)
    def _():
        greet()
        eg[...] = jnp.zeros_like(eg)
        own_grad[...] = jnp.zeros_like(own_grad)
        spread[...] = jnp.zeros_like(spread)
        await_greetings()
        sharing.start(0)

    own = own_ref[...]
    own = jnp.concatenate([own, own], axis=2)

    def side_by_side(values):
        return jnp.concatenate([values[:, 0:GROUP], values[:, GROUP : 2 * GROUP]], axis=2)

    for c in range(PHASES):
        back = dot(hg_ref[0, c], wgt_ref[...]).reshape(JOINTS, 2 * GROUP, SUBSETS * C_IN)
        for k in range(2):
            lanes = slice((k + 1) * C_IN, (k + 2) * C_IN)
            spread[c % 2, k, 0:HALF_ROWS, :] = (
                side_by_side(back[:, :, lanes]).reshape(HALF_ROWS, 2 * C_IN).astype(bf16)
            )
        direct = side_by_side(back[:, :, 0:C_IN])
        both = spread[c % 2].reshape(2 * C_OUT, C_OUT)
        result = dot(kront_ref[...], both).reshape(JOINTS, GROUP, 2 * C_IN) + direct * own
        if c % 2 == 0:
            short = dot(sg_ref[0, c // 2], wst_ref[...]).reshape(JOINTS, 2 * GROUP, C_IN)
            result = result + side_by_side(short)
        for side in range(2):
            natural[side, :, pl.ds(c, GROUP, stride=PHASES), :] = result[
                :, :, side * C_IN : (side + 1) * C_IN
            ]
        eg[...] += dot_nt(both, xq_ref[0, c])
        seen = xq_ref[0, c, 0:HALF_ROWS, :].astype(f32).reshape(JOINTS, GROUP, 2 * C_IN)
        own_grad[...] += seen * direct
    for side in range(2):
        for joint in range(JOINTS):
            ig_ref[side, joint] = natural[side, joint].astype(bf16)

    for level in range(5):

        @pl.when(step == min(level + 1, 5))
        def _(level=level):
            sharing.next(level)

    @pl.when(step == last)
    def _():
        lines = lax.broadcasted_iota(jnp.int32, (C_OUT, C_OUT), 0)
        spots = lax.broadcasted_iota(jnp.int32, (C_OUT, C_OUT), 1)
        same = lines % GROUP == spots % GROUP
        down = (lax.broadcasted_iota(jnp.int32, (32, C_OUT), 0) == lax.broadcasted_iota(
            jnp.int32, (32, C_OUT), 1
        ) // GROUP).astype(f32)
        sums = jnp.sum(own_grad[...], axis=1)
        sums = jnp.sum(sums, axis=1, keepdims=True)
        row = lax.broadcasted_iota(jnp.int32, (JOINTS, 128), 0)
        col = lax.broadcasted_iota(jnp.int32, (JOINTS, 128), 1)
        packed = jnp.where(row == col, jnp.broadcast_to(sums, (JOINTS, 128)), 0.0)
        packed = jnp.concatenate([packed, jnp.zeros((32 - JOINTS, 128), f32)], axis=0)
        for k in range(2):
            kept = jnp.where(same, eg[k * C_OUT : (k + 1) * C_OUT, :], 0.0)
            narrow = lax.dot_general(
                down, kept, (((1,), (1,)), ((), ())),
                preferred_element_type=f32, precision=lax.Precision.HIGHEST,
            )
            row = lax.broadcasted_iota(jnp.int32, (C_OUT, 128), 0)
            col = lax.broadcasted_iota(jnp.int32, (C_OUT, 128), 1)
            place = (row // GROUP + 32 * (k + 1) == col).astype(f32)
            packed = packed + jnp.dot(
                narrow, place, preferred_element_type=f32, precision=lax.Precision.HIGHEST
            )
        edge_ref[...] = sum_all(packed, as_buffers(buffers[0:6]))
        sharing.end(5)
        sum_ref[...] = sharing.full[...].reshape(sum_ref.shape)


def update(
    grads_ref, graph_grad_ref, edge_grad_ref, gm_ref, st_ref, cs_ref, bk_ref, fs_ref, ig_ref,
    *refs,
):
    groups = [refs[4 * k : 4 * k + 4] for k in range(5)]
    out_ig, out_norm = refs[20:22]
    outs = [refs[22 + 4 * k : 26 + 4 * k] for k in range(5)]
    squares, norm_grad = refs[42:44]
    step = pl.program_id(0)
    taps_rows = TAPS * C_OUT

    def edge_grad(k):
        values = edge_grad_ref[...]
        if k:
            values = pltpu.roll(values, 128 - 32 * k, 1)
        return values[0:JOINTS, 0:JOINTS] * gm_ref[k]

    def apply(group, out, at, gradient, rate, decay):
        factor = squares[0:1, 0:1]
        new = adam_update(*[ref[at] for ref in group], gradient, factor, rate, decay)
        for ref, value in zip(out, new):
            ref[at] = value

    @pl.when(step == 0)
    def _():
        stats = st_ref[...]
        norm = groups[4][0][...]
        mean, rstd, _, _ = first_moments(stats, norm)
        first_sum = fs_ref[0:1]
        first_norm = rstd * (fs_ref[1:2] - mean * first_sum)
        back_sum, back_conv, back_short = back_totals(
            bk_ref[...], second_moments(stats, cs_ref[...])
        )
        norm_grad[...] = jnp.concatenate(
            [first_norm, first_sum, back_conv, back_sum, back_short, back_sum], axis=0
        )
        total = jnp.zeros((GROUP, C_OUT), f32)
        for start in range(0, taps_rows + C_IN, C_IN):
            rows = grads_ref[start : start + C_IN, :].astype(f32)
            total = total + fold(rows * rows)
        for start in range(0, SUBSETS * C_IN, C_IN):
            rows = graph_grad_ref[start : start + C_IN, :].astype(f32)
            total = total + fold(rows * rows)
        whole = jnp.sum(total) + jnp.sum(norm_grad[...] * norm_grad[...])
        for k in range(SUBSETS):
            values = edge_grad(k)
            whole = whole + jnp.sum(values * values)
        size = jnp.sqrt(jnp.full((GROUP, 128), whole, f32))
        squares[...] = jnp.minimum(1.0, clip_limit / (size + 1e-06))
        out_norm[...] = size
        every = (slice(None), slice(None))
        apply(groups[4], outs[4], every, norm_grad[...], rate_small, 0.0)
        for k in range(SUBSETS):
            apply(groups[3], outs[3], k, edge_grad(k), rate_small, 0.0)

    @pl.when(step < TAPS)
    def _():
        rows = grads_ref[pl.ds(pl.multiple_of(step * C_OUT, C_OUT), C_OUT), :].astype(f32)
        apply(groups[1], outs[1], 0, rows.T, rate_matrix, decay_matrix)

    @pl.when(step >= TAPS)
    def _():
        k = step - TAPS
        rows = graph_grad_ref[pl.ds(pl.multiple_of(k * C_IN, C_IN), C_IN), :].astype(f32)
        every = (slice(None), slice(None))
        apply(groups[0], outs[0], every, rows, rate_matrix, decay_matrix)

    @pl.when(step == TAPS)
    def _():
        rows = grads_ref[taps_rows : taps_rows + C_IN, :].astype(f32)
        every = (slice(None), slice(None))
        apply(groups[2], outs[2], every, rows, rate_matrix, decay_matrix)

    out_ig[...] = ig_ref[...]


def whole_spec(shape):
    return pl.BlockSpec(shape, lambda i: (0,) * len(shape))


def lead_spec(shape):
    return pl.BlockSpec(shape, lambda i: (i,) + (0,) * (len(shape) - 1))


def spec(block, index):
    return pl.BlockSpec(block, index)


def by_step(block):
    return spec(block, lambda i: (i,) + (0,) * (len(block) - 1))


def call(body, steps, ins, outs, scratch, name, **more):
    def to_spec(where, shape):
        if where is None:
            return whole_spec(shape)
        return where if isinstance(where, pl.BlockSpec) else by_step(where)

    return pl.pallas_call(
        body,
        grid=(steps,),
        in_specs=[to_spec(where, array.shape) for array, where in ins],
        out_specs=[to_spec(where, shape) for shape, _, where in outs],
        out_shape=[jax.ShapeDtypeStruct(shape, kind) for shape, kind, _ in outs],
        scratch_shapes=scratch,
        compiler_params=params(**more),
        name=name,
    )(*[array for array, _ in ins])


def shards(
    inputs, cotangent, lengths, frame_mask, subsets,
    graph_weight, graph_moment, graph_square, graph_average,
    temporal_weight, temporal_moment, temporal_square, temporal_average,
    shortcut_weight, shortcut_moment, shortcut_square, shortcut_average,
    edge_weight, edge_moment, edge_square, edge_average,
    norm_params, norm_moment, norm_square, norm_average,
):
    clips = inputs.shape[0]
    frames = inputs.shape[1]
    pairs = clips // 2
    natural = jnp.transpose(inputs, (0, 2, 1, 3))
    cot = jnp.transpose(cotangent, (0, 2, 1, 3))

    x_block = (2, JOINTS, frames, C_IN)
    mask_block = (1, PHASES, 2 * GROUP, 128)
    wide_block = (1, PHASES, ROWS, C_OUT)
    out_block = (1, 4, ROWS, C_OUT)
    xe_block = (1, 4, ROWS, C_IN)
    a_block = (1, 2, 8, ROWS, C_OUT)
    rim_block = (1, 2, 64, C_OUT)
    xg_block = (1, PHASES, ROWS, SUBSETS * C_IN)
    xq_block = (1, PHASES, C_OUT, C_OUT)
    cot_block = (2, JOINTS, frames // 2, C_OUT)
    edge_block = (1, JOINTS, 2 * GROUP, C_IN)
    small = (8, C_OUT)
    dma = pltpu.SemaphoreType.DMA

    def full(block):
        return (pairs,) + block[1:]

    vmem = pl.BlockSpec(memory_space=pltpu.VMEM)
    shapes = [
        ((clips * frames, 128), f32),
        ((clips * GROUP, 128), f32),
        ((2 * HALF_ROWS, C_OUT), bf16),
        ((HALF_ROWS, 2 * C_OUT), bf16),
        ((JOINTS, GROUP, C_IN), f32),
        ((SUBSETS, JOINTS, JOINTS), f32),
        ((SUBSETS * C_IN, C_OUT), bf16),
        ((C_OUT, SUBSETS * C_IN), bf16),
        ((C_IN, C_OUT), bf16),
        ((C_OUT, C_IN), bf16),
        ((TAPS, C_OUT, C_OUT), bf16),
    ]
    masks, edge_masks, kron, kront, own, graph_mask, wg, wgt, ws, wst, taps = pl.pallas_call(
        prepare,
        in_specs=[pl.BlockSpec(memory_space=pltpu.SMEM)] + [vmem] * 6,
        out_specs=[vmem] * 11,
        out_shape=[jax.ShapeDtypeStruct(shape, kind) for shape, kind in shapes],
        compiler_params=pltpu.CompilerParams(vmem_limit_bytes=60 * 2**20),
        name="prepare",
    )(lengths, frame_mask, subsets, edge_weight, graph_weight, shortcut_weight, temporal_weight)
    masks = masks.reshape(pairs, PHASES, 2 * GROUP, 128)

    xg, xq, xe, hidden, stats, rims, rim_mask = call(
        graph_forward,
        pairs,
        [
            (natural, x_block),
            (masks, mask_block),
            (edge_masks, None),
            (kron, None),
            (own, None),
            (wg, None),
            (ws, None),
        ],
        [
            (full(xg_block), bf16, xg_block),
            (full(xq_block), bf16, xq_block),
            (full(xe_block), bf16, xe_block),
            (full(wide_block), bf16, wide_block),
            (small, f32, None),
            (full(edge_block), bf16, None),
            (edge_masks.shape, f32, None),
        ],
        [
            pltpu.VMEM((2, JOINTS, frames, C_IN), f32),
            pltpu.VMEM((4, GROUP, C_OUT), f32),
            pltpu.VMEM((2, 2 * GROUP, 128), f32),
            pltpu.VMEM(full(edge_block), bf16),
            pltpu.VMEM(full(edge_block), bf16),
            pltpu.VMEM(full(edge_block), bf16),
            pltpu.VMEM(edge_masks.shape, f32),
            pltpu.VMEM(edge_masks.shape, f32),
        ]
        + [dma((pairs + 1,))] * 4
        + sum_scratch(),
        "graph_forward",
        collective_id=1,
        has_side_effects=True,
    )

    active, conv, conv_stats = call(
        conv_forward,
        pairs,
        [
            (hidden, wide_block),
            (rims, edge_block),
            (masks, mask_block),
            (rim_mask, (2 * GROUP, 128)),
            (stats, None),
            (norm_params, None),
            (kron, None),
            (own, None),
            (wg, None),
            (taps, None),
        ],
        [
            (full(a_block), bf16, a_block),
            (full(out_block), f32, out_block),
            (small, f32, None),
        ],
        [
            pltpu.VMEM((C_OUT, C_OUT), bf16),
            pltpu.VMEM((2, ROWS, HALF), f32),
            pltpu.VMEM((4, 2, ROWS, HALF), f32),
            pltpu.VMEM((2, GROUP, C_OUT), f32),
        ]
        + sum_scratch(),
        "conv_forward",
        collective_id=2,
        has_side_effects=True,
    )

    outputs, upstream, back = call(
        output_part,
        pairs,
        [
            (conv, out_block),
            (xe, xe_block),
            (cot, cot_block),
            (masks, mask_block),
            (stats, None),
            (conv_stats, None),
            (norm_params, None),
            (ws, None),
        ],
        [
            (cot.shape, bf16, cot_block),
            (full(out_block), f32, out_block),
            (small, f32, None),
        ],
        [
            pltpu.VMEM((2, 2, JOINTS, frames // 2, HALF), f32),
            pltpu.VMEM((2, 2, JOINTS, frames // 2, HALF), f32),
            pltpu.VMEM((3, GROUP, C_OUT), f32),
        ],
        "output_part",
    )

    grad_rows = Sharing.padded(TAPS * C_OUT + C_IN)
    conv_grad, short_grad, left_rim, right_rim, grads, back = call(
        weight_part,
        pairs,
        [
            (conv, out_block),
            (upstream, out_block),
            (xe, xe_block),
            (active, a_block),
            (masks, mask_block),
            (stats, None),
            (conv_stats, None),
            (back, None),
            (norm_params, None),
            (ws, None),
        ],
        [
            (full(out_block), bf16, out_block),
            (full(out_block), bf16, out_block),
            (full(rim_block), bf16, None),
            (full(rim_block), bf16, None),
            ((grad_rows, C_OUT), bf16, None),
            (small, f32, None),
        ],
        [
            pltpu.VMEM((C_OUT, 4 * ROWS), bf16),
            pltpu.VMEM((2, ROWS, HALF), f32),
            pltpu.VMEM((TAPS, C_OUT, C_OUT), f32),
            pltpu.VMEM((C_IN, C_OUT), f32),
        ]
        + [pltpu.VMEM(full(rim_block), bf16)] * 4
        + [dma((pairs,))] * 4
        + sum_scratch(),
        "weight_part",
        collective_id=3,
        has_side_effects=True,
    )

    def early(block):
        return spec(block, lambda i: (jnp.minimum(i, pairs - 1),) + (0,) * (len(block) - 1))

    def late(block):
        return spec(block, lambda i: (jnp.maximum(i - pairs, 0),) + (0,) * (len(block) - 1))

    def twice(block):
        return spec(block, lambda i: (lax.rem(i, pairs),) + (0,) * (len(block) - 1))

    graph_rows = Sharing.padded(SUBSETS * C_IN)
    hidden_grad, first_sums, grad_sums, graph_grad = call(
        conv_back,
        2 * pairs,
        [
            (conv_grad, early(out_block)),
            (left_rim, early(rim_block)),
            (right_rim, early(rim_block)),
            (taps, None),
            (hidden, twice(wide_block)),
            (masks, twice(mask_block)),
            (stats, None),
            (norm_params, None),
            (xg, late(xg_block)),
            (grads, None),
        ],
        [
            (full(wide_block), bf16, late(wide_block)),
            (small, f32, None),
            ((grad_rows, C_OUT), bf16, None),
            ((graph_rows, C_OUT), bf16, None),
        ],
        [
            pltpu.VMEM((2, 2, ROWS, HALF), f32),
            pltpu.VMEM((8, ROWS, C_OUT), bf16),
            pltpu.VMEM((2, GROUP, C_OUT), f32),
            pltpu.VMEM(full(wide_block), f32),
            pltpu.VMEM((SUBSETS * C_IN, C_OUT), f32),
        ]
        + sum_scratch()
        + Sharing.scratch(grad_rows),
        "conv_back",
        collective_id=4,
        has_side_effects=True,
    )

    input_grad, graph_sum, edge_sum = call(
        graph_back,
        pairs,
        [
            (hidden_grad, wide_block),
            (xq, xq_block),
            (short_grad, out_block),
            (wgt, None),
            (wst, None),
            (kront, None),
            (own, None),
            (graph_grad, None),
        ],
        [
            (natural.shape, bf16, x_block),
            ((graph_rows, C_OUT), bf16, None),
            ((32, 128), f32, None),
        ],
        [
            pltpu.VMEM((2, 2, C_OUT, C_OUT), bf16),
            pltpu.VMEM((2, JOINTS, frames, C_IN), f32),
            pltpu.VMEM((2 * C_OUT, C_OUT), f32),
            pltpu.VMEM((JOINTS, GROUP, 2 * C_IN), f32),
        ]
        + sum_scratch((32, 128))
        + Sharing.scratch(graph_rows),
        "graph_back",
        collective_id=5,
        has_side_effects=True,
    )

    tap_spec = spec((1, C_OUT, C_OUT), lambda i: (jnp.minimum(i, TAPS - 1), 0, 0))
    graph_spec = spec((C_IN, C_OUT), lambda i: (0, jnp.maximum(i - TAPS, 0)))
    states = [
        (graph_weight, graph_moment, graph_square, graph_average),
        (temporal_weight, temporal_moment, temporal_square, temporal_average),
        (shortcut_weight, shortcut_moment, shortcut_square, shortcut_average),
        (edge_weight, edge_moment, edge_square, edge_average),
        (norm_params, norm_moment, norm_square, norm_average),
    ]
    places = [graph_spec, tap_spec, None, None, None]
    state_ins = [(array, place) for group, place in zip(states, places) for array in group]
    clip_block = (1, JOINTS, frames, C_IN)
    clip_spec = spec(clip_block, lambda i: (jnp.minimum(i, clips - 1), 0, 0, 0))
    new = call(
        update,
        max(clips, TAPS + SUBSETS),
        [
            (grad_sums, None),
            (graph_sum, None),
            (edge_sum, None),
            (graph_mask, None),
            (stats, None),
            (conv_stats, None),
            (back, None),
            (first_sums, None),
            (input_grad, clip_spec),
        ]
        + state_ins,
        [(natural.shape, bf16, clip_spec), ((GROUP, 128), f32, None)]
        + [(array.shape, f32, place) for array, place in state_ins],
        [pltpu.VMEM((GROUP, 128), f32), pltpu.VMEM((6, C_OUT), f32)],
        "update",
    )
    return (
        jnp.transpose(outputs, (0, 2, 1, 3)),
        jnp.transpose(new[0], (0, 2, 1, 3)),
        new[1][0, 0:1],
        *new[2:],
    )


def solution(mesh):
    rows = P("batch", "tm", None, None)
    in_specs = (rows, rows, P("batch"), P("batch", "tm")) + (P(),) * 21
    out_specs = (rows, rows) + (P(),) * 21
    return jax.shard_map(shards, mesh=mesh, in_specs=in_specs, out_specs=out_specs, check_vma=False)
```

```python
import functools

import jax
import jax.numpy as jnp
from jax import lax
from jax.experimental import pallas as pl
from jax.experimental.pallas import tpu as pltpu
from jax.sharding import PartitionSpec as P

C_IN = 128
C_OUT = 256
JOINTS = 25
SUBSETS = 3
TAPS = 9
GROUP = 8
PHASES = 8
UNITS = 2 * JOINTS
ROWS = UNITS * GROUP
HALF_ROWS = JOINTS * GROUP
HALF = C_IN
CUT = 5
DEPTH = 4 * ROWS + 64

f32 = jnp.float32
bf16 = jnp.bfloat16

norm_epsilon = 1e-05
beta_first = 0.9
beta_second = 0.999
adam_epsilon = 1e-08
clip_limit = 1.0
average_decay = 0.9
rate_matrix = 0.05
rate_small = 0.3
decay_matrix = 0.01
steps_taken = 3.0


def params(**more):
    return pltpu.CompilerParams(
        vmem_limit_bytes=60 * 2**20, dimension_semantics=("arbitrary",), **more
    )


def adjacency(subsets):
    linked = (subsets > 0).astype(f32)
    degree = jnp.sum(linked, axis=0)
    labels = jnp.arange(SUBSETS, dtype=jnp.int32) + 1
    chosen = (subsets[None, :, :] == labels[:, None, None]).astype(f32)
    return chosen / degree[None, None, :]


def adam_update(weight, moment, square, average, gradient, factor, rate, decay):
    fix_first = 1.0 - beta_first**steps_taken
    fix_second = 1.0 - beta_second**steps_taken
    clipped = gradient * factor
    moment_new = beta_first * moment + (1.0 - beta_first) * clipped
    square_new = beta_second * square + (1.0 - beta_second) * clipped * clipped
    scaled = square_new * (1.0 / fix_second)
    below = scaled * lax.rsqrt(scaled) + adam_epsilon
    guess = pl.reciprocal(below, approx=True)
    guess = guess * (2.0 - below * guess)
    stepped = moment_new * (1.0 / fix_first) * guess
    weight_new = weight - rate * (stepped + decay * weight)
    average_new = average_decay * average + (1.0 - average_decay) * weight_new
    return (weight_new, moment_new, square_new, average_new)


def dot(a, b):
    return jnp.dot(a, b, preferred_element_type=f32)


def dot_nt(a, b):
    return lax.dot_general(a, b, (((1,), (1,)), ((), ())), preferred_element_type=f32)


def dot_tn(a, b):
    return lax.dot_general(a, b, (((0,), (0,)), ((), ())), preferred_element_type=f32)


def fold(values):
    return jnp.sum(values.reshape(-1, GROUP, values.shape[-1]), axis=0)


MESH = pl.DeviceIdType.MESH


def peers(axis):
    count = lax.axis_size(axis)
    here = lax.axis_index(axis)
    return [(d, {axis: lax.rem(here + d, count)}) for d in range(1, count)]


def greet():
    barrier = pltpu.get_barrier_semaphore()
    for axis in ("tm", "batch"):
        for _, device in peers(axis):
            pl.semaphore_signal(barrier, inc=1, device_id=device, device_id_type=MESH)


def await_greetings():
    count = lax.axis_size("tm") + lax.axis_size("batch") - 2
    pl.semaphore_wait(pltpu.get_barrier_semaphore(), count)


class Total:
    def __init__(self, buffers):
        self.levels = list(zip(("tm", "batch"), (buffers[0:3], buffers[3:6])))

    def copies(self, level):
        axis, (slots, sent, received) = self.levels[level]
        here = lax.axis_index(axis)
        return [
            remote(slots.at[here], slots.at[here], sent.at[d], received.at[d], device)
            for d, device in peers(axis)
        ]

    def start(self, level, values):
        axis, (slots, _, _) = self.levels[level]
        slots[lax.axis_index(axis)] = values
        for copy in self.copies(level):
            copy.start()

    def end(self, level):
        axis, (slots, _, _) = self.levels[level]
        for copy in self.copies(level):
            copy.wait()
        values = slots[0]
        for k in range(1, lax.axis_size(axis)):
            values = values + slots[k]
        return values


def sum_all(values, buffers):
    total = Total(buffers)
    total.start(0, values)
    total.start(1, total.end(0))
    return total.end(1)


def sum_scratch(shape=(8, C_OUT)):
    found = []
    for axis in ("tm", "batch"):
        count = lax.axis_size(axis)
        found += [
            pltpu.VMEM((count, *shape), f32),
            pltpu.SemaphoreType.DMA((count,)),
            pltpu.SemaphoreType.DMA((count,)),
        ]
    return found


def remote(source, target, sent, received, device):
    return pltpu.make_async_remote_copy(
        src_ref=source,
        dst_ref=target,
        send_sem=sent,
        recv_sem=received,
        device_id=device,
        device_id_type=MESH,
    )


def with_neighbours(step, low, high, from_left, from_right, sems, act):
    here = lax.axis_index("tm")
    last = lax.axis_size("tm") - 1
    sent_right, got_left, sent_left, got_right = sems

    def rightward():
        return remote(high, from_left, sent_right.at[step], got_left.at[step], {"tm": here + 1})

    def leftward():
        return remote(low, from_right, sent_left.at[step], got_right.at[step], {"tm": here - 1})

    if act == "start":

        @pl.when(here < last)
        def _():
            rightward().start()

        @pl.when(here > 0)
        def _():
            leftward().start()

    else:

        @pl.when(here < last)
        def _():
            rightward().wait_send()
            leftward().wait_recv()

        @pl.when(here > 0)
        def _():
            leftward().wait_send()
            rightward().wait_recv()


def first_moments(stats, norm):
    count_in = stats[4:5]
    mean = stats[0:1] / count_in
    rstd = lax.rsqrt(stats[1:2] / count_in - mean * mean + norm_epsilon)
    return mean, rstd, norm[0:1] * rstd, norm[1:2] - norm[0:1] * rstd * mean


def one_hot_rows(rows, columns):
    row = lax.broadcasted_iota(jnp.int32, (rows, columns), 0)
    col = lax.broadcasted_iota(jnp.int32, (rows, columns), 1)
    return (row // GROUP == col).astype(bf16)


def prepare(
    length_ref, frame_ref, subset_ref, edge_ref, graph_ref, short_ref, taps_ref,
    m_ref, em_ref, kron_ref, kront_ref, own_ref, gm_ref, wg_ref, wgt_ref, ws_ref, wst_ref, low_ref,
):
    clips, frames = frame_ref.shape
    first = lax.axis_index("tm") * frames
    row = lax.broadcasted_iota(jnp.int32, (clips, frames), 0)
    ids = lax.broadcasted_iota(jnp.int32, (clips, frames), 1) + first
    ends = jnp.zeros((clips, frames), jnp.int32)
    for clip in range(clips):
        ends = jnp.where(row == clip, length_ref[clip], ends)
    mask = ((ids < ends) & (frame_ref[...] > 0)).astype(bf16)
    every = jnp.ones((frames, 128), bf16)

    def spread(rows, clip_of, frame_of):
        at = lax.broadcasted_iota(jnp.int32, (rows, clips), 0)
        chosen = (clip_of(at) == lax.broadcasted_iota(jnp.int32, (rows, clips), 1)).astype(bf16)
        lines = dot(chosen, mask)
        at = lax.broadcasted_iota(jnp.int32, (rows, frames), 0)
        kept = frame_of(at) == lax.broadcasted_iota(jnp.int32, (rows, frames), 1)
        return dot(jnp.where(kept, lines, 0.0).astype(bf16), every)

    side = 2 * GROUP
    m_ref[...] = spread(
        clips * frames,
        lambda at: 2 * (at // (PHASES * side)) + at // GROUP % 2,
        lambda at: PHASES * (at % GROUP) + at // side % PHASES,
    )
    em_ref[...] = spread(
        clips * GROUP, lambda at: at // GROUP, lambda at: (at % GROUP + frames - 4) % frames
    )
    subsets = subset_ref[...]
    degree = jnp.sum((subsets > 0).astype(f32), axis=0, keepdims=True)
    lift = one_hot_rows(HALF_ROWS, JOINTS)
    row = lax.broadcasted_iota(jnp.int32, (JOINTS, C_OUT), 0)
    drop = (row == lax.broadcasted_iota(jnp.int32, (JOINTS, C_OUT), 1) // GROUP).astype(bf16)
    row = lax.broadcasted_iota(jnp.int32, (HALF_ROWS, C_OUT), 0)
    same = row % GROUP == lax.broadcasted_iota(jnp.int32, (HALF_ROWS, C_OUT), 1) % GROUP
    for k in range(SUBSETS):
        share = (subsets == k + 1).astype(f32) / degree
        gm_ref[k] = share
        low = (share * edge_ref[k]).astype(bf16)
        if k == 0:
            row = lax.broadcasted_iota(jnp.int32, (JOINTS, JOINTS), 0)
            col = lax.broadcasted_iota(jnp.int32, (JOINTS, JOINTS), 1)
            diagonal = jnp.sum(jnp.where(row == col, low.astype(f32), 0.0), axis=1, keepdims=True)
            wide = jnp.broadcast_to(diagonal, (JOINTS, C_IN)).astype(bf16)
            own_ref[...] = dot(lift, wide).reshape(JOINTS, GROUP, C_IN)
        else:
            ahead = dot(lift, dot_tn(low, drop).astype(bf16))
            rows = slice((k - 1) * HALF_ROWS, k * HALF_ROWS)
            kron_ref[rows, :] = jnp.where(same, ahead, 0.0).astype(bf16)
            behind = dot(lift, dot(low, drop).astype(bf16))
            lanes = slice((k - 1) * C_OUT, k * C_OUT)
            kront_ref[:, lanes] = jnp.where(same, behind, 0.0).astype(bf16)
        block = graph_ref[:, k * C_OUT : (k + 1) * C_OUT]
        wg_ref[k * C_IN : (k + 1) * C_IN, :] = block.astype(bf16)
        wgt_ref[:, k * C_IN : (k + 1) * C_IN] = block.T.astype(bf16)
    ws_ref[...] = short_ref[...].astype(bf16)
    wst_ref[...] = short_ref[...].T.astype(bf16)
    low_ref[...] = taps_ref[...].astype(bf16)


def mix_rows(parts, scales, kron_ref, wide_ref):
    mixed = dot(kron_ref[...], wide_ref[...])
    sides = []
    for side in range(2):
        lanes = slice(side * HALF, (side + 1) * HALF)
        sides.append(
            jnp.concatenate(
                [
                    parts[side] * scales,
                    mixed[0:HALF_ROWS, lanes].reshape(JOINTS, GROUP, C_IN),
                    mixed[HALF_ROWS : 2 * HALF_ROWS, lanes].reshape(JOINTS, GROUP, C_IN),
                ],
                axis=2,
            )
        )
    return jnp.concatenate(sides, axis=1).reshape(ROWS, SUBSETS * C_IN).astype(bf16)


def put_wide(parts, wide_ref):
    wide = jnp.concatenate([part.reshape(HALF_ROWS, C_IN) for part in parts], axis=1)
    wide_ref[0:HALF_ROWS, :] = wide.astype(bf16)


def graph_forward(
    x_ref, head_ref, tail_ref, m_ref, em_ref, kron_ref, own_ref, wg_ref, ws_ref,
    xq_ref, xe_ref, h_ref, st_ref, rim_ref, rim_mask_ref,
    xs, xg, xe, sums, counts, mine, lefts, rights, mask_lefts, mask_rights,
    sent_right, got_left, sent_left, got_right, *sum_buffers,
):
    step = pl.program_id(0)
    last = pl.num_programs(0) - 1
    sems = (sent_right, got_left, sent_left, got_right)

    def rims(act):
        with_neighbours(0, mine, mine, lefts, rights, sems, act)
        with_neighbours(1, em_ref, em_ref, mask_lefts, mask_rights, sems, act)

    @pl.when(step == 0)
    def _():
        for ref in (lefts, rights, mask_lefts, mask_rights):
            ref[...] = jnp.zeros_like(ref)
        greet()
        for pair in range(mine.shape[0]):
            ends = []
            for clip in (2 * pair, 2 * pair + 1):
                above = pltpu.roll(tail_ref[clip].astype(f32)[:, GROUP:], 4, 1)
                below = pltpu.roll(head_ref[clip].astype(f32)[:, :GROUP], 4, 1)
                sub = lax.broadcasted_iota(jnp.int32, above.shape, 1)
                ends.append(jnp.where(sub < 4, above, below))
            mine[pair] = jnp.concatenate(ends, axis=1).astype(bf16)
        sums[...] = jnp.zeros_like(sums)
        counts[...] = jnp.zeros_like(counts)

    def permute():
        for side in range(2):
            for start in range(0, JOINTS, CUT):
                rows = x_ref[side, start : start + CUT].astype(f32)
                rows = jnp.swapaxes(rows.reshape(CUT, GROUP, PHASES, C_IN), 1, 2)
                for c in range(PHASES):
                    mask = m_ref[0, c, side * GROUP : (side + 1) * GROUP]
                    xs[c, side, start : start + CUT] = rows[:, c] * mask[None]

    def mix(c):
        xq_ref[0, c, HALF_ROWS:, :] = jnp.zeros((C_OUT - HALF_ROWS, C_OUT), bf16)
        parts = [xs[c, 0], xs[c, 1]]
        put_wide(parts, xq_ref.at[0, c])
        xg[c] = mix_rows(parts, own_ref[...], kron_ref, xq_ref.at[0, c])
        counts[0] += m_ref[0, c]
        if c % 2 == 0:
            counts[1] += m_ref[0, c]
            even = jnp.concatenate(parts, axis=1).reshape(ROWS, C_IN).astype(bf16)
            xe_ref[0, c // 2] = even
            xe[c // 2] = even

    def project(c):
        hidden = dot(xg[c : c + 2].reshape(2 * ROWS, SUBSETS * C_IN), wg_ref[...])
        h_ref[0, c : c + 2] = hidden.reshape(2, ROWS, C_OUT).astype(bf16)
        sums[0] += fold(hidden)
        sums[1] += fold(hidden * hidden)
        short = dot(xe[c // 2], ws_ref[...])
        sums[2] += fold(short)
        sums[3] += fold(short * short)

    @pl.when(step == 0)
    def _():
        permute()
        for c in range(PHASES):
            mix(c)

    @pl.when((step > 0) & (step < last))
    def _():
        permute()
        for c in range(0, PHASES, 2):
            project(c)
            mix(c)
            mix(c + 1)

    @pl.when(step == last)
    def _():
        for c in range(0, PHASES, 2):
            project(c)

    @pl.when(step == 1)
    def _():
        await_greetings()
        rims("start")

    @pl.when(step == last)
    def _():
        rows = [jnp.sum(sums[k], axis=0, keepdims=True) for k in range(4)]
        for k in range(2):
            total = JOINTS * jnp.sum(counts[k], axis=0, keepdims=True)
            rows.append(jnp.concatenate([total, total], axis=1))
        rows.append(jnp.zeros((2, C_OUT), f32))
        st_ref[...] = sum_all(jnp.concatenate(rows, axis=0), sum_buffers)
        rims("wait")
        sub = lax.broadcasted_iota(jnp.int32, mask_lefts.shape, 0) % GROUP
        rim_mask_ref[...] = jnp.where(sub < 4, mask_lefts[...], mask_rights[...])
        for pair in range(lefts.shape[0]):
            sub = lax.broadcasted_iota(jnp.int32, lefts.shape[1:], 1) % GROUP
            both = jnp.where(sub < 4, lefts[pair].astype(f32), rights[pair].astype(f32))
            rim_ref[pair] = both.astype(bf16)


def insert_and_roll(tiles, fill, side):
    sub = lax.broadcasted_iota(jnp.int32, tiles.shape, 1)
    joined = jnp.where(sub == side, fill, tiles)
    return pltpu.roll(joined, 1 if side == 7 else GROUP - 1, 1)


def conv_forward(
    h_ref, xh_ref, m_ref, mh_ref, st_ref, norm_ref, kron_ref, own_ref, wg_ref, taps_ref,
    a_ref, conv_ref, out_ref,
    pad, rims, fills, sums, *sum_buffers,
):
    step = pl.program_id(0)

    @pl.when(step == 0)
    def _():
        greet()
        sums[...] = jnp.zeros_like(sums)
        pad[...] = jnp.zeros_like(pad)

    _, _, scale, shift = first_moments(st_ref[...], norm_ref[...])
    scale, shift = 0.5 * scale, 0.5 * shift

    def activate(values, mask):
        half = values * scale + shift
        return (half + half * jnp.tanh(half)).reshape(-1, 2 * GROUP, C_OUT) * mask

    def wide(mask):
        return jnp.concatenate([mask, mask], axis=1)[None]

    rim_mask = mh_ref[...]
    rim_rows = xh_ref[0].astype(f32) * rim_mask[None]
    parts = [rim_rows[:, side * GROUP : (side + 1) * GROUP] for side in range(2)]
    put_wide(parts, pad)
    rim_hidden = dot(mix_rows(parts, own_ref[...], kron_ref, pad), wg_ref[...])
    rim_active = activate(rim_hidden, wide(rim_mask)).reshape(ROWS, C_OUT)
    for lane in range(2):
        rims[lane] = rim_active[:, lane * HALF : (lane + 1) * HALF]
    for p in range(2):
        for q in range(2):
            for lane in range(2):
                fills[2 * p + q, lane, pl.ds(7, UNITS, stride=GROUP), :] = rims[
                    lane, pl.ds(2 * q + p, UNITS, stride=GROUP), :
                ]
                fills[2 * p + q, lane, pl.ds(0, UNITS, stride=GROUP), :] = rims[
                    lane, pl.ds(4 + 2 * q + p, UNITS, stride=GROUP), :
                ]

    a_ref[0, 1, 7, 0:64, :] = jnp.zeros((64, C_OUT), bf16)
    for c in range(PHASES):
        p, q = c % 2, c // 2
        mask = wide(m_ref[0, c])
        for start in range(0, JOINTS, CUT):
            rows = slice(start * 2 * GROUP, (start + CUT) * 2 * GROUP)
            active = activate(h_ref[0, c, rows, :].astype(f32), mask)
            a_ref[0, p, q + 2, rows, :] = active.reshape(-1, C_OUT).astype(bf16)
            if p == 1 and q == 1:
                continue
            tiles = active.reshape(-1, GROUP, C_OUT)
            fill = jnp.concatenate(
                [fills[2 * p + q % 2, lane, rows, :] for lane in range(2)], axis=1
            ).reshape(-1, GROUP, C_OUT)
            moved = insert_and_roll(tiles, fill, 7 if q >= 2 else 0)
            at = q - 2 if q >= 2 else q + 6
            a_ref[0, p, at, rows, :] = moved.reshape(-1, C_OUT).astype(bf16)

    total = None
    for j in range(TAPS):
        window = a_ref[0, j % 2, j // 2 : j // 2 + 4].reshape(4 * ROWS, C_OUT)
        part = dot(window, taps_ref[j])
        total = part if total is None else total + part
    conv_ref[0] = total.reshape(4, ROWS, C_OUT)
    for q in range(4):
        block = total[q * ROWS : (q + 1) * ROWS].reshape(JOINTS, 2 * GROUP, C_OUT)
        live = block * wide(m_ref[0, 2 * q])
        sums[0] += fold(live)
        sums[1] += fold(live * block)

    @pl.when(step == pl.num_programs(0) - 1)
    def _():
        await_greetings()
        rows = [jnp.sum(sums[k], axis=0, keepdims=True) for k in range(2)]
        rows.append(jnp.zeros((6, C_OUT), f32))
        out_ref[...] = sum_all(jnp.concatenate(rows, axis=0), sum_buffers)


def second_moments(stats, conv_stats):
    count_out = stats[5:6]
    mean_conv = conv_stats[0:1] / count_out
    rstd_conv = lax.rsqrt(conv_stats[1:2] / count_out - mean_conv * mean_conv + norm_epsilon)
    mean_short = stats[2:3] / count_out
    rstd_short = lax.rsqrt(stats[3:4] / count_out - mean_short * mean_short + norm_epsilon)
    return mean_conv, rstd_conv, mean_short, rstd_short


def back_totals(back, moments):
    mean_conv, rstd_conv, mean_short, rstd_short = moments
    back_sum = back[0:1]
    back_conv = rstd_conv * (back[1:2] - mean_conv * back_sum)
    back_short = rstd_short * (back[2:3] - mean_short * back_sum)
    return back_sum, back_conv, back_short


def middle(
    conv_ref, xe_ref, cot_ref, a_ref, m_ref, st_ref, cs_ref, norm_ref, ws_ref,
    o_ref, cg_ref, sg_ref, left_ref, right_ref, grad_ref, total_ref,
    cots, outs, sums, conv_kept, up_kept, turned, edges, tg, shg, low_rims, high_rims, lefts, rights,
    sent_right, got_left, sent_left, got_right, *sum_buffers,
):
    step = pl.program_id(0)
    pairs = low_rims.shape[0]
    sems = (sent_right, got_left, sent_left, got_right)

    def rims(at, act):
        with_neighbours(
            at, low_rims.at[at], high_rims.at[at], lefts.at[at], rights.at[at], sems, act
        )

    norm = norm_ref[...]
    stats = st_ref[...]
    moments = second_moments(stats, cs_ref[...])
    mean_conv, rstd_conv, mean_short, rstd_short = moments

    @pl.when(step == 0)
    def _():
        for ref in (sums, lefts, rights, tg, shg, turned, low_rims, high_rims):
            ref[...] = jnp.zeros_like(ref)
        greet()

    @pl.when(step < pairs)
    def _():
        scale_conv = 0.5 * norm[2:3] * rstd_conv
        scale_short = 0.5 * norm[4:5] * rstd_short
        shift = 0.5 * (norm[3:4] + norm[5:6]) - scale_conv * mean_conv - scale_short * mean_short
        for side in range(2):
            for joint in range(JOINTS):
                for lane in range(2):
                    cots[side, lane, joint] = cot_ref[
                        side, joint, :, lane * HALF : (lane + 1) * HALF
                    ].astype(f32)
        for q in range(4):
            mask = m_ref[0, 2 * q]
            mask = jnp.concatenate([mask, mask], axis=1)[None]
            short_all = dot(xe_ref[0, q], ws_ref[...])
            for start in range(0, JOINTS, CUT):
                rows = slice(start * 2 * GROUP, (start + CUT) * 2 * GROUP)
                conv = conv_ref[0, q, rows, :]
                conv_kept[step, q, rows, :] = conv
                short = short_all[rows]
                half = conv * scale_conv + short * scale_short + shift
                turn = jnp.tanh(half)
                grow = (0.5 + 0.5 * turn).reshape(CUT, 2 * GROUP, C_OUT) * mask
                half = half.reshape(CUT, 2 * GROUP, C_OUT)
                turn = turn.reshape(CUT, 2 * GROUP, C_OUT)
                result = (half + half) * grow
                slope = grow + grow * (half - half * turn)
                cot = jnp.concatenate(
                    [
                        jnp.concatenate(
                            [
                                cots[side, lane, start : start + CUT, pl.ds(q, GROUP, stride=4), :]
                                for lane in range(2)
                            ],
                            axis=2,
                        )
                        for side in range(2)
                    ],
                    axis=1,
                )
                for side in range(2):
                    for lane in range(2):
                        outs[
                            side, lane, start : start + CUT, pl.ds(q, GROUP, stride=4), :
                        ] = result[
                            :, side * GROUP : (side + 1) * GROUP, lane * HALF : (lane + 1) * HALF
                        ]
                up = (cot * slope).reshape(-1, C_OUT)
                up_kept[step, q, rows, :] = up
                sums[0] += fold(up)
                sums[1] += fold(up * conv)
                sums[2] += fold(up * short)
        for side in range(2):
            for joint in range(JOINTS):
                for lane in range(2):
                    o_ref[side, joint, :, lane * HALF : (lane + 1) * HALF] = outs[
                        side, lane, joint
                    ].astype(bf16)

    @pl.when(step == pairs - 1)
    def _():
        rows = [jnp.sum(sums[k], axis=0, keepdims=True) for k in range(3)]
        rows.append(jnp.zeros((5, C_OUT), f32))
        await_greetings()
        total_ref[...] = sum_all(jnp.concatenate(rows, axis=0), sum_buffers)

    def gradients(pair, q):
        back_sum, back_conv, back_short = back_totals(total_ref[...], moments)
        count_out = stats[5:6]

        def terms(gain, mean, rstd, back):
            lead = gain * rstd
            slope = lead * rstd * back / count_out
            return lead, slope, lead * back_sum / count_out - slope * mean

        lead_c, slope_c, shift_c = terms(norm[2:3], mean_conv, rstd_conv, back_conv)
        lead_s, slope_s, shift_s = terms(norm[4:5], mean_short, rstd_short, back_short)
        mask = m_ref[0, 2 * q]
        mask = jnp.concatenate([mask, mask], axis=1)[None]
        short_all = dot(xe_ref[0, q], ws_ref[...])
        for start in range(0, JOINTS, CUT):
            rows = slice(start * 2 * GROUP, (start + CUT) * 2 * GROUP)
            up = up_kept[pair, q, rows, :]

            def masked(values):
                return (values.reshape(CUT, 2 * GROUP, C_OUT) * mask).reshape(-1, C_OUT)

            cg = up * lead_c - masked(conv_kept[pair, q, rows, :] * slope_c + shift_c)
            cg_ref[0, q, rows, :] = cg.astype(bf16)
            for lane in range(2):
                edges[lane, rows, :] = cg[:, lane * HALF : (lane + 1) * HALF]
            sg = up * lead_s - masked(short_all[rows] * slope_s + shift_s)
            sg_ref[0, q, rows, :] = sg.astype(bf16)
        for lane in range(2):
            at = slice(lane * HALF, (lane + 1) * HALF)
            target = low_rims if q < 2 else high_rims
            outer = edges[lane, pl.ds(0 if q < 2 else 7, UNITS, stride=GROUP), :]
            target[pair, q % 2, 0:UNITS, at] = outer.astype(bf16)

    def turn_over():
        turned[:, 0 : 4 * ROWS] = cg_ref[0].reshape(4 * ROWS, C_OUT).T
        shg[...] += dot_tn(
            xe_ref[0].reshape(4 * ROWS, C_IN), sg_ref[0].reshape(4 * ROWS, C_OUT)
        )

    def taps_of(first, end):
        every = a_ref[0].reshape(16 * ROWS, C_OUT)
        for j in range(first, end):
            at = (8 * (j % 2) + j // 2) * ROWS
            tg[j] += dot(turned[...], every[at : at + DEPTH])

    @pl.when(step == pairs)
    def _():
        for q in range(4):
            gradients(0, q)
        turn_over()

    @pl.when((step > pairs) & (step < 2 * pairs))
    def _():
        for q in range(4):
            taps_of(2 * q, 2 * q + 2)
            gradients(step - pairs, q)
        taps_of(8, 9)
        turn_over()

    @pl.when((step >= pairs) & (step < 2 * pairs))
    def _():
        rims(step - pairs, "start")

    @pl.when(step == 2 * pairs)
    def _():
        taps_of(0, 9)
        for j in range(TAPS):
            grad_ref[j * C_OUT : (j + 1) * C_OUT, :] = tg[j].astype(bf16)
        grad_ref[TAPS * C_OUT : TAPS * C_OUT + C_IN, :] = shg[...].astype(bf16)
        rest = grad_ref.shape[0] - TAPS * C_OUT - C_IN
        if rest:
            grad_ref[TAPS * C_OUT + C_IN :, :] = jnp.zeros((rest, C_OUT), bf16)
        for pair in range(pairs):
            rims(pair, "wait")
        left_ref[...] = lefts[...]
        right_ref[...] = rights[...]


def padded(rows):
    unit = 16 * lax.axis_size("tm") * lax.axis_size("batch")
    return (rows + unit - 1) // unit * unit


class Places:
    def __init__(self, rows):
        tm = lax.axis_index("tm")
        self.core = tm % 2
        self.line = tm // 2
        self.lines = lax.axis_size("tm") // 2
        self.batch = lax.axis_index("batch")
        self.batches = lax.axis_size("batch")
        self.half = rows // 2
        self.part = self.half // self.lines
        self.piece = self.part // self.batches

    def core_peer(self):
        return {"tm": 2 * self.line + 1 - self.core}

    def line_peers(self):
        for d in range(1, self.lines):
            to = lax.rem(self.line + d, self.lines)
            yield d, to, {"tm": 2 * to + self.core}

    def batch_peers(self):
        for d in range(1, self.batches):
            to = lax.rem(self.batch + d, self.batches)
            yield d, to, {"batch": to}

    def rows(self, index, count):
        return pl.ds(pl.multiple_of(index * count, 16), count)


def three_levels(rows):
    lines, batches = lax.axis_size("tm") // 2, lax.axis_size("batch")
    half = rows // 2
    return lines, batches, half, half // lines, half // lines // batches


class Scatter(Places):
    def __init__(self, source, refs):
        super().__init__(source.shape[0])
        self.source = source
        self.here, self.up, self.out, self.firsts, self.seconds, self.thirds = refs[0:6]
        self.sems = refs[6:12]

    @staticmethod
    def scratch(rows):
        lines, batches, half, part, piece = three_levels(rows)
        shapes = ((half,), (part,), (piece,), (half,), (lines, part), (batches, piece))
        found = [pltpu.VMEM((*shape, C_OUT), bf16) for shape in shapes]
        for count in (1, lines, batches):
            found += [pltpu.SemaphoreType.DMA((count,))] * 2
        return found

    def copies(self, level):
        sent, got = self.sems[2 * level], self.sems[2 * level + 1]
        if level == 0:
            source = self.source.at[self.rows(1 - self.core, self.half)]
            return [remote(source, self.firsts, sent.at[0], got.at[0], self.core_peer())]
        if level == 1:
            return [
                remote(
                    self.here.at[self.rows(to, self.part)], self.seconds.at[self.line],
                    sent.at[d], got.at[d], device,
                )
                for d, to, device in self.line_peers()
            ]
        return [
            remote(
                self.up.at[self.rows(to, self.piece)], self.thirds.at[self.batch],
                sent.at[d], got.at[d], device,
            )
            for d, to, device in self.batch_peers()
        ]

    def start(self, level):
        for copy in self.copies(level):
            copy.start()

    def end(self, level):
        for copy in self.copies(level):
            copy.wait()
        if level == 0:
            own = self.source[self.rows(self.core, self.half), :].astype(f32)
            self.here[...] = (own + self.firsts[...].astype(f32)).astype(bf16)
        if level == 1:
            own = self.here[self.rows(self.line, self.part), :].astype(f32)
            for d in range(1, self.lines):
                own = own + self.seconds[lax.rem(self.line + d, self.lines)].astype(f32)
            self.up[...] = own.astype(bf16)
        if level == 2:
            own = self.up[self.rows(self.batch, self.piece), :].astype(f32)
            for d in range(1, self.batches):
                own = own + self.thirds[lax.rem(self.batch + d, self.batches)].astype(f32)
            self.out[...] = own.astype(bf16)


class Gather(Places):
    def __init__(self, rows, refs):
        super().__init__(rows)
        self.gathered, self.joined, self.full = refs[0:3]
        self.sems = refs[3:9]

    @staticmethod
    def scratch(rows):
        lines, batches, half, part, piece = three_levels(rows)
        shapes = ((batches, piece), (lines, part), (2, half))
        found = [pltpu.VMEM((*shape, C_OUT), bf16) for shape in shapes]
        for count in (batches, lines, 1):
            found += [pltpu.SemaphoreType.DMA((count,))] * 2
        return found

    def copies(self, level):
        sent, got = self.sems[2 * level], self.sems[2 * level + 1]
        if level == 0:
            slot = self.gathered.at[self.batch]
            peers_here = self.batch_peers()
        elif level == 1:
            slot = self.joined.at[self.line]
            peers_here = self.line_peers()
        else:
            slot = self.full.at[self.core]
            return [remote(slot, slot, sent.at[0], got.at[0], self.core_peer())]
        return [remote(slot, slot, sent.at[d], got.at[d], device) for d, _, device in peers_here]

    def start(self, level, share=None):
        if level == 0:
            self.gathered[self.batch] = share
        if level == 1:
            self.joined[self.line] = self.gathered[...].reshape(self.part, C_OUT)
        if level == 2:
            self.full[self.core] = self.joined[...].reshape(self.half, C_OUT)
        for copy in self.copies(level):
            copy.start()

    def end(self, level):
        for copy in self.copies(level):
            copy.wait()


def conv_back(
    cg_ref, left_ref, right_ref, taps_ref, h_ref, m_ref, st_ref, norm_ref, xq_ref, kron_ref, own_ref,
    grad_ref,
    hg_ref, out_ref, sum_ref, gg_ref,
    fills, ext, sums, fg, kept, raw, xg, gg, *buffers,
):
    step = pl.program_id(0)
    pairs = pl.num_programs(0) // 2
    scatter = Scatter(grad_ref, buffers[6:])
    stats = st_ref[...]
    norm = norm_ref[...]
    mean, rstd, scale, shift = first_moments(stats, norm)

    @pl.when(step == 0)
    def _():
        greet()
        sums[...] = jnp.zeros_like(sums)
        gg[...] = jnp.zeros_like(gg)

    half_scale, half_shift = 0.5 * scale, 0.5 * shift

    def extend():
        kept[step] = h_ref[0]
        for q in range(2):
            for lane in range(2):
                at = slice(lane * HALF, (lane + 1) * HALF)
                fills[q, lane, pl.ds(7, UNITS, stride=GROUP), :] = left_ref[
                    0, q, 0:UNITS, at
                ].astype(f32)
                fills[q, lane, pl.ds(0, UNITS, stride=GROUP), :] = right_ref[
                    0, q, 0:UNITS, at
                ].astype(f32)
        for q in range(4):
            ext[q + 2] = cg_ref[0, q]
            for start in range(0, JOINTS, CUT):
                rows = slice(start * 2 * GROUP, (start + CUT) * 2 * GROUP)
                tiles = cg_ref[0, q, rows, :].astype(f32).reshape(-1, GROUP, C_OUT)
                fill = jnp.concatenate([fills[q % 2, lane, rows, :] for lane in range(2)], axis=1)
                fill = fill.reshape(-1, GROUP, C_OUT)
                moved = insert_and_roll(tiles, fill, 7 if q >= 2 else 0)
                at = q - 2 if q >= 2 else q + 6
                ext[at, rows, :] = moved.reshape(-1, C_OUT).astype(bf16)

    def convolve(c):
        p, q = c % 2, c // 2
        total = None
        for i in range(5 - p):
            part = dot_nt(ext[4 - i + q], taps_ref[2 * i + p])
            total = part if total is None else total + part
        raw[c] = total

    def activate_back(c):
        mask = 0.5 * m_ref[0, c]
        mask = jnp.concatenate([mask, mask], axis=1)[None]
        for start in range(0, JOINTS, CUT):
            rows = slice(start * 2 * GROUP, (start + CUT) * 2 * GROUP)
            hidden = kept[step - 1, c, rows, :].astype(f32)
            half = hidden * half_scale + half_shift
            turn = jnp.tanh(half)
            slope = (1.0 + turn) * (1.0 + (half - half * turn))
            slope = (slope.reshape(CUT, 2 * GROUP, C_OUT) * mask).reshape(-1, C_OUT)
            grad = raw[c, rows, :] * slope
            fg[step - 1, c, rows, :] = grad
            sums[0] += fold(grad)
            sums[1] += fold(grad * hidden)

    order = (0, 2, 4, 6, 1, 3, 5, 7)

    @pl.when(step == 0)
    def _():
        extend()
        for c in order:
            convolve(c)

    @pl.when((step > 0) & (step < pairs))
    def _():
        extend()
        for c in order:
            activate_back(c)
            convolve(c)

    @pl.when(step == pairs)
    def _():
        for c in order:
            activate_back(c)

    @pl.when(step > pairs)
    def _():
        pair = step - pairs - 1
        count_in = stats[4:5]
        back_sum = out_ref[0:1]
        back_norm = rstd * (out_ref[1:2] - mean * back_sum)
        lead = norm[0:1] * rstd
        slope = lead * rstd * back_norm / count_in
        offset = lead * back_sum / count_in - slope * mean
        for c in range(PHASES):
            mask = m_ref[0, c]
            mask = jnp.concatenate([mask, mask], axis=1)[None]
            for start in range(0, JOINTS, CUT):
                rows = slice(start * 2 * GROUP, (start + CUT) * 2 * GROUP)
                hidden = kept[pair, c, rows, :].astype(f32)
                taken = (hidden * slope + offset).reshape(CUT, 2 * GROUP, C_OUT) * mask
                taken = taken.reshape(-1, C_OUT)
                hg_ref[0, c, rows, :] = (fg[pair, c, rows, :] * lead - taken).astype(bf16)
            seen = xq_ref[0, c, 0:HALF_ROWS, :].astype(f32).reshape(JOINTS, GROUP, 2 * C_IN)
            parts = [seen[:, :, side * C_IN : (side + 1) * C_IN] for side in range(2)]
            xg[c] = mix_rows(parts, own_ref[...], kron_ref, xq_ref.at[0, c])
        gg[...] += dot_tn(
            xg[...].reshape(PHASES * ROWS, SUBSETS * C_IN),
            hg_ref[0].reshape(PHASES * ROWS, C_OUT),
        )

    @pl.when(step == 0)
    def _():
        await_greetings()
        scatter.start(0)

    for level, at in ((0, 1), (1, pairs - 2)):

        @pl.when(step == at)
        def _(level=level):
            scatter.end(level)
            scatter.start(level + 1)

    @pl.when(step == pairs)
    def _():
        rows = [jnp.sum(sums[k], axis=0, keepdims=True) for k in range(2)]
        rows.append(jnp.zeros((6, C_OUT), f32))
        out_ref[...] = sum_all(jnp.concatenate(rows, axis=0), buffers[0:6])

    @pl.when(step == 2 * pairs)
    def _():
        gg_ref[0 : SUBSETS * C_IN, :] = gg[...].astype(bf16)
        rest = gg_ref.shape[0] - SUBSETS * C_IN
        if rest:
            gg_ref[SUBSETS * C_IN :, :] = jnp.zeros((rest, C_OUT), bf16)
        scatter.end(2)
        sum_ref[...] = scatter.out[...]


def graph_back(
    hg_ref, xq_ref, sg_ref, wgt_ref, wst_ref, kront_ref, own_ref, piece_ref, grad_ref,
    ig_ref, taps_sum_ref, sum_ref, edge_ref,
    spread, staged, eg, own_grad, *buffers,
):
    step = pl.program_id(0)
    pairs = pl.num_programs(0) // 2
    total = Total(buffers[0:6])
    gather_taps = Gather(taps_sum_ref.shape[0], buffers[6:15])
    scatter = Scatter(grad_ref, buffers[15:27])
    gather = Gather(grad_ref.shape[0], buffers[27:36])

    @pl.when(step == 0)
    def _():
        greet()
        eg[...] = jnp.zeros_like(eg)
        own_grad[...] = jnp.zeros_like(own_grad)

    def side_by_side(values):
        return jnp.concatenate([values[:, 0:GROUP], values[:, GROUP : 2 * GROUP]], axis=2)

    @pl.when(step < pairs)
    def _():
        rest = jnp.zeros((C_OUT - HALF_ROWS, C_OUT), f32)
        found = None
        owned = None
        for c in range(PHASES):
            if c % 2 == 0:
                pair_back = dot(hg_ref[0, c : c + 2].reshape(2 * ROWS, C_OUT), wgt_ref[...])
                pair_back = pair_back.reshape(2, JOINTS, 2 * GROUP, SUBSETS * C_IN)
            back = pair_back[c % 2]
            for k in range(SUBSETS):
                both = side_by_side(back[:, :, k * C_IN : (k + 1) * C_IN])
                if k == 0:
                    seen = xq_ref[0, c, 0:HALF_ROWS, :].astype(f32)
                    part = seen.reshape(JOINTS, GROUP, 2 * C_IN) * both
                    owned = part if owned is None else owned + part
                both = jnp.concatenate([both.reshape(HALF_ROWS, 2 * C_IN), rest], axis=0)
                spread[step, c, k] = both.astype(bf16)
        for c in range(PHASES):
            both = spread[step, c, 1:3].reshape(2 * C_OUT, C_OUT)
            part = dot_nt(both, xq_ref[0, c])
            found = part if found is None else found + part
        eg[...] += found
        own_grad[...] += owned

    @pl.when(step >= pairs)
    def _():
        pair = step - pairs
        own = own_ref[...]
        own = jnp.concatenate([own, own], axis=2)
        short = dot(sg_ref[0].reshape(4 * ROWS, C_OUT), wst_ref[...])
        short = short.reshape(4, JOINTS, 2 * GROUP, C_IN)
        for c in range(PHASES):
            mixed = dot(kront_ref[...], spread[pair, c, 1:3].reshape(2 * C_OUT, C_OUT))
            direct = spread[pair, c, 0, 0:HALF_ROWS, :].astype(f32)
            result = mixed.reshape(JOINTS, GROUP, 2 * C_IN)
            result = result + direct.reshape(JOINTS, GROUP, 2 * C_IN) * own
            if c % 2 == 0:
                result = result + side_by_side(short[c // 2])
            staged[c] = result
        for side in range(2):
            lanes = slice(side * C_IN, (side + 1) * C_IN)
            for start in range(0, JOINTS, CUT):
                rows = [staged[c, start : start + CUT, :, lanes] for c in range(PHASES)]
                rows = jnp.swapaxes(jnp.stack(rows, axis=1), 1, 2)
                rows = rows.reshape(CUT, GROUP * PHASES, C_IN)
                ig_ref[side, start : start + CUT] = rows.astype(bf16)

    @pl.when(step == 0)
    def _():
        await_greetings()
        scatter.start(0)
        gather_taps.start(0, piece_ref[...])

    for level, at in ((0, 1), (1, 2)):

        @pl.when(step == at)
        def _(level=level):
            scatter.end(level)
            scatter.start(level + 1)

    @pl.when(step == 4)
    def _():
        scatter.end(2)
        gather.start(0, scatter.out[...])
        gather_taps.end(0)
        gather_taps.start(1)

    @pl.when(step == pairs - 1)
    def _():
        lines = lax.broadcasted_iota(jnp.int32, (C_OUT, C_OUT), 0)
        spots = lax.broadcasted_iota(jnp.int32, (C_OUT, C_OUT), 1)
        same = lines % GROUP == spots % GROUP
        row = lax.broadcasted_iota(jnp.int32, (32, C_OUT), 0)
        col = lax.broadcasted_iota(jnp.int32, (32, C_OUT), 1)
        down = (row == col // GROUP).astype(f32)
        sums = jnp.sum(own_grad[...], axis=1)
        sums = jnp.sum(sums, axis=1, keepdims=True)
        row = lax.broadcasted_iota(jnp.int32, (JOINTS, 128), 0)
        col = lax.broadcasted_iota(jnp.int32, (JOINTS, 128), 1)
        packed = jnp.where(row == col, jnp.broadcast_to(sums, (JOINTS, 128)), 0.0)
        packed = jnp.concatenate([packed, jnp.zeros((32 - JOINTS, 128), f32)], axis=0)
        row = lax.broadcasted_iota(jnp.int32, (C_OUT, 128), 0)
        col = lax.broadcasted_iota(jnp.int32, (C_OUT, 128), 1)
        for k in range(2):
            kept = jnp.where(same, eg[k * C_OUT : (k + 1) * C_OUT, :], 0.0)
            narrow = lax.dot_general(
                down, kept, (((1,), (1,)), ((), ())),
                preferred_element_type=f32, precision=lax.Precision.HIGHEST,
            )
            place = (row // GROUP + 32 * (k + 1) == col).astype(f32)
            packed = packed + jnp.dot(
                narrow, place, preferred_element_type=f32, precision=lax.Precision.HIGHEST
            )
        total.start(0, packed)

    @pl.when(step == pairs)
    def _():
        gather.end(0)
        gather.start(1)

    @pl.when(step == pairs + 1)
    def _():
        total.start(1, total.end(0))

    @pl.when(step == pairs + 2)
    def _():
        gather_taps.end(1)
        gather_taps.start(2)

    @pl.when(step == pairs + 3)
    def _():
        gather.end(1)
        gather.start(2)

    @pl.when(step == 2 * pairs - 1)
    def _():
        edge_ref[...] = total.end(1)
        gather_taps.end(2)
        taps_sum_ref[...] = gather_taps.full[...].reshape(taps_sum_ref.shape)
        gather.end(2)
        sum_ref[...] = gather.full[...].reshape(sum_ref.shape)


def update(
    grads_ref, graph_grad_ref, edge_grad_ref, gm_ref, st_ref, cs_ref, bk_ref, fs_ref, ig_ref, o_ref,
    *refs,
):
    groups = [refs[4 * k : 4 * k + 4] for k in range(5)]
    out_ig, out_o, out_norm = refs[20:23]
    outs = [refs[23 + 4 * k : 27 + 4 * k] for k in range(5)]
    squares, norm_grad = refs[43:45]
    step = pl.program_id(0)
    taps_rows = TAPS * C_OUT

    def edge_grad(k):
        values = edge_grad_ref[...]
        if k:
            values = pltpu.roll(values, 128 - 32 * k, 1)
        return values[0:JOINTS, 0:JOINTS] * gm_ref[k]

    def apply(group, out, at, gradient, rate, decay):
        factor = squares[0:1, 0:1]
        new = adam_update(*[ref[at] for ref in group], gradient, factor, rate, decay)
        for ref, value in zip(out, new):
            ref[at] = value

    @pl.when(step == 0)
    def _():
        stats = st_ref[...]
        norm = groups[4][0][...]
        mean, rstd, _, _ = first_moments(stats, norm)
        first_sum = fs_ref[0:1]
        first_norm = rstd * (fs_ref[1:2] - mean * first_sum)
        back_sum, back_conv, back_short = back_totals(
            bk_ref[...], second_moments(stats, cs_ref[...])
        )
        norm_grad[...] = jnp.concatenate(
            [first_norm, first_sum, back_conv, back_sum, back_short, back_sum], axis=0
        )
        total = jnp.zeros((GROUP, C_OUT), f32)
        for start in range(0, taps_rows + C_IN, C_IN):
            rows = grads_ref[start : start + C_IN, :].astype(f32)
            total = total + fold(rows * rows)
        for start in range(0, SUBSETS * C_IN, C_IN):
            rows = graph_grad_ref[start : start + C_IN, :].astype(f32)
            total = total + fold(rows * rows)
        whole = jnp.sum(total) + jnp.sum(norm_grad[...] * norm_grad[...])
        for k in range(SUBSETS):
            values = edge_grad(k)
            whole = whole + jnp.sum(values * values)
        size = jnp.sqrt(jnp.full((GROUP, 128), whole, f32))
        squares[...] = jnp.minimum(1.0, clip_limit / (size + 1e-06))
        out_norm[...] = size
        every = (slice(None), slice(None))
        apply(groups[4], outs[4], every, norm_grad[...], rate_small, 0.0)
        for k in range(SUBSETS):
            apply(groups[3], outs[3], k, edge_grad(k), rate_small, 0.0)

    for k in range(3):
        row = (3 * (step // 2) + k) * C_OUT
        lane = (step % 2) * C_IN
        at = (pl.ds(pl.multiple_of(row, C_OUT), C_OUT), pl.ds(pl.multiple_of(lane, C_IN), C_IN))
        apply(groups[1], outs[1], k, grads_ref[at].astype(f32).T, rate_matrix, decay_matrix)
    rows = graph_grad_ref[pl.ds(pl.multiple_of(step * 64, 64), 64), :].astype(f32)
    every = (slice(None), slice(None))
    apply(groups[0], outs[0], every, rows, rate_matrix, decay_matrix)

    @pl.when(step == 0)
    def _():
        rows = grads_ref[taps_rows : taps_rows + C_IN, :].astype(f32)
        every = (slice(None), slice(None))
        apply(groups[2], outs[2], every, rows, rate_matrix, decay_matrix)

    out_ig[...] = ig_ref[...]
    out_o[...] = o_ref[...]


def whole_spec(shape):
    return pl.BlockSpec(shape, lambda i: (0,) * len(shape))


def lead_spec(shape):
    return pl.BlockSpec(shape, lambda i: (i,) + (0,) * (len(shape) - 1))


def spec(block, index):
    return pl.BlockSpec(block, index)


def by_step(block):
    return spec(block, lambda i: (i,) + (0,) * (len(block) - 1))


def call(body, steps, ins, outs, scratch, name, **more):
    def to_spec(where, shape):
        if where is None:
            return whole_spec(shape)
        return where if isinstance(where, pl.BlockSpec) else by_step(where)

    return pl.pallas_call(
        body,
        grid=(steps,),
        in_specs=[to_spec(where, array.shape) for array, where in ins],
        out_specs=[to_spec(where, shape) for shape, _, where in outs],
        out_shape=[jax.ShapeDtypeStruct(shape, kind) for shape, kind, _ in outs],
        scratch_shapes=scratch,
        compiler_params=params(**more),
        name=name,
    )(*[array for array, _ in ins])


def shards(
    inputs, cotangent, lengths, frame_mask, subsets,
    graph_weight, graph_moment, graph_square, graph_average,
    temporal_weight, temporal_moment, temporal_square, temporal_average,
    shortcut_weight, shortcut_moment, shortcut_square, shortcut_average,
    edge_weight, edge_moment, edge_square, edge_average,
    norm_params, norm_moment, norm_square, norm_average,
):
    clips = inputs.shape[0]
    frames = inputs.shape[1]
    pairs = clips // 2
    natural = jnp.transpose(inputs, (0, 2, 1, 3))
    cot = jnp.transpose(cotangent, (0, 2, 1, 3))

    x_block = (2, JOINTS, frames, C_IN)
    mask_block = (1, PHASES, 2 * GROUP, 128)
    wide_block = (1, PHASES, ROWS, C_OUT)
    out_block = (1, 4, ROWS, C_OUT)
    xe_block = (1, 4, ROWS, C_IN)
    a_block = (1, 2, 8, ROWS, C_OUT)
    rim_block = (1, 2, 64, C_OUT)
    xq_block = (1, PHASES, C_OUT, C_OUT)
    cot_block = (2, JOINTS, frames // 2, C_OUT)
    edge_block = (1, JOINTS, 2 * GROUP, C_IN)
    end_block = (clips, JOINTS, 2 * GROUP, C_IN)
    small = (8, C_OUT)
    dma = pltpu.SemaphoreType.DMA

    def full(block):
        return (pairs,) + block[1:]

    def by_pair(block, pair):
        return spec(block, lambda i: (jnp.clip(pair(i), 0, pairs - 1),) + (0,) * (len(block) - 1))

    def early(block):
        return by_pair(block, lambda i: i)

    def behind(block):
        return by_pair(block, lambda i: i - 1)

    def late(block):
        return by_pair(block, lambda i: i - pairs)

    def later(block):
        return by_pair(block, lambda i: i - pairs - 1)

    vmem = pl.BlockSpec(memory_space=pltpu.VMEM)
    shapes = [
        ((clips * frames, 128), f32),
        ((clips * GROUP, 128), f32),
        ((2 * HALF_ROWS, C_OUT), bf16),
        ((HALF_ROWS, 2 * C_OUT), bf16),
        ((JOINTS, GROUP, C_IN), f32),
        ((SUBSETS, JOINTS, JOINTS), f32),
        ((SUBSETS * C_IN, C_OUT), bf16),
        ((C_OUT, SUBSETS * C_IN), bf16),
        ((C_IN, C_OUT), bf16),
        ((C_OUT, C_IN), bf16),
        ((TAPS, C_OUT, C_OUT), bf16),
    ]
    masks, edge_masks, kron, kront, own, graph_mask, wg, wgt, ws, wst, taps = pl.pallas_call(
        prepare,
        in_specs=[pl.BlockSpec(memory_space=pltpu.SMEM)] + [vmem] * 6,
        out_specs=[vmem] * 11,
        out_shape=[jax.ShapeDtypeStruct(shape, kind) for shape, kind in shapes],
        compiler_params=pltpu.CompilerParams(vmem_limit_bytes=60 * 2**20),
        name="prepare",
    )(lengths, frame_mask, subsets, edge_weight, graph_weight, shortcut_weight, temporal_weight)
    masks = masks.reshape(pairs, PHASES, 2 * GROUP, 128)

    xq, xe, hidden, stats, rims, rim_mask = call(
        graph_forward,
        pairs + 1,
        [
            (natural, early(x_block)),
            (natural, spec(end_block, lambda i: (0, 0, 0, 0))),
            (natural, spec(end_block, lambda i: (0, 0, frames // end_block[2] - 1, 0))),
            (masks, early(mask_block)),
            (edge_masks, None),
            (kron, None),
            (own, None),
            (wg, None),
            (ws, None),
        ],
        [
            (full(xq_block), bf16, early(xq_block)),
            (full(xe_block), bf16, early(xe_block)),
            (full(wide_block), bf16, behind(wide_block)),
            (small, f32, None),
            (full(edge_block), bf16, None),
            (edge_masks.shape, f32, None),
        ],
        [
            pltpu.VMEM((PHASES, 2, JOINTS, GROUP, C_IN), f32),
            pltpu.VMEM((PHASES, ROWS, SUBSETS * C_IN), bf16),
            pltpu.VMEM((4, ROWS, C_IN), bf16),
            pltpu.VMEM((4, GROUP, C_OUT), f32),
            pltpu.VMEM((2, 2 * GROUP, 128), f32),
            pltpu.VMEM(full(edge_block), bf16),
            pltpu.VMEM(full(edge_block), bf16),
            pltpu.VMEM(full(edge_block), bf16),
            pltpu.VMEM(edge_masks.shape, f32),
            pltpu.VMEM(edge_masks.shape, f32),
        ]
        + [dma((2,))] * 4
        + sum_scratch(),
        "graph_forward",
        collective_id=1,
        has_side_effects=True,
    )

    active, conv, conv_stats = call(
        conv_forward,
        pairs,
        [
            (hidden, wide_block),
            (rims, edge_block),
            (masks, mask_block),
            (rim_mask, (2 * GROUP, 128)),
            (stats, None),
            (norm_params, None),
            (kron, None),
            (own, None),
            (wg, None),
            (taps, None),
        ],
        [
            (full(a_block), bf16, a_block),
            (full(out_block), f32, out_block),
            (small, f32, None),
        ],
        [
            pltpu.VMEM((C_OUT, C_OUT), bf16),
            pltpu.VMEM((2, ROWS, HALF), f32),
            pltpu.VMEM((4, 2, ROWS, HALF), f32),
            pltpu.VMEM((2, GROUP, C_OUT), f32),
        ]
        + sum_scratch(),
        "conv_forward",
        collective_id=2,
        has_side_effects=True,
    )

    def both_ways(block):
        return by_pair(block, lambda i: jnp.where(i < pairs, i, i - pairs))

    grad_rows = padded(TAPS * C_OUT + C_IN)
    outputs, conv_grad, short_grad, left_rim, right_rim, grads, back = call(
        middle,
        2 * pairs + 1,
        [
            (conv, early(out_block)),
            (xe, both_ways(xe_block)),
            (cot, early(cot_block)),
            (active, later(a_block)),
            (masks, both_ways(mask_block)),
            (stats, None),
            (conv_stats, None),
            (norm_params, None),
            (ws, None),
        ],
        [
            (cot.shape, bf16, early(cot_block)),
            (full(out_block), bf16, late(out_block)),
            (full(out_block), bf16, late(out_block)),
            (full(rim_block), bf16, None),
            (full(rim_block), bf16, None),
            ((grad_rows, C_OUT), bf16, None),
            (small, f32, None),
        ],
        [
            pltpu.VMEM((2, 2, JOINTS, frames // 2, HALF), f32),
            pltpu.VMEM((2, 2, JOINTS, frames // 2, HALF), f32),
            pltpu.VMEM((3, GROUP, C_OUT), f32),
            pltpu.VMEM(full(out_block), f32),
            pltpu.VMEM(full(out_block), f32),
            pltpu.VMEM((C_OUT, DEPTH), bf16),
            pltpu.VMEM((2, ROWS, HALF), f32),
            pltpu.VMEM((TAPS, C_OUT, C_OUT), f32),
            pltpu.VMEM((C_IN, C_OUT), f32),
        ]
        + [pltpu.VMEM(full(rim_block), bf16)] * 4
        + [dma((pairs,))] * 4
        + sum_scratch(),
        "middle",
        collective_id=3,
        has_side_effects=True,
    )

    graph_rows = padded(SUBSETS * C_IN)
    hidden_grad, first_sums, grad_piece, graph_grad = call(
        conv_back,
        2 * pairs + 1,
        [
            (conv_grad, early(out_block)),
            (left_rim, early(rim_block)),
            (right_rim, early(rim_block)),
            (taps, None),
            (hidden, early(wide_block)),
            (masks, by_pair(mask_block, lambda i: jnp.where(i <= pairs, i - 1, i - pairs - 1))),
            (stats, None),
            (norm_params, None),
            (xq, later(xq_block)),
            (kron, None),
            (own, None),
            (grads, None),
        ],
        [
            (full(wide_block), bf16, later(wide_block)),
            (small, f32, None),
            ((grad_rows // lax.axis_size(("tm", "batch")), C_OUT), bf16, None),
            ((graph_rows, C_OUT), bf16, None),
        ],
        [
            pltpu.VMEM((2, 2, ROWS, HALF), f32),
            pltpu.VMEM((8, ROWS, C_OUT), bf16),
            pltpu.VMEM((2, GROUP, C_OUT), f32),
            pltpu.VMEM(full(wide_block), f32),
            pltpu.VMEM(full(wide_block), bf16),
            pltpu.VMEM((PHASES, ROWS, C_OUT), f32),
            pltpu.VMEM((PHASES, ROWS, SUBSETS * C_IN), bf16),
            pltpu.VMEM((SUBSETS * C_IN, C_OUT), f32),
        ]
        + sum_scratch()
        + Scatter.scratch(grad_rows),
        "conv_back",
        collective_id=4,
        has_side_effects=True,
    )

    input_grad, grad_sums, graph_sum, edge_sum = call(
        graph_back,
        2 * pairs,
        [
            (hidden_grad, early(wide_block)),
            (xq, early(xq_block)),
            (short_grad, late(out_block)),
            (wgt, None),
            (wst, None),
            (kront, None),
            (own, None),
            (grad_piece, None),
            (graph_grad, None),
        ],
        [
            (natural.shape, bf16, late(x_block)),
            ((grad_rows, C_OUT), bf16, None),
            ((graph_rows, C_OUT), bf16, None),
            ((32, 128), f32, None),
        ],
        [
            pltpu.VMEM((pairs, PHASES, SUBSETS, C_OUT, C_OUT), bf16),
            pltpu.VMEM((PHASES, JOINTS, GROUP, 2 * C_IN), f32),
            pltpu.VMEM((2 * C_OUT, C_OUT), f32),
            pltpu.VMEM((JOINTS, GROUP, 2 * C_IN), f32),
        ]
        + sum_scratch((32, 128))
        + Gather.scratch(grad_rows)
        + Scatter.scratch(graph_rows)
        + Gather.scratch(graph_rows),
        "graph_back",
        collective_id=5,
        has_side_effects=True,
    )

    tap_spec = spec((TAPS // 3, C_IN, C_OUT), lambda i: (i // 2, i % 2, 0))
    graph_spec = spec((64, C_OUT), lambda i: (i % 2, i // 2))
    states = [
        (graph_weight, graph_moment, graph_square, graph_average),
        (temporal_weight, temporal_moment, temporal_square, temporal_average),
        (shortcut_weight, shortcut_moment, shortcut_square, shortcut_average),
        (edge_weight, edge_moment, edge_square, edge_average),
        (norm_params, norm_moment, norm_square, norm_average),
    ]
    places = [graph_spec, tap_spec, None, None, None]
    state_ins = [(array, place) for group, place in zip(states, places) for array in group]
    clip_spec = spec((clips // 6, JOINTS, frames, C_IN), lambda i: (i, 0, 0, 0))
    out_spec = spec((clips // 6, JOINTS, frames // 2, C_OUT), lambda i: (i, 0, 0, 0))
    new = call(
        update,
        6,
        [
            (grad_sums, None),
            (graph_sum, None),
            (edge_sum, None),
            (graph_mask, None),
            (stats, None),
            (conv_stats, None),
            (back, None),
            (first_sums, None),
            (input_grad, clip_spec),
            (outputs, out_spec),
        ]
        + state_ins,
        [(natural.shape, bf16, clip_spec), (cot.shape, bf16, out_spec), ((GROUP, 128), f32, None)]
        + [(array.shape, f32, place) for array, place in state_ins],
        [pltpu.VMEM((GROUP, 128), f32), pltpu.VMEM((6, C_OUT), f32)],
        "update",
    )
    return (
        jnp.transpose(new[1], (0, 2, 1, 3)),
        jnp.transpose(new[0], (0, 2, 1, 3)),
        new[2][0, 0:1],
        *new[3:],
    )


def solution(mesh):
    rows = P("batch", "tm", None, None)
    in_specs = (rows, rows, P("batch"), P("batch", "tm")) + (P(),) * 21
    out_specs = (rows, rows) + (P(),) * 21
    return jax.shard_map(shards, mesh=mesh, in_specs=in_specs, out_specs=out_specs, check_vma=False)
```

```python
import functools

import jax
import jax.numpy as jnp
from jax import lax
from jax.experimental import pallas as pl
from jax.experimental.pallas import tpu as pltpu
from jax.sharding import PartitionSpec as P

C_IN = 128
C_OUT = 256
JOINTS = 25
SUBSETS = 3
TAPS = 9
GROUP = 8
PHASES = 8
UNITS = 2 * JOINTS
ROWS = UNITS * GROUP
HALF_ROWS = JOINTS * GROUP
HALF = C_IN
CUT = 5
DEPTH = 4 * ROWS + 64

f32 = jnp.float32
bf16 = jnp.bfloat16

norm_epsilon = 1e-05
beta_first = 0.9
beta_second = 0.999
adam_epsilon = 1e-08
clip_limit = 1.0
average_decay = 0.9
rate_matrix = 0.05
rate_small = 0.3
decay_matrix = 0.01
steps_taken = 3.0


def params(**more):
    return pltpu.CompilerParams(
        vmem_limit_bytes=60 * 2**20, dimension_semantics=("arbitrary",), **more
    )


def adjacency(subsets):
    linked = (subsets > 0).astype(f32)
    degree = jnp.sum(linked, axis=0)
    labels = jnp.arange(SUBSETS, dtype=jnp.int32) + 1
    chosen = (subsets[None, :, :] == labels[:, None, None]).astype(f32)
    return chosen / degree[None, None, :]


def adam_update(weight, moment, square, average, gradient, factor, rate, decay):
    fix_first = 1.0 - beta_first**steps_taken
    fix_second = 1.0 - beta_second**steps_taken
    clipped = gradient * factor
    moment_new = beta_first * moment + (1.0 - beta_first) * clipped
    square_new = beta_second * square + (1.0 - beta_second) * clipped * clipped
    scaled = square_new * (1.0 / fix_second)
    below = scaled * lax.rsqrt(scaled) + adam_epsilon
    guess = pl.reciprocal(below, approx=True)
    guess = guess * (2.0 - below * guess)
    stepped = moment_new * (1.0 / fix_first) * guess
    weight_new = weight - rate * (stepped + decay * weight)
    average_new = average_decay * average + (1.0 - average_decay) * weight_new
    return (weight_new, moment_new, square_new, average_new)


def dot(a, b):
    return jnp.dot(a, b, preferred_element_type=f32)


def dot_nt(a, b):
    return lax.dot_general(a, b, (((1,), (1,)), ((), ())), preferred_element_type=f32)


def dot_tn(a, b):
    return lax.dot_general(a, b, (((0,), (0,)), ((), ())), preferred_element_type=f32)


def fold(values):
    return jnp.sum(values.reshape(-1, GROUP, values.shape[-1]), axis=0)


MESH = pl.DeviceIdType.MESH


def peers(axis):
    count = lax.axis_size(axis)
    here = lax.axis_index(axis)
    return [(d, {axis: lax.rem(here + d, count)}) for d in range(1, count)]


def greet():
    barrier = pltpu.get_barrier_semaphore()
    for axis in ("tm", "batch"):
        for _, device in peers(axis):
            pl.semaphore_signal(barrier, inc=1, device_id=device, device_id_type=MESH)


def await_greetings():
    count = lax.axis_size("tm") + lax.axis_size("batch") - 2
    pl.semaphore_wait(pltpu.get_barrier_semaphore(), count)


class Total:
    def __init__(self, buffers):
        self.levels = list(zip(("tm", "batch"), (buffers[0:3], buffers[3:6])))

    def copies(self, level):
        axis, (slots, sent, received) = self.levels[level]
        here = lax.axis_index(axis)
        return [
            remote(slots.at[here], slots.at[here], sent.at[d], received.at[d], device)
            for d, device in peers(axis)
        ]

    def start(self, level, values):
        axis, (slots, _, _) = self.levels[level]
        slots[lax.axis_index(axis)] = values
        for copy in self.copies(level):
            copy.start()

    def end(self, level):
        axis, (slots, _, _) = self.levels[level]
        for copy in self.copies(level):
            copy.wait()
        values = slots[0]
        for k in range(1, lax.axis_size(axis)):
            values = values + slots[k]
        return values


def sum_all(values, buffers):
    total = Total(buffers)
    total.start(0, values)
    total.start(1, total.end(0))
    return total.end(1)


def sum_scratch(shape=(8, C_OUT)):
    found = []
    for axis in ("tm", "batch"):
        count = lax.axis_size(axis)
        found += [
            pltpu.VMEM((count, *shape), f32),
            pltpu.SemaphoreType.DMA((count,)),
            pltpu.SemaphoreType.DMA((count,)),
        ]
    return found


def remote(source, target, sent, received, device):
    return pltpu.make_async_remote_copy(
        src_ref=source,
        dst_ref=target,
        send_sem=sent,
        recv_sem=received,
        device_id=device,
        device_id_type=MESH,
    )


def with_neighbours(step, low, high, from_left, from_right, sems, act):
    here = lax.axis_index("tm")
    last = lax.axis_size("tm") - 1
    sent_right, got_left, sent_left, got_right = sems

    def rightward():
        return remote(high, from_left, sent_right.at[step], got_left.at[step], {"tm": here + 1})

    def leftward():
        return remote(low, from_right, sent_left.at[step], got_right.at[step], {"tm": here - 1})

    if act == "start":

        @pl.when(here < last)
        def _():
            rightward().start()

        @pl.when(here > 0)
        def _():
            leftward().start()

    else:

        @pl.when(here < last)
        def _():
            rightward().wait_send()
            leftward().wait_recv()

        @pl.when(here > 0)
        def _():
            leftward().wait_send()
            rightward().wait_recv()


def first_moments(stats, norm):
    count_in = stats[4:5]
    mean = stats[0:1] / count_in
    rstd = lax.rsqrt(stats[1:2] / count_in - mean * mean + norm_epsilon)
    return mean, rstd, norm[0:1] * rstd, norm[1:2] - norm[0:1] * rstd * mean


def one_hot_rows(rows, columns):
    row = lax.broadcasted_iota(jnp.int32, (rows, columns), 0)
    col = lax.broadcasted_iota(jnp.int32, (rows, columns), 1)
    return (row // GROUP == col).astype(bf16)


def prepare(
    length_ref, frame_ref, subset_ref, edge_ref, graph_ref, short_ref, taps_ref,
    m_ref, em_ref, kron_ref, kront_ref, own_ref, gm_ref, wg_ref, wgt_ref, ws_ref, wst_ref, low_ref,
):
    clips, frames = frame_ref.shape
    first = lax.axis_index("tm") * frames
    row = lax.broadcasted_iota(jnp.int32, (clips, frames), 0)
    ids = lax.broadcasted_iota(jnp.int32, (clips, frames), 1) + first
    ends = jnp.zeros((clips, frames), jnp.int32)
    for clip in range(clips):
        ends = jnp.where(row == clip, length_ref[clip], ends)
    mask = ((ids < ends) & (frame_ref[...] > 0)).astype(bf16)
    every = jnp.ones((frames, 128), bf16)

    def spread(rows, clip_of, frame_of):
        at = lax.broadcasted_iota(jnp.int32, (rows, clips), 0)
        chosen = (clip_of(at) == lax.broadcasted_iota(jnp.int32, (rows, clips), 1)).astype(bf16)
        lines = dot(chosen, mask)
        at = lax.broadcasted_iota(jnp.int32, (rows, frames), 0)
        kept = frame_of(at) == lax.broadcasted_iota(jnp.int32, (rows, frames), 1)
        return dot(jnp.where(kept, lines, 0.0).astype(bf16), every)

    side = 2 * GROUP
    m_ref[...] = spread(
        clips * frames,
        lambda at: 2 * (at // (PHASES * side)) + at // GROUP % 2,
        lambda at: PHASES * (at % GROUP) + at // side % PHASES,
    )
    em_ref[...] = spread(
        clips * GROUP, lambda at: at // GROUP, lambda at: (at % GROUP + frames - 4) % frames
    )
    subsets = subset_ref[...]
    degree = jnp.sum((subsets > 0).astype(f32), axis=0, keepdims=True)
    lift = one_hot_rows(HALF_ROWS, JOINTS)
    row = lax.broadcasted_iota(jnp.int32, (JOINTS, C_OUT), 0)
    drop = (row == lax.broadcasted_iota(jnp.int32, (JOINTS, C_OUT), 1) // GROUP).astype(bf16)
    row = lax.broadcasted_iota(jnp.int32, (HALF_ROWS, C_OUT), 0)
    same = row % GROUP == lax.broadcasted_iota(jnp.int32, (HALF_ROWS, C_OUT), 1) % GROUP
    for k in range(SUBSETS):
        share = (subsets == k + 1).astype(f32) / degree
        gm_ref[k] = share
        low = (share * edge_ref[k]).astype(bf16)
        if k == 0:
            row = lax.broadcasted_iota(jnp.int32, (JOINTS, JOINTS), 0)
            col = lax.broadcasted_iota(jnp.int32, (JOINTS, JOINTS), 1)
            diagonal = jnp.sum(jnp.where(row == col, low.astype(f32), 0.0), axis=1, keepdims=True)
            wide = jnp.broadcast_to(diagonal, (JOINTS, C_IN)).astype(bf16)
            own_ref[...] = dot(lift, wide).reshape(JOINTS, GROUP, C_IN)
        else:
            ahead = dot(lift, dot_tn(low, drop).astype(bf16))
            rows = slice((k - 1) * HALF_ROWS, k * HALF_ROWS)
            kron_ref[rows, :] = jnp.where(same, ahead, 0.0).astype(bf16)
            behind = dot(lift, dot(low, drop).astype(bf16))
            lanes = slice((k - 1) * C_OUT, k * C_OUT)
            kront_ref[:, lanes] = jnp.where(same, behind, 0.0).astype(bf16)
        block = graph_ref[:, k * C_OUT : (k + 1) * C_OUT]
        wg_ref[k * C_IN : (k + 1) * C_IN, :] = block.astype(bf16)
        wgt_ref[:, k * C_IN : (k + 1) * C_IN] = block.T.astype(bf16)
    ws_ref[...] = short_ref[...].astype(bf16)
    wst_ref[...] = short_ref[...].T.astype(bf16)
    low_ref[...] = taps_ref[...].astype(bf16)


def mix_rows(parts, scales, kron_ref, wide_ref):
    mixed = dot(kron_ref[...], wide_ref[...])
    sides = []
    for side in range(2):
        lanes = slice(side * HALF, (side + 1) * HALF)
        sides.append(
            jnp.concatenate(
                [
                    parts[side] * scales,
                    mixed[0:HALF_ROWS, lanes].reshape(JOINTS, GROUP, C_IN),
                    mixed[HALF_ROWS : 2 * HALF_ROWS, lanes].reshape(JOINTS, GROUP, C_IN),
                ],
                axis=2,
            )
        )
    return jnp.concatenate(sides, axis=1).reshape(ROWS, SUBSETS * C_IN).astype(bf16)


def put_wide(parts, wide_ref):
    wide = jnp.concatenate([part.reshape(HALF_ROWS, C_IN) for part in parts], axis=1)
    wide_ref[0:HALF_ROWS, :] = wide.astype(bf16)


def graph_forward(
    x_ref, all_ref, m_ref, em_ref, kron_ref, own_ref, wg_ref, ws_ref,
    xq_ref, xe_ref, h_ref, st_ref, rim_ref, rim_mask_ref,
    xs, xg, xe, head, tail, end_sems, sums, counts, mine, lefts, rights, mask_lefts, mask_rights,
    sent_right, got_left, sent_left, got_right, *sum_buffers,
):
    step = pl.program_id(0)
    last = pl.num_programs(0) - 1
    sems = (sent_right, got_left, sent_left, got_right)

    def rims(act):
        with_neighbours(0, mine, mine, lefts, rights, sems, act)
        with_neighbours(1, em_ref, em_ref, mask_lefts, mask_rights, sems, act)

    depth = head.shape[2]
    end_copies = [
        pltpu.make_async_copy(all_ref.at[:, :, 0:depth], head, end_sems.at[0]),
        pltpu.make_async_copy(
            all_ref.at[:, :, all_ref.shape[2] - depth : all_ref.shape[2]], tail, end_sems.at[1]
        ),
    ]

    @pl.when(step == 0)
    def _():
        for ref in (lefts, rights, mask_lefts, mask_rights):
            ref[...] = jnp.zeros_like(ref)
        greet()
        for copy in end_copies:
            copy.start()
        sums[...] = jnp.zeros_like(sums)
        counts[...] = jnp.zeros_like(counts)

    def permute():
        for side in range(2):
            for start in range(0, JOINTS, CUT):
                rows = x_ref[side, start : start + CUT].astype(f32)
                rows = jnp.swapaxes(rows.reshape(CUT, GROUP, PHASES, C_IN), 1, 2)
                for c in range(PHASES):
                    mask = m_ref[0, c, side * GROUP : (side + 1) * GROUP]
                    xs[c, side, start : start + CUT] = rows[:, c] * mask[None]

    def mix(c):
        xq_ref[0, c, HALF_ROWS:, :] = jnp.zeros((C_OUT - HALF_ROWS, C_OUT), bf16)
        parts = [xs[c, 0], xs[c, 1]]
        put_wide(parts, xq_ref.at[0, c])
        xg[c] = mix_rows(parts, own_ref[...], kron_ref, xq_ref.at[0, c])
        counts[0] += m_ref[0, c]
        if c % 2 == 0:
            counts[1] += m_ref[0, c]
            even = jnp.concatenate(parts, axis=1).reshape(ROWS, C_IN).astype(bf16)
            xe_ref[0, c // 2] = even
            xe[c // 2] = even

    def project(c):
        hidden = dot(xg[c : c + 2].reshape(2 * ROWS, SUBSETS * C_IN), wg_ref[...])
        h_ref[0, c : c + 2] = hidden.reshape(2, ROWS, C_OUT).astype(bf16)
        sums[0] += fold(hidden)
        sums[1] += fold(hidden * hidden)
        short = dot(xe[c // 2], ws_ref[...])
        sums[2] += fold(short)
        sums[3] += fold(short * short)

    @pl.when(step == 0)
    def _():
        permute()
        for c in range(PHASES):
            mix(c)

    @pl.when((step > 0) & (step < last))
    def _():
        permute()
        for c in range(0, PHASES, 2):
            project(c)
            mix(c)
            mix(c + 1)

    @pl.when(step == last)
    def _():
        for c in range(0, PHASES, 2):
            project(c)

    @pl.when(step == 1)
    def _():
        for copy in end_copies:
            copy.wait()
        for pair in range(mine.shape[0]):
            ends = []
            for clip in (2 * pair, 2 * pair + 1):
                above = pltpu.roll(tail[clip].astype(f32)[:, GROUP:], 4, 1)
                below = pltpu.roll(head[clip].astype(f32)[:, :GROUP], 4, 1)
                sub = lax.broadcasted_iota(jnp.int32, above.shape, 1)
                ends.append(jnp.where(sub < 4, above, below))
            mine[pair] = jnp.concatenate(ends, axis=1).astype(bf16)
        await_greetings()
        rims("start")

    @pl.when(step == last)
    def _():
        rows = [jnp.sum(sums[k], axis=0, keepdims=True) for k in range(4)]
        for k in range(2):
            total = JOINTS * jnp.sum(counts[k], axis=0, keepdims=True)
            rows.append(jnp.concatenate([total, total], axis=1))
        rows.append(jnp.zeros((2, C_OUT), f32))
        total = Total(sum_buffers)
        total.start(0, jnp.concatenate(rows, axis=0))
        rims("wait")
        sub = lax.broadcasted_iota(jnp.int32, mask_lefts.shape, 0) % GROUP
        rim_mask_ref[...] = jnp.where(sub < 4, mask_lefts[...], mask_rights[...])
        total.start(1, total.end(0))
        for pair in range(lefts.shape[0]):
            sub = lax.broadcasted_iota(jnp.int32, lefts.shape[1:], 1) % GROUP
            both = jnp.where(sub < 4, lefts[pair].astype(f32), rights[pair].astype(f32))
            rim_ref[pair] = both.astype(bf16)
        st_ref[...] = total.end(1)


def insert_and_roll(tiles, fill, side):
    sub = lax.broadcasted_iota(jnp.int32, tiles.shape, 1)
    joined = jnp.where(sub == side, fill, tiles)
    return pltpu.roll(joined, 1 if side == 7 else GROUP - 1, 1)


def conv_forward(
    h_ref, xh_ref, m_ref, mh_ref, st_ref, norm_ref, kron_ref, own_ref, wg_ref, taps_ref,
    a_ref, conv_ref, out_ref,
    pad, rims, fills, sums, *sum_buffers,
):
    step = pl.program_id(0)

    @pl.when(step == 0)
    def _():
        greet()
        sums[...] = jnp.zeros_like(sums)
        pad[...] = jnp.zeros_like(pad)

    _, _, scale, shift = first_moments(st_ref[...], norm_ref[...])
    scale, shift = 0.5 * scale, 0.5 * shift

    def activate(values, offset):
        half = values.reshape(-1, 2 * GROUP, C_OUT) * scale + offset
        return half + half * jnp.tanh(half)

    def wide(mask):
        return jnp.concatenate([mask, mask], axis=1)[None]

    rim_mask = mh_ref[...]
    rim_rows = xh_ref[0].astype(f32) * rim_mask[None]
    parts = [rim_rows[:, side * GROUP : (side + 1) * GROUP] for side in range(2)]
    put_wide(parts, pad)
    rim_hidden = dot(mix_rows(parts, own_ref[...], kron_ref, pad), wg_ref[...])
    rim_active = activate(rim_hidden, wide(rim_mask) * shift).reshape(ROWS, C_OUT)
    for lane in range(2):
        rims[lane] = rim_active[:, lane * HALF : (lane + 1) * HALF]
    for p in range(2):
        for q in range(2):
            for lane in range(2):
                fills[2 * p + q, lane, pl.ds(7, UNITS, stride=GROUP), :] = rims[
                    lane, pl.ds(2 * q + p, UNITS, stride=GROUP), :
                ]
                fills[2 * p + q, lane, pl.ds(0, UNITS, stride=GROUP), :] = rims[
                    lane, pl.ds(4 + 2 * q + p, UNITS, stride=GROUP), :
                ]

    a_ref[0, 1, 7, 0:64, :] = jnp.zeros((64, C_OUT), bf16)
    for c in range(PHASES):
        p, q = c % 2, c // 2
        offset = wide(m_ref[0, c]) * shift
        for start in range(0, JOINTS, CUT):
            rows = slice(start * 2 * GROUP, (start + CUT) * 2 * GROUP)
            active = activate(h_ref[0, c, rows, :].astype(f32), offset)
            a_ref[0, p, q + 2, rows, :] = active.reshape(-1, C_OUT).astype(bf16)
            if p == 1 and q == 1:
                continue
            tiles = active.reshape(-1, GROUP, C_OUT)
            fill = jnp.concatenate(
                [fills[2 * p + q % 2, lane, rows, :] for lane in range(2)], axis=1
            ).reshape(-1, GROUP, C_OUT)
            moved = insert_and_roll(tiles, fill, 7 if q >= 2 else 0)
            at = q - 2 if q >= 2 else q + 6
            a_ref[0, p, at, rows, :] = moved.reshape(-1, C_OUT).astype(bf16)

    total = None
    for j in range(TAPS):
        window = a_ref[0, j % 2, j // 2 : j // 2 + 4].reshape(4 * ROWS, C_OUT)
        part = dot(window, taps_ref[j])
        total = part if total is None else total + part
    for q in range(4):
        block = total[q * ROWS : (q + 1) * ROWS].reshape(JOINTS, 2 * GROUP, C_OUT)
        live = block * wide(m_ref[0, 2 * q])
        conv_ref[0, q] = live.reshape(ROWS, C_OUT)
        sums[0] += fold(live)
        sums[1] += fold(live * live)

    @pl.when(step == pl.num_programs(0) - 1)
    def _():
        await_greetings()
        rows = [jnp.sum(sums[k], axis=0, keepdims=True) for k in range(2)]
        rows.append(jnp.zeros((6, C_OUT), f32))
        out_ref[...] = sum_all(jnp.concatenate(rows, axis=0), sum_buffers)


def second_moments(stats, conv_stats):
    count_out = stats[5:6]
    mean_conv = conv_stats[0:1] / count_out
    rstd_conv = lax.rsqrt(conv_stats[1:2] / count_out - mean_conv * mean_conv + norm_epsilon)
    mean_short = stats[2:3] / count_out
    rstd_short = lax.rsqrt(stats[3:4] / count_out - mean_short * mean_short + norm_epsilon)
    return mean_conv, rstd_conv, mean_short, rstd_short


def back_totals(back, moments):
    mean_conv, rstd_conv, mean_short, rstd_short = moments
    back_sum = back[0:1]
    back_conv = rstd_conv * (back[1:2] - mean_conv * back_sum)
    back_short = rstd_short * (back[2:3] - mean_short * back_sum)
    return back_sum, back_conv, back_short


def middle(
    conv_ref, xe_ref, cot_ref, a_ref, m_ref, st_ref, cs_ref, norm_ref, ws_ref,
    o_ref, cg_ref, sg_ref, left_ref, right_ref, grad_ref, total_ref,
    cots, outs, sums, conv_kept, up_kept, turned, edges, tg, shg, low_rims, high_rims, lefts, rights,
    sent_right, got_left, sent_left, got_right, *sum_buffers,
):
    step = pl.program_id(0)
    pairs = low_rims.shape[0]
    sems = (sent_right, got_left, sent_left, got_right)

    def rims(at, act):
        with_neighbours(
            at, low_rims.at[at], high_rims.at[at], lefts.at[at], rights.at[at], sems, act
        )

    norm = norm_ref[...]
    stats = st_ref[...]
    moments = second_moments(stats, cs_ref[...])
    mean_conv, rstd_conv, mean_short, rstd_short = moments

    @pl.when(step == 0)
    def _():
        for ref in (sums, lefts, rights, tg, shg, turned, low_rims, high_rims):
            ref[...] = jnp.zeros_like(ref)
        greet()

    @pl.when(step < pairs)
    def _():
        scale_conv = 0.5 * norm[2:3] * rstd_conv
        scale_short = 0.5 * norm[4:5] * rstd_short
        shift = 0.5 * (norm[3:4] + norm[5:6]) - scale_conv * mean_conv - scale_short * mean_short
        for side in range(2):
            for joint in range(JOINTS):
                for lane in range(2):
                    cots[side, lane, joint] = cot_ref[
                        side, joint, :, lane * HALF : (lane + 1) * HALF
                    ].astype(f32)
        for q in range(4):
            mask = m_ref[0, 2 * q]
            mask = jnp.concatenate([mask, mask], axis=1)[None]
            short_all = dot(xe_ref[0, q], ws_ref[...])
            for start in range(0, JOINTS, CUT):
                rows = slice(start * 2 * GROUP, (start + CUT) * 2 * GROUP)
                conv = conv_ref[0, q, rows, :]
                conv_kept[step, q, rows, :] = conv
                short = short_all[rows]
                half = conv * scale_conv + short * scale_short + shift
                turn = jnp.tanh(half)
                grow = (1.0 + turn).reshape(CUT, 2 * GROUP, C_OUT) * mask
                half = half.reshape(CUT, 2 * GROUP, C_OUT)
                turn = turn.reshape(CUT, 2 * GROUP, C_OUT)
                result = half * grow
                slope = grow * (1.0 + (half - half * turn))
                cot = jnp.concatenate(
                    [
                        jnp.concatenate(
                            [
                                cots[side, lane, start : start + CUT, pl.ds(q, GROUP, stride=4), :]
                                for lane in range(2)
                            ],
                            axis=2,
                        )
                        for side in range(2)
                    ],
                    axis=1,
                )
                for side in range(2):
                    for lane in range(2):
                        outs[
                            side, lane, start : start + CUT, pl.ds(q, GROUP, stride=4), :
                        ] = result[
                            :, side * GROUP : (side + 1) * GROUP, lane * HALF : (lane + 1) * HALF
                        ]
                up = (cot * slope).reshape(-1, C_OUT)
                up_kept[step, q, rows, :] = up
                sums[0] += fold(up)
                sums[1] += fold(up * conv)
                sums[2] += fold(up * short)
        for side in range(2):
            for joint in range(JOINTS):
                for lane in range(2):
                    o_ref[side, joint, :, lane * HALF : (lane + 1) * HALF] = outs[
                        side, lane, joint
                    ].astype(bf16)

    @pl.when(step == pairs - 1)
    def _():
        rows = [0.5 * jnp.sum(sums[k], axis=0, keepdims=True) for k in range(3)]
        rows.append(jnp.zeros((5, C_OUT), f32))
        await_greetings()
        total_ref[...] = sum_all(jnp.concatenate(rows, axis=0), sum_buffers)

    def gradients(pair, q):
        back_sum, back_conv, back_short = back_totals(total_ref[...], moments)
        count_out = stats[5:6]

        def terms(gain, mean, rstd, back):
            lead = gain * rstd
            slope = lead * rstd * back / count_out
            return lead, slope, lead * back_sum / count_out - slope * mean

        lead_c, slope_c, shift_c = terms(norm[2:3], mean_conv, rstd_conv, back_conv)
        lead_s, slope_s, shift_s = terms(norm[4:5], mean_short, rstd_short, back_short)
        mask = m_ref[0, 2 * q]
        mask = jnp.concatenate([mask, mask], axis=1)[None]
        half_c, half_s = 0.5 * lead_c, 0.5 * lead_s
        offset_c, offset_s = mask * shift_c, mask * shift_s
        short_all = dot(xe_ref[0, q], ws_ref[...])
        for start in range(0, JOINTS, CUT):
            rows = slice(start * 2 * GROUP, (start + CUT) * 2 * GROUP)
            up = up_kept[pair, q, rows, :]

            def taken(values, slope, offset):
                shifted = values.reshape(CUT, 2 * GROUP, C_OUT) * slope + offset
                return shifted.reshape(-1, C_OUT)

            cg = up * half_c - taken(conv_kept[pair, q, rows, :], slope_c, offset_c)
            cg_ref[0, q, rows, :] = cg.astype(bf16)
            for lane in range(2):
                edges[lane, rows, :] = cg[:, lane * HALF : (lane + 1) * HALF]
            sg = up * half_s - taken(short_all[rows], slope_s, offset_s)
            sg_ref[0, q, rows, :] = sg.astype(bf16)
        for lane in range(2):
            at = slice(lane * HALF, (lane + 1) * HALF)
            target = low_rims if q < 2 else high_rims
            outer = edges[lane, pl.ds(0 if q < 2 else 7, UNITS, stride=GROUP), :]
            target[pair, q % 2, 0:UNITS, at] = outer.astype(bf16)

    def turn_over():
        turned[:, 0 : 4 * ROWS] = cg_ref[0].reshape(4 * ROWS, C_OUT).T
        shg[...] += dot_tn(
            xe_ref[0].reshape(4 * ROWS, C_IN), sg_ref[0].reshape(4 * ROWS, C_OUT)
        )

    def taps_of(first, end):
        every = a_ref[0].reshape(16 * ROWS, C_OUT)
        for j in range(first, end):
            at = (8 * (j % 2) + j // 2) * ROWS
            tg[j] += dot(turned[...], every[at : at + DEPTH])

    @pl.when(step == pairs)
    def _():
        for q in range(4):
            gradients(0, q)
        turn_over()

    @pl.when((step > pairs) & (step < 2 * pairs))
    def _():
        for q in range(4):
            taps_of(2 * q, 2 * q + 2)
            gradients(step - pairs, q)
        taps_of(8, 9)
        turn_over()

    @pl.when((step >= pairs) & (step < 2 * pairs))
    def _():
        rims(step - pairs, "start")

    @pl.when(step == 2 * pairs)
    def _():
        taps_of(0, 9)
        for j in range(TAPS):
            grad_ref[j * C_OUT : (j + 1) * C_OUT, :] = tg[j].astype(bf16)
        grad_ref[TAPS * C_OUT : TAPS * C_OUT + C_IN, :] = shg[...].astype(bf16)
        rest = grad_ref.shape[0] - TAPS * C_OUT - C_IN
        if rest:
            grad_ref[TAPS * C_OUT + C_IN :, :] = jnp.zeros((rest, C_OUT), bf16)
        for pair in range(pairs):
            rims(pair, "wait")
        left_ref[...] = lefts[...]
        right_ref[...] = rights[...]


def padded(rows):
    unit = 16 * lax.axis_size("tm") * lax.axis_size("batch")
    return (rows + unit - 1) // unit * unit


class Places:
    def __init__(self, rows, cores):
        tm = lax.axis_index("tm")
        self.cores = cores
        self.core = tm % cores
        self.line = tm // cores
        self.lines = lax.axis_size("tm") // cores
        self.batch = lax.axis_index("batch")
        self.batches = lax.axis_size("batch")
        self.half = rows // cores
        self.part = self.half // self.lines
        self.piece = self.part // self.batches

    def core_peer(self):
        return {"tm": 2 * self.line + 1 - self.core}

    def line_peers(self):
        for d in range(1, self.lines):
            to = lax.rem(self.line + d, self.lines)
            yield d, to, {"tm": self.cores * to + self.core}

    def batch_peers(self):
        for d in range(1, self.batches):
            to = lax.rem(self.batch + d, self.batches)
            yield d, to, {"batch": to}

    def rows(self, index, count):
        return pl.ds(pl.multiple_of(index * count, 16), count)


def three_levels(rows, cores):
    lines, batches = lax.axis_size("tm") // cores, lax.axis_size("batch")
    half = rows // cores
    return lines, batches, half, half // lines, half // lines // batches


class Scatter(Places):
    def __init__(self, source, refs, cores=2):
        super().__init__(source.shape[0], cores)
        self.source = source
        self.here, self.up, self.out, self.firsts, self.seconds, self.thirds = refs[0:6]
        if cores == 1:
            self.here = source
        self.sems = refs[6:12]

    @staticmethod
    def scratch(rows, cores=2):
        lines, batches, half, part, piece = three_levels(rows, cores)
        core = half if cores == 2 else 16
        shapes = ((core,), (part,), (piece,), (core,), (lines, part), (batches, piece))
        found = [pltpu.VMEM((*shape, C_OUT), bf16) for shape in shapes]
        for count in (1, lines, batches):
            found += [pltpu.SemaphoreType.DMA((count,))] * 2
        return found

    def copies(self, level):
        sent, got = self.sems[2 * level], self.sems[2 * level + 1]
        if level == 0:
            source = self.source.at[self.rows(1 - self.core, self.half)]
            return [remote(source, self.firsts, sent.at[0], got.at[0], self.core_peer())]
        if level == 1:
            return [
                remote(
                    self.here.at[self.rows(to, self.part)], self.seconds.at[self.line],
                    sent.at[d], got.at[d], device,
                )
                for d, to, device in self.line_peers()
            ]
        return [
            remote(
                self.up.at[self.rows(to, self.piece)], self.thirds.at[self.batch],
                sent.at[d], got.at[d], device,
            )
            for d, to, device in self.batch_peers()
        ]

    def start(self, level):
        for copy in self.copies(level):
            copy.start()

    def end(self, level):
        for copy in self.copies(level):
            copy.wait()
        if level == 0:
            own = self.source[self.rows(self.core, self.half), :].astype(f32)
            self.here[...] = (own + self.firsts[...].astype(f32)).astype(bf16)
        if level == 1:
            own = self.here[self.rows(self.line, self.part), :].astype(f32)
            for d in range(1, self.lines):
                own = own + self.seconds[lax.rem(self.line + d, self.lines)].astype(f32)
            self.up[...] = own.astype(bf16)
        if level == 2:
            own = self.up[self.rows(self.batch, self.piece), :].astype(f32)
            for d in range(1, self.batches):
                own = own + self.thirds[lax.rem(self.batch + d, self.batches)].astype(f32)
            self.out[...] = own.astype(bf16)


class Gather(Places):
    def __init__(self, rows, refs, cores=2):
        super().__init__(rows, cores)
        self.gathered, self.joined, self.full = refs[0:3]
        self.sems = refs[3:9]

    @staticmethod
    def scratch(rows, cores=2):
        lines, batches, half, part, piece = three_levels(rows, cores)
        shapes = ((batches, piece), (lines, part), (cores, half))
        found = [pltpu.VMEM((*shape, C_OUT), bf16) for shape in shapes]
        for count in (batches, lines, 1):
            found += [pltpu.SemaphoreType.DMA((count,))] * 2
        return found

    def copies(self, level):
        sent, got = self.sems[2 * level], self.sems[2 * level + 1]
        if level == 0:
            slot = self.gathered.at[self.batch]
            peers_here = self.batch_peers()
        elif level == 1:
            slot = self.joined.at[self.line]
            peers_here = self.line_peers()
        else:
            slot = self.full.at[self.core]
            return [remote(slot, slot, sent.at[0], got.at[0], self.core_peer())]
        return [remote(slot, slot, sent.at[d], got.at[d], device) for d, _, device in peers_here]

    def start(self, level, share=None):
        if level == 0:
            self.gathered[self.batch] = share
        if level == 1:
            self.joined[self.line] = self.gathered[...].reshape(self.part, C_OUT)
        if level == 2:
            self.full[self.core] = self.joined[...].reshape(self.half, C_OUT)
        for copy in self.copies(level):
            copy.start()

    def end(self, level):
        for copy in self.copies(level):
            copy.wait()


def conv_back(
    cg_ref, left_ref, right_ref, taps_ref, h_ref, m_ref, st_ref, norm_ref, xq_ref, kron_ref, own_ref,
    grad_ref,
    hg_ref, out_ref, sum_ref, gg_ref,
    fills, ext, sums, fg, kept, raw, xg, gg, *buffers,
):
    step = pl.program_id(0)
    pairs = pl.num_programs(0) // 2
    scatter = Scatter(grad_ref, buffers[6:])
    stats = st_ref[...]
    norm = norm_ref[...]
    mean, rstd, scale, shift = first_moments(stats, norm)

    @pl.when(step == 0)
    def _():
        greet()
        sums[...] = jnp.zeros_like(sums)
        gg[...] = jnp.zeros_like(gg)

    half_scale, half_shift = 0.5 * scale, 0.5 * shift

    def extend():
        kept[step] = h_ref[0]
        for q in range(2):
            for lane in range(2):
                at = slice(lane * HALF, (lane + 1) * HALF)
                fills[q, lane, pl.ds(7, UNITS, stride=GROUP), :] = left_ref[
                    0, q, 0:UNITS, at
                ].astype(f32)
                fills[q, lane, pl.ds(0, UNITS, stride=GROUP), :] = right_ref[
                    0, q, 0:UNITS, at
                ].astype(f32)
        for q in range(4):
            ext[q + 2] = cg_ref[0, q]
            for start in range(0, JOINTS, CUT):
                rows = slice(start * 2 * GROUP, (start + CUT) * 2 * GROUP)
                tiles = cg_ref[0, q, rows, :].astype(f32).reshape(-1, GROUP, C_OUT)
                fill = jnp.concatenate([fills[q % 2, lane, rows, :] for lane in range(2)], axis=1)
                fill = fill.reshape(-1, GROUP, C_OUT)
                moved = insert_and_roll(tiles, fill, 7 if q >= 2 else 0)
                at = q - 2 if q >= 2 else q + 6
                ext[at, rows, :] = moved.reshape(-1, C_OUT).astype(bf16)

    def convolve(c):
        p, q = c % 2, c // 2
        total = None
        for i in range(5 - p):
            part = dot_nt(ext[4 - i + q], taps_ref[2 * i + p])
            total = part if total is None else total + part
        raw[c] = total

    def activate_back(c):
        mask = 0.5 * m_ref[0, c]
        mask = jnp.concatenate([mask, mask], axis=1)[None]
        for start in range(0, JOINTS, CUT):
            rows = slice(start * 2 * GROUP, (start + CUT) * 2 * GROUP)
            hidden = kept[step - 1, c, rows, :].astype(f32)
            half = hidden * half_scale + half_shift
            turn = jnp.tanh(half)
            slope = (1.0 + turn) * (1.0 + (half - half * turn))
            slope = (slope.reshape(CUT, 2 * GROUP, C_OUT) * mask).reshape(-1, C_OUT)
            grad = raw[c, rows, :] * slope
            fg[step - 1, c, rows, :] = grad
            sums[0] += fold(grad)
            sums[1] += fold(grad * hidden)

    order = (0, 2, 4, 6, 1, 3, 5, 7)

    @pl.when(step == 0)
    def _():
        extend()
        for c in order:
            convolve(c)

    @pl.when((step > 0) & (step < pairs))
    def _():
        extend()
        for c in order:
            activate_back(c)
            convolve(c)

    @pl.when(step == pairs)
    def _():
        for c in order:
            activate_back(c)

    @pl.when(step > pairs)
    def _():
        pair = step - pairs - 1
        count_in = stats[4:5]
        back_sum = out_ref[0:1]
        back_norm = rstd * (out_ref[1:2] - mean * back_sum)
        lead = norm[0:1] * rstd
        slope = lead * rstd * back_norm / count_in
        offset = lead * back_sum / count_in - slope * mean
        for c in range(PHASES):
            mask = m_ref[0, c]
            shifts = jnp.concatenate([mask, mask], axis=1)[None] * offset
            for start in range(0, JOINTS, CUT):
                rows = slice(start * 2 * GROUP, (start + CUT) * 2 * GROUP)
                hidden = kept[pair, c, rows, :].astype(f32)
                taken = hidden.reshape(CUT, 2 * GROUP, C_OUT) * slope + shifts
                taken = taken.reshape(-1, C_OUT)
                hg_ref[0, c, rows, :] = (fg[pair, c, rows, :] * lead - taken).astype(bf16)
            seen = xq_ref[0, c, 0:HALF_ROWS, :].astype(f32).reshape(JOINTS, GROUP, 2 * C_IN)
            parts = [seen[:, :, side * C_IN : (side + 1) * C_IN] for side in range(2)]
            xg[c] = mix_rows(parts, own_ref[...], kron_ref, xq_ref.at[0, c])
        gg[...] += dot_tn(
            xg[...].reshape(PHASES * ROWS, SUBSETS * C_IN),
            hg_ref[0].reshape(PHASES * ROWS, C_OUT),
        )

    @pl.when(step == 0)
    def _():
        await_greetings()
        scatter.start(0)

    for level, at in ((0, 1), (1, pairs - 2)):

        @pl.when(step == at)
        def _(level=level):
            scatter.end(level)
            scatter.start(level + 1)

    @pl.when(step == pairs)
    def _():
        rows = [jnp.sum(sums[k], axis=0, keepdims=True) for k in range(2)]
        rows.append(jnp.zeros((6, C_OUT), f32))
        out_ref[...] = sum_all(jnp.concatenate(rows, axis=0), buffers[0:6])

    @pl.when(step == 2 * pairs)
    def _():
        gg_ref[0 : SUBSETS * C_IN, :] = gg[...].astype(bf16)
        rest = gg_ref.shape[0] - SUBSETS * C_IN
        if rest:
            gg_ref[SUBSETS * C_IN :, :] = jnp.zeros((rest, C_OUT), bf16)
        scatter.end(2)
        sum_ref[...] = scatter.out[...]


def graph_back(
    hg_ref, xq_ref, sg_ref, wgt_ref, wst_ref, kront_ref, own_ref, piece_ref, grad_ref,
    ig_ref, taps_sum_ref, sum_ref, edge_ref,
    spread, staged, eg, own_grad, *buffers,
):
    step = pl.program_id(0)
    pairs = pl.num_programs(0) // 2
    total = Total(buffers[0:6])
    gather_taps = Gather(taps_sum_ref.shape[0], buffers[6:15])
    scatter = Scatter(grad_ref, buffers[15:27], 1)
    gather = Gather(grad_ref.shape[0], buffers[27:36], 1)

    @pl.when(step == 0)
    def _():
        greet()
        eg[...] = jnp.zeros_like(eg)
        own_grad[...] = jnp.zeros_like(own_grad)

    def side_by_side(values):
        return jnp.concatenate([values[:, 0:GROUP], values[:, GROUP : 2 * GROUP]], axis=2)

    own = own_ref[...]
    own = jnp.concatenate([own, own], axis=2)

    def spread_out(first):
        rest = jnp.zeros((C_OUT - HALF_ROWS, C_OUT), f32)
        found = None
        owned = None
        for c in range(first, first + 4):
            if c % 2 == 0:
                pair_back = dot(hg_ref[0, c : c + 2].reshape(2 * ROWS, C_OUT), wgt_ref[...])
                pair_back = pair_back.reshape(2, JOINTS, 2 * GROUP, SUBSETS * C_IN)
            back = pair_back[c % 2]
            for k in range(SUBSETS):
                both = side_by_side(back[:, :, k * C_IN : (k + 1) * C_IN])
                if k == 0:
                    seen = xq_ref[0, c, 0:HALF_ROWS, :].astype(f32)
                    part = seen.reshape(JOINTS, GROUP, 2 * C_IN) * both
                    owned = part if owned is None else owned + part
                both = jnp.concatenate([both.reshape(HALF_ROWS, 2 * C_IN), rest], axis=0)
                spread[step, c, k] = both.astype(bf16)
        for c in range(first, first + 4):
            both = spread[step, c, 1:3].reshape(2 * C_OUT, C_OUT)
            part = dot_nt(both, xq_ref[0, c])
            found = part if found is None else found + part
        eg[...] += found
        own_grad[...] += owned

    def mix_back(first):
        pair = step - pairs
        for c in range(first, first + 4):
            mixed = dot(kront_ref[...], spread[pair, c, 1:3].reshape(2 * C_OUT, C_OUT))
            direct = spread[pair, c, 0, 0:HALF_ROWS, :].astype(f32)
            result = mixed.reshape(JOINTS, GROUP, 2 * C_IN)
            result = result + direct.reshape(JOINTS, GROUP, 2 * C_IN) * own
            if c % 4 == 0:
                short = dot(sg_ref[0, c // 2 : c // 2 + 2].reshape(2 * ROWS, C_OUT), wst_ref[...])
                short = short.reshape(2, JOINTS, 2 * GROUP, C_IN)
            if c % 2 == 0:
                result = result + side_by_side(short[c % 4 // 2])
            staged[c] = result

    def put_natural():
        for side in range(2):
            lanes = slice(side * C_IN, (side + 1) * C_IN)
            for start in range(0, JOINTS, CUT):
                rows = [staged[c, start : start + CUT, :, lanes] for c in range(PHASES)]
                rows = jnp.swapaxes(jnp.stack(rows, axis=1), 1, 2)
                rows = rows.reshape(CUT, GROUP * PHASES, C_IN)
                ig_ref[side, start : start + CUT] = rows.astype(bf16)

    def pack_edges():
        lines = lax.broadcasted_iota(jnp.int32, (C_OUT, C_OUT), 0)
        spots = lax.broadcasted_iota(jnp.int32, (C_OUT, C_OUT), 1)
        same = lines % GROUP == spots % GROUP
        row = lax.broadcasted_iota(jnp.int32, (32, C_OUT), 0)
        col = lax.broadcasted_iota(jnp.int32, (32, C_OUT), 1)
        down = (row == col // GROUP).astype(f32)
        sums = jnp.sum(own_grad[...], axis=1)
        sums = jnp.sum(sums, axis=1, keepdims=True)
        row = lax.broadcasted_iota(jnp.int32, (JOINTS, 128), 0)
        col = lax.broadcasted_iota(jnp.int32, (JOINTS, 128), 1)
        packed = jnp.where(row == col, jnp.broadcast_to(sums, (JOINTS, 128)), 0.0)
        packed = jnp.concatenate([packed, jnp.zeros((32 - JOINTS, 128), f32)], axis=0)
        row = lax.broadcasted_iota(jnp.int32, (C_OUT, 128), 0)
        col = lax.broadcasted_iota(jnp.int32, (C_OUT, 128), 1)
        for k in range(2):
            kept = jnp.where(same, eg[k * C_OUT : (k + 1) * C_OUT, :], 0.0)
            narrow = lax.dot_general(
                down, kept, (((1,), (1,)), ((), ())),
                preferred_element_type=f32, precision=lax.Precision.HIGHEST,
            )
            place = (row // GROUP + 32 * (k + 1) == col).astype(f32)
            packed = packed + jnp.dot(
                narrow, place, preferred_element_type=f32, precision=lax.Precision.HIGHEST
            )
        return packed

    def begin():
        await_greetings()
        scatter.start(1)
        gather_taps.start(0, piece_ref[...])

    def second():
        scatter.end(1)
        scatter.start(2)

    def taps_second():
        gather_taps.end(0)
        gather_taps.start(1)

    def third():
        scatter.end(2)
        gather.start(0, scatter.out[...])
        total.start(0, pack_edges())

    def fourth():
        total.start(1, total.end(0))

    def fifth():
        gather.end(0)
        gather.start(1)

    def taps_third():
        gather_taps.end(1)
        gather_taps.start(2)

    def finish():
        edge_ref[...] = total.end(1)
        gather_taps.end(2)
        taps_sum_ref[...] = gather_taps.full[...].reshape(taps_sum_ref.shape)
        gather.end(1)
        sum_ref[...] = gather.joined[...].reshape(sum_ref.shape)

    schedule = {
        (3, 1): second,
        (4, 0): taps_second,
        (pairs - 1, 1): third,
        (pairs + 1, 1): fourth,
        (pairs + 2, 1): fifth,
        (pairs + 3, 0): taps_third,
        (2 * pairs - 1, 1): finish,
    }

    def advance(half):
        for (at, part), act in schedule.items():
            if part == half:
                pl.when(step == at)(act)

    pl.when(step == 2)(begin)

    @pl.when(step < pairs)
    def _():
        spread_out(0)

    @pl.when(step >= pairs)
    def _():
        mix_back(0)

    advance(0)

    @pl.when(step < pairs)
    def _():
        spread_out(4)

    @pl.when(step >= pairs)
    def _():
        mix_back(4)
        put_natural()

    advance(1)


def update(
    grads_ref, graph_grad_ref, edge_grad_ref, gm_ref, st_ref, cs_ref, bk_ref, fs_ref, ig_ref, o_ref,
    *refs,
):
    groups = [refs[4 * k : 4 * k + 4] for k in range(5)]
    out_ig, out_o, out_norm = refs[20:23]
    outs = [refs[23 + 4 * k : 27 + 4 * k] for k in range(5)]
    squares, norm_grad = refs[43:45]
    step = pl.program_id(0)
    taps_rows = TAPS * C_OUT

    def edge_grad(k):
        values = edge_grad_ref[...]
        if k:
            values = pltpu.roll(values, 128 - 32 * k, 1)
        return values[0:JOINTS, 0:JOINTS] * gm_ref[k]

    def apply(group, out, at, gradient, rate, decay):
        factor = squares[0:1, 0:1]
        new = adam_update(*[ref[at] for ref in group], gradient, factor, rate, decay)
        for ref, value in zip(out, new):
            ref[at] = value

    @pl.when(step == 0)
    def _():
        stats = st_ref[...]
        norm = groups[4][0][...]
        mean, rstd, _, _ = first_moments(stats, norm)
        first_sum = fs_ref[0:1]
        first_norm = rstd * (fs_ref[1:2] - mean * first_sum)
        back_sum, back_conv, back_short = back_totals(
            bk_ref[...], second_moments(stats, cs_ref[...])
        )
        norm_grad[...] = jnp.concatenate(
            [first_norm, first_sum, back_conv, back_sum, back_short, back_sum], axis=0
        )
        total = jnp.zeros((GROUP, C_OUT), f32)
        for start in range(0, taps_rows + C_IN, C_IN):
            rows = grads_ref[start : start + C_IN, :].astype(f32)
            total = total + fold(rows * rows)
        for start in range(0, SUBSETS * C_IN, C_IN):
            rows = graph_grad_ref[start : start + C_IN, :].astype(f32)
            total = total + fold(rows * rows)
        whole = jnp.sum(total) + jnp.sum(norm_grad[...] * norm_grad[...])
        for k in range(SUBSETS):
            values = edge_grad(k)
            whole = whole + jnp.sum(values * values)
        size = jnp.sqrt(jnp.full((GROUP, 128), whole, f32))
        squares[...] = jnp.minimum(1.0, clip_limit / (size + 1e-06))
        out_norm[0] = jnp.max(size)
        every = (slice(None), slice(None))
        apply(groups[4], outs[4], every, norm_grad[...], rate_small, 0.0)
        for k in range(SUBSETS):
            apply(groups[3], outs[3], k, edge_grad(k), rate_small, 0.0)

    for k in range(3):
        row = (3 * (step // 2) + k) * C_OUT
        lane = (step % 2) * C_IN
        at = (pl.ds(pl.multiple_of(row, C_OUT), C_OUT), pl.ds(pl.multiple_of(lane, C_IN), C_IN))
        apply(groups[1], outs[1], k, grads_ref[at].T.astype(f32), rate_matrix, decay_matrix)
    rows = graph_grad_ref[pl.ds(pl.multiple_of(step * 64, 64), 64), :].astype(f32)
    every = (slice(None), slice(None))
    apply(groups[0], outs[0], every, rows, rate_matrix, decay_matrix)

    @pl.when(step == 0)
    def _():
        rows = grads_ref[taps_rows : taps_rows + C_IN, :].astype(f32)
        every = (slice(None), slice(None))
        apply(groups[2], outs[2], every, rows, rate_matrix, decay_matrix)

    out_ig[...] = ig_ref[...]
    out_o[...] = o_ref[...]


def whole_spec(shape):
    return pl.BlockSpec(shape, lambda i: (0,) * len(shape))


def lead_spec(shape):
    return pl.BlockSpec(shape, lambda i: (i,) + (0,) * (len(shape) - 1))


def spec(block, index):
    return pl.BlockSpec(block, index)


def by_step(block):
    return spec(block, lambda i: (i,) + (0,) * (len(block) - 1))


def call(body, steps, ins, outs, scratch, name, **more):
    def to_spec(where, shape):
        if where is None:
            return whole_spec(shape)
        return where if isinstance(where, pl.BlockSpec) else by_step(where)

    return pl.pallas_call(
        body,
        grid=(steps,),
        in_specs=[to_spec(where, array.shape) for array, where in ins],
        out_specs=[to_spec(where, shape) for shape, _, where in outs],
        out_shape=[jax.ShapeDtypeStruct(shape, kind) for shape, kind, _ in outs],
        scratch_shapes=scratch,
        compiler_params=params(**more),
        name=name,
    )(*[array for array, _ in ins])


def shards(
    inputs, cotangent, lengths, frame_mask, subsets,
    graph_weight, graph_moment, graph_square, graph_average,
    temporal_weight, temporal_moment, temporal_square, temporal_average,
    shortcut_weight, shortcut_moment, shortcut_square, shortcut_average,
    edge_weight, edge_moment, edge_square, edge_average,
    norm_params, norm_moment, norm_square, norm_average,
):
    clips = inputs.shape[0]
    frames = inputs.shape[1]
    pairs = clips // 2
    natural = jnp.transpose(inputs, (0, 2, 1, 3))
    cot = jnp.transpose(cotangent, (0, 2, 1, 3))

    x_block = (2, JOINTS, frames, C_IN)
    mask_block = (1, PHASES, 2 * GROUP, 128)
    wide_block = (1, PHASES, ROWS, C_OUT)
    out_block = (1, 4, ROWS, C_OUT)
    xe_block = (1, 4, ROWS, C_IN)
    a_block = (1, 2, 8, ROWS, C_OUT)
    rim_block = (1, 2, 64, C_OUT)
    xq_block = (1, PHASES, C_OUT, C_OUT)
    cot_block = (2, JOINTS, frames // 2, C_OUT)
    edge_block = (1, JOINTS, 2 * GROUP, C_IN)
    end_block = (clips, JOINTS, 2 * GROUP, C_IN)
    small = (8, C_OUT)
    dma = pltpu.SemaphoreType.DMA

    def full(block):
        return (pairs,) + block[1:]

    def by_pair(block, pair):
        return spec(block, lambda i: (jnp.clip(pair(i), 0, pairs - 1),) + (0,) * (len(block) - 1))

    def early(block):
        return by_pair(block, lambda i: i)

    def behind(block):
        return by_pair(block, lambda i: i - 1)

    def late(block):
        return by_pair(block, lambda i: i - pairs)

    def later(block):
        return by_pair(block, lambda i: i - pairs - 1)

    vmem = pl.BlockSpec(memory_space=pltpu.VMEM)
    shapes = [
        ((clips * frames, 128), f32),
        ((clips * GROUP, 128), f32),
        ((2 * HALF_ROWS, C_OUT), bf16),
        ((HALF_ROWS, 2 * C_OUT), bf16),
        ((JOINTS, GROUP, C_IN), f32),
        ((SUBSETS, JOINTS, JOINTS), f32),
        ((SUBSETS * C_IN, C_OUT), bf16),
        ((C_OUT, SUBSETS * C_IN), bf16),
        ((C_IN, C_OUT), bf16),
        ((C_OUT, C_IN), bf16),
        ((TAPS, C_OUT, C_OUT), bf16),
    ]
    masks, edge_masks, kron, kront, own, graph_mask, wg, wgt, ws, wst, taps = pl.pallas_call(
        prepare,
        in_specs=[pl.BlockSpec(memory_space=pltpu.SMEM)] + [vmem] * 6,
        out_specs=[vmem] * 11,
        out_shape=[jax.ShapeDtypeStruct(shape, kind) for shape, kind in shapes],
        compiler_params=pltpu.CompilerParams(vmem_limit_bytes=60 * 2**20),
        name="prepare",
    )(lengths, frame_mask, subsets, edge_weight, graph_weight, shortcut_weight, temporal_weight)
    masks = masks.reshape(pairs, PHASES, 2 * GROUP, 128)

    xq, xe, hidden, stats, rims, rim_mask = call(
        graph_forward,
        pairs + 1,
        [
            (natural, early(x_block)),
            (natural, pl.BlockSpec(memory_space=pl.ANY)),
            (masks, early(mask_block)),
            (edge_masks, None),
            (kron, None),
            (own, None),
            (wg, None),
            (ws, None),
        ],
        [
            (full(xq_block), bf16, early(xq_block)),
            (full(xe_block), bf16, early(xe_block)),
            (full(wide_block), bf16, behind(wide_block)),
            (small, f32, None),
            (full(edge_block), bf16, None),
            (edge_masks.shape, f32, None),
        ],
        [
            pltpu.VMEM((PHASES, 2, JOINTS, GROUP, C_IN), f32),
            pltpu.VMEM((PHASES, ROWS, SUBSETS * C_IN), bf16),
            pltpu.VMEM((4, ROWS, C_IN), bf16),
            pltpu.VMEM(end_block, bf16),
            pltpu.VMEM(end_block, bf16),
            dma((2,)),
            pltpu.VMEM((4, GROUP, C_OUT), f32),
            pltpu.VMEM((2, 2 * GROUP, 128), f32),
            pltpu.VMEM(full(edge_block), bf16),
            pltpu.VMEM(full(edge_block), bf16),
            pltpu.VMEM(full(edge_block), bf16),
            pltpu.VMEM(edge_masks.shape, f32),
            pltpu.VMEM(edge_masks.shape, f32),
        ]
        + [dma((2,))] * 4
        + sum_scratch(),
        "graph_forward",
        collective_id=1,
        has_side_effects=True,
    )

    active, conv, conv_stats = call(
        conv_forward,
        pairs,
        [
            (hidden, wide_block),
            (rims, edge_block),
            (masks, mask_block),
            (rim_mask, (2 * GROUP, 128)),
            (stats, None),
            (norm_params, None),
            (kron, None),
            (own, None),
            (wg, None),
            (taps, None),
        ],
        [
            (full(a_block), bf16, a_block),
            (full(out_block), f32, out_block),
            (small, f32, None),
        ],
        [
            pltpu.VMEM((C_OUT, C_OUT), bf16),
            pltpu.VMEM((2, ROWS, HALF), f32),
            pltpu.VMEM((4, 2, ROWS, HALF), f32),
            pltpu.VMEM((2, GROUP, C_OUT), f32),
        ]
        + sum_scratch(),
        "conv_forward",
        collective_id=2,
        has_side_effects=True,
    )

    def both_ways(block):
        return by_pair(block, lambda i: jnp.where(i < pairs, i, i - pairs))

    grad_rows = padded(TAPS * C_OUT + C_IN)
    outputs, conv_grad, short_grad, left_rim, right_rim, grads, back = call(
        middle,
        2 * pairs + 1,
        [
            (conv, early(out_block)),
            (xe, both_ways(xe_block)),
            (cot, early(cot_block)),
            (active, later(a_block)),
            (masks, both_ways(mask_block)),
            (stats, None),
            (conv_stats, None),
            (norm_params, None),
            (ws, None),
        ],
        [
            (cot.shape, bf16, early(cot_block)),
            (full(out_block), bf16, late(out_block)),
            (full(out_block), bf16, late(out_block)),
            (full(rim_block), bf16, None),
            (full(rim_block), bf16, None),
            ((grad_rows, C_OUT), bf16, None),
            (small, f32, None),
        ],
        [
            pltpu.VMEM((2, 2, JOINTS, frames // 2, HALF), f32),
            pltpu.VMEM((2, 2, JOINTS, frames // 2, HALF), f32),
            pltpu.VMEM((3, GROUP, C_OUT), f32),
            pltpu.VMEM(full(out_block), f32),
            pltpu.VMEM(full(out_block), f32),
            pltpu.VMEM((C_OUT, DEPTH), bf16),
            pltpu.VMEM((2, ROWS, HALF), f32),
            pltpu.VMEM((TAPS, C_OUT, C_OUT), f32),
            pltpu.VMEM((C_IN, C_OUT), f32),
        ]
        + [pltpu.VMEM(full(rim_block), bf16)] * 4
        + [dma((pairs,))] * 4
        + sum_scratch(),
        "middle",
        collective_id=3,
        has_side_effects=True,
    )

    graph_rows = padded(SUBSETS * C_IN)
    hidden_grad, first_sums, grad_piece, graph_grad = call(
        conv_back,
        2 * pairs + 1,
        [
            (conv_grad, early(out_block)),
            (left_rim, early(rim_block)),
            (right_rim, early(rim_block)),
            (taps, None),
            (hidden, early(wide_block)),
            (masks, by_pair(mask_block, lambda i: jnp.where(i <= pairs, i - 1, i - pairs - 1))),
            (stats, None),
            (norm_params, None),
            (xq, later(xq_block)),
            (kron, None),
            (own, None),
            (grads, None),
        ],
        [
            (full(wide_block), bf16, later(wide_block)),
            (small, f32, None),
            ((grad_rows // lax.axis_size(("tm", "batch")), C_OUT), bf16, None),
            ((graph_rows, C_OUT), bf16, None),
        ],
        [
            pltpu.VMEM((2, 2, ROWS, HALF), f32),
            pltpu.VMEM((8, ROWS, C_OUT), bf16),
            pltpu.VMEM((2, GROUP, C_OUT), f32),
            pltpu.VMEM(full(wide_block), f32),
            pltpu.VMEM(full(wide_block), bf16),
            pltpu.VMEM((PHASES, ROWS, C_OUT), f32),
            pltpu.VMEM((PHASES, ROWS, SUBSETS * C_IN), bf16),
            pltpu.VMEM((SUBSETS * C_IN, C_OUT), f32),
        ]
        + sum_scratch()
        + Scatter.scratch(grad_rows),
        "conv_back",
        collective_id=4,
        has_side_effects=True,
    )

    input_grad, grad_sums, graph_sum, edge_sum = call(
        graph_back,
        2 * pairs,
        [
            (hidden_grad, early(wide_block)),
            (xq, early(xq_block)),
            (short_grad, late(out_block)),
            (wgt, None),
            (wst, None),
            (kront, None),
            (own, None),
            (grad_piece, None),
            (graph_grad, None),
        ],
        [
            (natural.shape, bf16, late(x_block)),
            ((grad_rows, C_OUT), bf16, None),
            ((graph_rows, C_OUT), bf16, None),
            ((32, 128), f32, None),
        ],
        [
            pltpu.VMEM((pairs, PHASES, SUBSETS, C_OUT, C_OUT), bf16),
            pltpu.VMEM((PHASES, JOINTS, GROUP, 2 * C_IN), f32),
            pltpu.VMEM((2 * C_OUT, C_OUT), f32),
            pltpu.VMEM((JOINTS, GROUP, 2 * C_IN), f32),
        ]
        + sum_scratch((32, 128))
        + Gather.scratch(grad_rows)
        + Scatter.scratch(graph_rows, 1)
        + Gather.scratch(graph_rows, 1),
        "graph_back",
        collective_id=5,
        has_side_effects=True,
    )

    tap_spec = spec((TAPS // 3, C_IN, C_OUT), lambda i: (i // 2, i % 2, 0))
    graph_spec = spec((64, C_OUT), lambda i: (i % 2, i // 2))
    states = [
        (graph_weight, graph_moment, graph_square, graph_average),
        (temporal_weight, temporal_moment, temporal_square, temporal_average),
        (shortcut_weight, shortcut_moment, shortcut_square, shortcut_average),
        (edge_weight, edge_moment, edge_square, edge_average),
        (norm_params, norm_moment, norm_square, norm_average),
    ]
    places = [graph_spec, tap_spec, None, None, None]
    state_ins = [(array, place) for group, place in zip(states, places) for array in group]
    clip_spec = spec((clips // 6, JOINTS, frames, C_IN), lambda i: (i, 0, 0, 0))
    out_spec = spec((clips // 6, JOINTS, frames // 2, C_OUT), lambda i: (i, 0, 0, 0))
    new = call(
        update,
        6,
        [
            (grad_sums, None),
            (graph_sum, None),
            (edge_sum, None),
            (graph_mask, None),
            (stats, None),
            (conv_stats, None),
            (back, None),
            (first_sums, None),
            (input_grad, clip_spec),
            (outputs, out_spec),
        ]
        + state_ins,
        [(natural.shape, bf16, clip_spec), (cot.shape, bf16, out_spec), ((1,), f32, pl.BlockSpec(memory_space=pltpu.SMEM))]
        + [(array.shape, f32, place) for array, place in state_ins],
        [pltpu.VMEM((GROUP, 128), f32), pltpu.VMEM((6, C_OUT), f32)],
        "update",
    )
    return (
        jnp.transpose(new[1], (0, 2, 1, 3)),
        jnp.transpose(new[0], (0, 2, 1, 3)),
        new[2],
        *new[3:],
    )


def solution(mesh):
    rows = P("batch", "tm", None, None)
    in_specs = (rows, rows, P("batch"), P("batch", "tm")) + (P(),) * 21
    out_specs = (rows, rows) + (P(),) * 21
    return jax.shard_map(shards, mesh=mesh, in_specs=in_specs, out_specs=out_specs, check_vma=False)
```

```python
import functools

import jax
import jax.numpy as jnp
from jax import lax
from jax.experimental import pallas as pl
from jax.experimental.pallas import tpu as pltpu
from jax.sharding import PartitionSpec as P

C_IN = 128
C_OUT = 256
JOINTS = 25
SUBSETS = 3
TAPS = 9
GROUP = 8
PHASES = 8
UNITS = 2 * JOINTS
ROWS = UNITS * GROUP
HALF_ROWS = JOINTS * GROUP
HALF = C_IN
CUT = 5
DEPTH = 4 * ROWS + 64

f32 = jnp.float32
bf16 = jnp.bfloat16

norm_epsilon = 1e-05
beta_first = 0.9
beta_second = 0.999
adam_epsilon = 1e-08
clip_limit = 1.0
average_decay = 0.9
rate_matrix = 0.05
rate_small = 0.3
decay_matrix = 0.01
steps_taken = 3.0


def params(**more):
    return pltpu.CompilerParams(
        vmem_limit_bytes=60 * 2**20, dimension_semantics=("arbitrary",), **more
    )


def adjacency(subsets):
    linked = (subsets > 0).astype(f32)
    degree = jnp.sum(linked, axis=0)
    labels = jnp.arange(SUBSETS, dtype=jnp.int32) + 1
    chosen = (subsets[None, :, :] == labels[:, None, None]).astype(f32)
    return chosen / degree[None, None, :]


def adam_update(weight, moment, square, average, gradient, factor, rate, decay):
    fix_first = 1.0 - beta_first**steps_taken
    fix_second = 1.0 - beta_second**steps_taken
    clipped = gradient * factor
    moment_new = beta_first * moment + (1.0 - beta_first) * clipped
    square_new = beta_second * square + (1.0 - beta_second) * clipped * clipped
    scaled = square_new * (1.0 / fix_second)
    below = scaled * lax.rsqrt(scaled) + adam_epsilon
    guess = pl.reciprocal(below, approx=True)
    guess = guess * (2.0 - below * guess)
    stepped = moment_new * (1.0 / fix_first) * guess
    weight_new = weight - rate * (stepped + decay * weight)
    average_new = average_decay * average + (1.0 - average_decay) * weight_new
    return (weight_new, moment_new, square_new, average_new)


def dot(a, b):
    return jnp.dot(a, b, preferred_element_type=f32)


def dot_nt(a, b):
    return lax.dot_general(a, b, (((1,), (1,)), ((), ())), preferred_element_type=f32)


def dot_tn(a, b):
    return lax.dot_general(a, b, (((0,), (0,)), ((), ())), preferred_element_type=f32)


def fold(values):
    return jnp.sum(values.reshape(-1, GROUP, values.shape[-1]), axis=0)


MESH = pl.DeviceIdType.MESH


def peers(axis):
    count = lax.axis_size(axis)
    here = lax.axis_index(axis)
    return [(d, {axis: lax.rem(here + d, count)}) for d in range(1, count)]


def greet():
    barrier = pltpu.get_barrier_semaphore()
    for axis in ("tm", "batch"):
        for _, device in peers(axis):
            pl.semaphore_signal(barrier, inc=1, device_id=device, device_id_type=MESH)


def await_greetings():
    count = lax.axis_size("tm") + lax.axis_size("batch") - 2
    pl.semaphore_wait(pltpu.get_barrier_semaphore(), count)


class Total:
    def __init__(self, buffers):
        self.levels = list(zip(("tm", "batch"), (buffers[0:3], buffers[3:6])))

    def copies(self, level):
        axis, (slots, sent, received) = self.levels[level]
        here = lax.axis_index(axis)
        return [
            remote(slots.at[here], slots.at[here], sent.at[d], received.at[d], device)
            for d, device in peers(axis)
        ]

    def start(self, level, values):
        axis, (slots, _, _) = self.levels[level]
        slots[lax.axis_index(axis)] = values
        for copy in self.copies(level):
            copy.start()

    def end(self, level):
        axis, (slots, _, _) = self.levels[level]
        for copy in self.copies(level):
            copy.wait()
        values = slots[0]
        for k in range(1, lax.axis_size(axis)):
            values = values + slots[k]
        return values


def sum_all(values, buffers):
    total = Total(buffers)
    total.start(0, values)
    total.start(1, total.end(0))
    return total.end(1)


def sum_scratch(shape=(8, C_OUT)):
    found = []
    for axis in ("tm", "batch"):
        count = lax.axis_size(axis)
        found += [
            pltpu.VMEM((count, *shape), f32),
            pltpu.SemaphoreType.DMA((count,)),
            pltpu.SemaphoreType.DMA((count,)),
        ]
    return found


def remote(source, target, sent, received, device):
    return pltpu.make_async_remote_copy(
        src_ref=source,
        dst_ref=target,
        send_sem=sent,
        recv_sem=received,
        device_id=device,
        device_id_type=MESH,
    )


def with_neighbours(step, low, high, from_left, from_right, sems, act):
    here = lax.axis_index("tm")
    last = lax.axis_size("tm") - 1
    sent_right, got_left, sent_left, got_right = sems

    def rightward():
        return remote(high, from_left, sent_right.at[step], got_left.at[step], {"tm": here + 1})

    def leftward():
        return remote(low, from_right, sent_left.at[step], got_right.at[step], {"tm": here - 1})

    if act == "start":

        @pl.when(here < last)
        def _():
            rightward().start()

        @pl.when(here > 0)
        def _():
            leftward().start()

    else:

        @pl.when(here < last)
        def _():
            rightward().wait_send()
            leftward().wait_recv()

        @pl.when(here > 0)
        def _():
            leftward().wait_send()
            rightward().wait_recv()


def first_moments(stats, norm):
    count_in = stats[4:5]
    mean = stats[0:1] / count_in
    rstd = lax.rsqrt(stats[1:2] / count_in - mean * mean + norm_epsilon)
    return mean, rstd, norm[0:1] * rstd, norm[1:2] - norm[0:1] * rstd * mean


def one_hot_rows(rows, columns):
    row = lax.broadcasted_iota(jnp.int32, (rows, columns), 0)
    col = lax.broadcasted_iota(jnp.int32, (rows, columns), 1)
    return (row // GROUP == col).astype(bf16)


def prepare(
    length_ref, frame_ref, subset_ref, edge_ref, graph_ref, short_ref, taps_ref,
    m_ref, em_ref, kron_ref, kront_ref, own_ref, gm_ref, wg_ref, wgt_ref, ws_ref, wst_ref, low_ref,
):
    low_ref[...] = taps_ref[...].astype(bf16)

    @pl.when(pl.program_id(0) == 0)
    def _():
        clips, frames = frame_ref.shape
        first = lax.axis_index("tm") * frames
        row = lax.broadcasted_iota(jnp.int32, (clips, frames), 0)
        ids = lax.broadcasted_iota(jnp.int32, (clips, frames), 1) + first
        ends = jnp.zeros((clips, frames), jnp.int32)
        for clip in range(clips):
            ends = jnp.where(row == clip, length_ref[clip], ends)
        mask = ((ids < ends) & (frame_ref[...] > 0)).astype(bf16)
        every = jnp.ones((frames, 128), bf16)

        def spread(rows, clip_of, frame_of):
            at = lax.broadcasted_iota(jnp.int32, (rows, clips), 0)
            chosen = (clip_of(at) == lax.broadcasted_iota(jnp.int32, (rows, clips), 1)).astype(bf16)
            lines = dot(chosen, mask)
            at = lax.broadcasted_iota(jnp.int32, (rows, frames), 0)
            kept = frame_of(at) == lax.broadcasted_iota(jnp.int32, (rows, frames), 1)
            return dot(jnp.where(kept, lines, 0.0).astype(bf16), every)

        side = 2 * GROUP
        m_ref[...] = spread(
            clips * frames,
            lambda at: 2 * (at // (PHASES * side)) + at // GROUP % 2,
            lambda at: PHASES * (at % GROUP) + at // side % PHASES,
        )
        em_ref[...] = spread(
            clips * GROUP, lambda at: at // GROUP, lambda at: (at % GROUP + frames - 4) % frames
        )
        subsets = subset_ref[...]
        degree = jnp.sum((subsets > 0).astype(f32), axis=0, keepdims=True)
        lift = one_hot_rows(HALF_ROWS, JOINTS)
        row = lax.broadcasted_iota(jnp.int32, (JOINTS, C_OUT), 0)
        drop = (row == lax.broadcasted_iota(jnp.int32, (JOINTS, C_OUT), 1) // GROUP).astype(bf16)
        row = lax.broadcasted_iota(jnp.int32, (HALF_ROWS, C_OUT), 0)
        same = row % GROUP == lax.broadcasted_iota(jnp.int32, (HALF_ROWS, C_OUT), 1) % GROUP
        for k in range(SUBSETS):
            share = (subsets == k + 1).astype(f32) / degree
            gm_ref[k] = share
            low = (share * edge_ref[k]).astype(bf16)
            if k == 0:
                row = lax.broadcasted_iota(jnp.int32, (JOINTS, JOINTS), 0)
                col = lax.broadcasted_iota(jnp.int32, (JOINTS, JOINTS), 1)
                diagonal = jnp.sum(jnp.where(row == col, low.astype(f32), 0.0), axis=1, keepdims=True)
                wide = jnp.broadcast_to(diagonal, (JOINTS, C_IN)).astype(bf16)
                own_ref[...] = dot(lift, wide).reshape(JOINTS, GROUP, C_IN)
            else:
                ahead = dot(lift, dot_tn(low, drop).astype(bf16))
                rows = slice((k - 1) * HALF_ROWS, k * HALF_ROWS)
                kron_ref[rows, :] = jnp.where(same, ahead, 0.0).astype(bf16)
                behind = dot(lift, dot(low, drop).astype(bf16))
                lanes = slice((k - 1) * C_OUT, k * C_OUT)
                kront_ref[:, lanes] = jnp.where(same, behind, 0.0).astype(bf16)
            block = graph_ref[:, k * C_OUT : (k + 1) * C_OUT]
            wg_ref[k * C_IN : (k + 1) * C_IN, :] = block.astype(bf16)
            wgt_ref[:, k * C_IN : (k + 1) * C_IN] = block.T.astype(bf16)
        ws_ref[...] = short_ref[...].astype(bf16)
        wst_ref[...] = short_ref[...].T.astype(bf16)


def mix_rows(parts, scales, kron_ref, wide_ref):
    mixed = dot(kron_ref[...], wide_ref[...])
    sides = []
    for side in range(2):
        lanes = slice(side * HALF, (side + 1) * HALF)
        sides.append(
            jnp.concatenate(
                [
                    parts[side] * scales,
                    mixed[0:HALF_ROWS, lanes].reshape(JOINTS, GROUP, C_IN),
                    mixed[HALF_ROWS : 2 * HALF_ROWS, lanes].reshape(JOINTS, GROUP, C_IN),
                ],
                axis=2,
            )
        )
    return jnp.concatenate(sides, axis=1).reshape(ROWS, SUBSETS * C_IN).astype(bf16)


def put_wide(parts, wide_ref):
    wide = jnp.concatenate([part.reshape(HALF_ROWS, C_IN) for part in parts], axis=1)
    wide_ref[0:HALF_ROWS, :] = wide.astype(bf16)


def graph_forward(
    x_ref, all_ref, m_ref, em_ref, kron_ref, own_ref, wg_ref, ws_ref,
    xq_ref, xe_ref, h_ref, st_ref, rim_ref, rim_mask_ref,
    xs, xg, xe, head, tail, end_sems, sums, counts, mine, lefts, rights, mask_lefts, mask_rights,
    sent_right, got_left, sent_left, got_right, *sum_buffers,
):
    step = pl.program_id(0)
    last = pl.num_programs(0) - 1
    sems = (sent_right, got_left, sent_left, got_right)

    def rims(act):
        with_neighbours(0, mine, mine, lefts, rights, sems, act)
        with_neighbours(1, em_ref, em_ref, mask_lefts, mask_rights, sems, act)

    depth = head.shape[2]
    end_copies = [
        pltpu.make_async_copy(all_ref.at[:, :, 0:depth], head, end_sems.at[0]),
        pltpu.make_async_copy(
            all_ref.at[:, :, all_ref.shape[2] - depth : all_ref.shape[2]], tail, end_sems.at[1]
        ),
    ]

    @pl.when(step == 0)
    def _():
        for ref in (lefts, rights, mask_lefts, mask_rights):
            ref[...] = jnp.zeros_like(ref)
        greet()
        for copy in end_copies:
            copy.start()
        sums[...] = jnp.zeros_like(sums)
        counts[...] = jnp.zeros_like(counts)

    def permute():
        for side in range(2):
            for start in range(0, JOINTS, CUT):
                rows = x_ref[side, start : start + CUT].astype(f32)
                rows = jnp.swapaxes(rows.reshape(CUT, GROUP, PHASES, C_IN), 1, 2)
                for c in range(PHASES):
                    mask = m_ref[0, c, side * GROUP : (side + 1) * GROUP]
                    xs[c, side, start : start + CUT] = rows[:, c] * mask[None]

    def mix(c):
        xq_ref[0, c, HALF_ROWS:, :] = jnp.zeros((C_OUT - HALF_ROWS, C_OUT), bf16)
        parts = [xs[c, 0], xs[c, 1]]
        put_wide(parts, xq_ref.at[0, c])
        xg[c] = mix_rows(parts, own_ref[...], kron_ref, xq_ref.at[0, c])
        counts[0] += m_ref[0, c]
        if c % 2 == 0:
            counts[1] += m_ref[0, c]
            even = jnp.concatenate(parts, axis=1).reshape(ROWS, C_IN).astype(bf16)
            xe_ref[0, c // 2] = even
            xe[c // 2] = even

    def project(c):
        hidden = dot(xg[c : c + 2].reshape(2 * ROWS, SUBSETS * C_IN), wg_ref[...])
        h_ref[0, c : c + 2] = hidden.reshape(2, ROWS, C_OUT).astype(bf16)
        sums[0] += fold(hidden)
        sums[1] += fold(hidden * hidden)
        short = dot(xe[c // 2], ws_ref[...])
        sums[2] += fold(short)
        sums[3] += fold(short * short)

    @pl.when(step == 0)
    def _():
        permute()
        for c in range(PHASES):
            mix(c)

    @pl.when((step > 0) & (step < last))
    def _():
        permute()
        for c in range(0, PHASES, 2):
            project(c)
            mix(c)
            mix(c + 1)

    @pl.when(step == last)
    def _():
        for c in range(0, PHASES, 2):
            project(c)

    @pl.when(step == 1)
    def _():
        for copy in end_copies:
            copy.wait()
        for pair in range(mine.shape[0]):
            ends = []
            for clip in (2 * pair, 2 * pair + 1):
                above = pltpu.roll(tail[clip].astype(f32)[:, GROUP:], 4, 1)
                below = pltpu.roll(head[clip].astype(f32)[:, :GROUP], 4, 1)
                sub = lax.broadcasted_iota(jnp.int32, above.shape, 1)
                ends.append(jnp.where(sub < 4, above, below))
            mine[pair] = jnp.concatenate(ends, axis=1).astype(bf16)
        await_greetings()
        rims("start")

    @pl.when(step == last)
    def _():
        rows = [jnp.sum(sums[k], axis=0, keepdims=True) for k in range(4)]
        for k in range(2):
            total = JOINTS * jnp.sum(counts[k], axis=0, keepdims=True)
            rows.append(jnp.concatenate([total, total], axis=1))
        rows.append(jnp.zeros((2, C_OUT), f32))
        total = Total(sum_buffers)
        total.start(0, jnp.concatenate(rows, axis=0))
        rims("wait")
        sub = lax.broadcasted_iota(jnp.int32, mask_lefts.shape, 0) % GROUP
        rim_mask_ref[...] = jnp.where(sub < 4, mask_lefts[...], mask_rights[...])
        total.start(1, total.end(0))
        for pair in range(lefts.shape[0]):
            sub = lax.broadcasted_iota(jnp.int32, lefts.shape[1:], 1) % GROUP
            both = jnp.where(sub < 4, lefts[pair].astype(f32), rights[pair].astype(f32))
            rim_ref[pair] = both.astype(bf16)
        st_ref[...] = total.end(1)


def insert_and_roll(tiles, fill, side):
    sub = lax.broadcasted_iota(jnp.int32, tiles.shape, 1)
    joined = jnp.where(sub == side, fill, tiles)
    return pltpu.roll(joined, 1 if side == 7 else GROUP - 1, 1)


def conv_forward(
    h_ref, xh_ref, m_ref, mh_ref, st_ref, norm_ref, kron_ref, own_ref, wg_ref, taps_ref,
    a_ref, conv_ref, out_ref,
    pad, rims, fills, sums, *sum_buffers,
):
    step = pl.program_id(0)

    @pl.when(step == 0)
    def _():
        greet()
        sums[...] = jnp.zeros_like(sums)
        pad[...] = jnp.zeros_like(pad)

    _, _, scale, shift = first_moments(st_ref[...], norm_ref[...])
    scale, shift = 0.5 * scale, 0.5 * shift

    def activate(values, offset):
        half = values.reshape(-1, 2 * GROUP, C_OUT) * scale + offset
        return half + half * jnp.tanh(half)

    def wide(mask):
        return jnp.concatenate([mask, mask], axis=1)[None]

    rim_mask = mh_ref[...]
    rim_rows = xh_ref[0].astype(f32) * rim_mask[None]
    parts = [rim_rows[:, side * GROUP : (side + 1) * GROUP] for side in range(2)]
    put_wide(parts, pad)
    rim_hidden = dot(mix_rows(parts, own_ref[...], kron_ref, pad), wg_ref[...])
    rim_active = activate(rim_hidden, wide(rim_mask) * shift).reshape(ROWS, C_OUT)
    for lane in range(2):
        rims[lane] = rim_active[:, lane * HALF : (lane + 1) * HALF]
    for p in range(2):
        for q in range(2):
            for lane in range(2):
                fills[2 * p + q, lane, pl.ds(7, UNITS, stride=GROUP), :] = rims[
                    lane, pl.ds(2 * q + p, UNITS, stride=GROUP), :
                ]
                fills[2 * p + q, lane, pl.ds(0, UNITS, stride=GROUP), :] = rims[
                    lane, pl.ds(4 + 2 * q + p, UNITS, stride=GROUP), :
                ]

    a_ref[0, 1, 7, 0:64, :] = jnp.zeros((64, C_OUT), bf16)
    for c in range(PHASES):
        p, q = c % 2, c // 2
        offset = wide(m_ref[0, c]) * shift
        for start in range(0, JOINTS, CUT):
            rows = slice(start * 2 * GROUP, (start + CUT) * 2 * GROUP)
            active = activate(h_ref[0, c, rows, :].astype(f32), offset)
            a_ref[0, p, q + 2, rows, :] = active.reshape(-1, C_OUT).astype(bf16)
            if p == 1 and q == 1:
                continue
            tiles = active.reshape(-1, GROUP, C_OUT)
            fill = jnp.concatenate(
                [fills[2 * p + q % 2, lane, rows, :] for lane in range(2)], axis=1
            ).reshape(-1, GROUP, C_OUT)
            moved = insert_and_roll(tiles, fill, 7 if q >= 2 else 0)
            at = q - 2 if q >= 2 else q + 6
            a_ref[0, p, at, rows, :] = moved.reshape(-1, C_OUT).astype(bf16)

    total = None
    for j in range(TAPS):
        window = a_ref[0, j % 2, j // 2 : j // 2 + 4].reshape(4 * ROWS, C_OUT)
        part = dot(window, taps_ref[j])
        total = part if total is None else total + part
    for q in range(4):
        block = total[q * ROWS : (q + 1) * ROWS].reshape(JOINTS, 2 * GROUP, C_OUT)
        live = block * wide(m_ref[0, 2 * q])
        conv_ref[0, q] = live.reshape(ROWS, C_OUT)
        sums[0] += fold(live)
        sums[1] += fold(live * live)

    @pl.when(step == pl.num_programs(0) - 1)
    def _():
        await_greetings()
        rows = [jnp.sum(sums[k], axis=0, keepdims=True) for k in range(2)]
        rows.append(jnp.zeros((6, C_OUT), f32))
        out_ref[...] = sum_all(jnp.concatenate(rows, axis=0), sum_buffers)


def second_moments(stats, conv_stats):
    count_out = stats[5:6]
    mean_conv = conv_stats[0:1] / count_out
    rstd_conv = lax.rsqrt(conv_stats[1:2] / count_out - mean_conv * mean_conv + norm_epsilon)
    mean_short = stats[2:3] / count_out
    rstd_short = lax.rsqrt(stats[3:4] / count_out - mean_short * mean_short + norm_epsilon)
    return mean_conv, rstd_conv, mean_short, rstd_short


def back_totals(back, moments):
    mean_conv, rstd_conv, mean_short, rstd_short = moments
    back_sum = back[0:1]
    back_conv = rstd_conv * (back[1:2] - mean_conv * back_sum)
    back_short = rstd_short * (back[2:3] - mean_short * back_sum)
    return back_sum, back_conv, back_short


def middle(
    conv_ref, xe_ref, cot_ref, a_ref, m_ref, st_ref, cs_ref, norm_ref, ws_ref,
    o_ref, cg_ref, sg_ref, left_ref, right_ref, grad_ref, total_ref,
    cots, outs, sums, conv_kept, up_kept, turned, edges, tg, shg, low_rims, high_rims, lefts, rights,
    sent_right, got_left, sent_left, got_right, *sum_buffers,
):
    step = pl.program_id(0)
    pairs = low_rims.shape[0]
    sems = (sent_right, got_left, sent_left, got_right)

    def rims(at, act):
        with_neighbours(
            at, low_rims.at[at], high_rims.at[at], lefts.at[at], rights.at[at], sems, act
        )

    norm = norm_ref[...]
    stats = st_ref[...]
    moments = second_moments(stats, cs_ref[...])
    mean_conv, rstd_conv, mean_short, rstd_short = moments

    @pl.when(step == 0)
    def _():
        for ref in (sums, lefts, rights, tg, shg, turned, low_rims, high_rims):
            ref[...] = jnp.zeros_like(ref)
        greet()

    @pl.when(step < pairs)
    def _():
        scale_conv = 0.5 * norm[2:3] * rstd_conv
        scale_short = 0.5 * norm[4:5] * rstd_short
        shift = 0.5 * (norm[3:4] + norm[5:6]) - scale_conv * mean_conv - scale_short * mean_short
        for side in range(2):
            for joint in range(JOINTS):
                for lane in range(2):
                    cots[side, lane, joint] = cot_ref[
                        side, joint, :, lane * HALF : (lane + 1) * HALF
                    ].astype(f32)
        for q in range(4):
            mask = m_ref[0, 2 * q]
            mask = jnp.concatenate([mask, mask], axis=1)[None]
            short_all = dot(xe_ref[0, q], ws_ref[...])
            for start in range(0, JOINTS, CUT):
                rows = slice(start * 2 * GROUP, (start + CUT) * 2 * GROUP)
                conv = conv_ref[0, q, rows, :]
                conv_kept[step, q, rows, :] = conv
                short = short_all[rows]
                half = conv * scale_conv + short * scale_short + shift
                turn = jnp.tanh(half)
                grow = (1.0 + turn).reshape(CUT, 2 * GROUP, C_OUT) * mask
                half = half.reshape(CUT, 2 * GROUP, C_OUT)
                turn = turn.reshape(CUT, 2 * GROUP, C_OUT)
                result = half * grow
                slope = grow * (1.0 + (half - half * turn))
                cot = jnp.concatenate(
                    [
                        jnp.concatenate(
                            [
                                cots[side, lane, start : start + CUT, pl.ds(q, GROUP, stride=4), :]
                                for lane in range(2)
                            ],
                            axis=2,
                        )
                        for side in range(2)
                    ],
                    axis=1,
                )
                for side in range(2):
                    for lane in range(2):
                        outs[
                            side, lane, start : start + CUT, pl.ds(q, GROUP, stride=4), :
                        ] = result[
                            :, side * GROUP : (side + 1) * GROUP, lane * HALF : (lane + 1) * HALF
                        ]
                up = (cot * slope).reshape(-1, C_OUT)
                up_kept[step, q, rows, :] = up
                sums[0] += fold(up)
                sums[1] += fold(up * conv)
                sums[2] += fold(up * short)
        for side in range(2):
            for joint in range(JOINTS):
                for lane in range(2):
                    o_ref[side, joint, :, lane * HALF : (lane + 1) * HALF] = outs[
                        side, lane, joint
                    ].astype(bf16)

    @pl.when(step == pairs - 1)
    def _():
        rows = [0.5 * jnp.sum(sums[k], axis=0, keepdims=True) for k in range(3)]
        rows.append(jnp.zeros((5, C_OUT), f32))
        await_greetings()
        total_ref[...] = sum_all(jnp.concatenate(rows, axis=0), sum_buffers)

    def gradients(pair, q):
        back_sum, back_conv, back_short = back_totals(total_ref[...], moments)
        count_out = stats[5:6]

        def terms(gain, mean, rstd, back):
            lead = gain * rstd
            slope = lead * rstd * back / count_out
            return lead, slope, lead * back_sum / count_out - slope * mean

        lead_c, slope_c, shift_c = terms(norm[2:3], mean_conv, rstd_conv, back_conv)
        lead_s, slope_s, shift_s = terms(norm[4:5], mean_short, rstd_short, back_short)
        mask = m_ref[0, 2 * q]
        mask = jnp.concatenate([mask, mask], axis=1)[None]
        half_c, half_s = 0.5 * lead_c, 0.5 * lead_s
        offset_c, offset_s = mask * shift_c, mask * shift_s
        short_all = dot(xe_ref[0, q], ws_ref[...])
        for start in range(0, JOINTS, CUT):
            rows = slice(start * 2 * GROUP, (start + CUT) * 2 * GROUP)
            up = up_kept[pair, q, rows, :]

            def taken(values, slope, offset):
                shifted = values.reshape(CUT, 2 * GROUP, C_OUT) * slope + offset
                return shifted.reshape(-1, C_OUT)

            cg = up * half_c - taken(conv_kept[pair, q, rows, :], slope_c, offset_c)
            cg_ref[0, q, rows, :] = cg.astype(bf16)
            for lane in range(2):
                edges[lane, rows, :] = cg[:, lane * HALF : (lane + 1) * HALF]
            sg = up * half_s - taken(short_all[rows], slope_s, offset_s)
            sg_ref[0, q, rows, :] = sg.astype(bf16)
        for lane in range(2):
            at = slice(lane * HALF, (lane + 1) * HALF)
            target = low_rims if q < 2 else high_rims
            outer = edges[lane, pl.ds(0 if q < 2 else 7, UNITS, stride=GROUP), :]
            target[pair, q % 2, 0:UNITS, at] = outer.astype(bf16)

    def turn_over():
        turned[:, 0 : 4 * ROWS] = cg_ref[0].reshape(4 * ROWS, C_OUT).T
        shg[...] += dot_tn(
            xe_ref[0].reshape(4 * ROWS, C_IN), sg_ref[0].reshape(4 * ROWS, C_OUT)
        )

    def taps_of(first, end):
        every = a_ref[0].reshape(16 * ROWS, C_OUT)
        for j in range(first, end):
            at = (8 * (j % 2) + j // 2) * ROWS
            tg[j] += dot(turned[...], every[at : at + DEPTH])

    @pl.when(step == pairs)
    def _():
        for q in range(4):
            gradients(0, q)
        turn_over()

    @pl.when((step > pairs) & (step < 2 * pairs))
    def _():
        for q in range(4):
            taps_of(2 * q, 2 * q + 2)
            gradients(step - pairs, q)
        taps_of(8, 9)
        turn_over()

    @pl.when((step >= pairs) & (step < 2 * pairs))
    def _():
        rims(step - pairs, "start")

    @pl.when(step == 2 * pairs)
    def _():
        taps_of(0, 9)
        for j in range(TAPS):
            grad_ref[j * C_OUT : (j + 1) * C_OUT, :] = tg[j].astype(bf16)
        grad_ref[TAPS * C_OUT : TAPS * C_OUT + C_IN, :] = shg[...].astype(bf16)
        rest = grad_ref.shape[0] - TAPS * C_OUT - C_IN
        if rest:
            grad_ref[TAPS * C_OUT + C_IN :, :] = jnp.zeros((rest, C_OUT), bf16)
        for pair in range(pairs):
            rims(pair, "wait")
        left_ref[...] = lefts[...]
        right_ref[...] = rights[...]


def padded(rows):
    unit = 16 * lax.axis_size("tm") * lax.axis_size("batch")
    return (rows + unit - 1) // unit * unit


class Places:
    def __init__(self, rows, cores):
        tm = lax.axis_index("tm")
        self.cores = cores
        self.core = tm % cores
        self.line = tm // cores
        self.lines = lax.axis_size("tm") // cores
        self.batch = lax.axis_index("batch")
        self.batches = lax.axis_size("batch")
        self.half = rows // cores
        self.part = self.half // self.lines
        self.piece = self.part // self.batches

    def core_peer(self):
        return {"tm": 2 * self.line + 1 - self.core}

    def line_peers(self):
        for d in range(1, self.lines):
            to = lax.rem(self.line + d, self.lines)
            yield d, to, {"tm": self.cores * to + self.core}

    def batch_peers(self):
        for d in range(1, self.batches):
            to = lax.rem(self.batch + d, self.batches)
            yield d, to, {"batch": to}

    def rows(self, index, count):
        return pl.ds(pl.multiple_of(index * count, 16), count)


def three_levels(rows, cores):
    lines, batches = lax.axis_size("tm") // cores, lax.axis_size("batch")
    half = rows // cores
    return lines, batches, half, half // lines, half // lines // batches


class Scatter(Places):
    def __init__(self, source, refs, cores=2):
        super().__init__(source.shape[0], cores)
        self.source = source
        self.here, self.up, self.out, self.firsts, self.seconds, self.thirds = refs[0:6]
        if cores == 1:
            self.here = source
        self.sems = refs[6:12]

    @staticmethod
    def scratch(rows, cores=2):
        lines, batches, half, part, piece = three_levels(rows, cores)
        core = half if cores == 2 else 16
        shapes = ((core,), (part,), (piece,), (core,), (lines, part), (batches, piece))
        found = [pltpu.VMEM((*shape, C_OUT), bf16) for shape in shapes]
        for count in (1, lines, batches):
            found += [pltpu.SemaphoreType.DMA((count,))] * 2
        return found

    def copies(self, level):
        sent, got = self.sems[2 * level], self.sems[2 * level + 1]
        if level == 0:
            source = self.source.at[self.rows(1 - self.core, self.half)]
            return [remote(source, self.firsts, sent.at[0], got.at[0], self.core_peer())]
        if level == 1:
            return [
                remote(
                    self.here.at[self.rows(to, self.part)], self.seconds.at[self.line],
                    sent.at[d], got.at[d], device,
                )
                for d, to, device in self.line_peers()
            ]
        return [
            remote(
                self.up.at[self.rows(to, self.piece)], self.thirds.at[self.batch],
                sent.at[d], got.at[d], device,
            )
            for d, to, device in self.batch_peers()
        ]

    def start(self, level):
        for copy in self.copies(level):
            copy.start()

    def end(self, level):
        for copy in self.copies(level):
            copy.wait()
        if level == 0:
            own = self.source[self.rows(self.core, self.half), :].astype(f32)
            self.here[...] = (own + self.firsts[...].astype(f32)).astype(bf16)
        if level == 1:
            own = self.here[self.rows(self.line, self.part), :].astype(f32)
            for d in range(1, self.lines):
                own = own + self.seconds[lax.rem(self.line + d, self.lines)].astype(f32)
            self.up[...] = own.astype(bf16)
        if level == 2:
            own = self.up[self.rows(self.batch, self.piece), :].astype(f32)
            for d in range(1, self.batches):
                own = own + self.thirds[lax.rem(self.batch + d, self.batches)].astype(f32)
            self.out[...] = own.astype(bf16)


class Gather(Places):
    def __init__(self, rows, refs, cores=2):
        super().__init__(rows, cores)
        self.gathered, self.joined, self.full = refs[0:3]
        self.sems = refs[3:9]

    @staticmethod
    def scratch(rows, cores=2):
        lines, batches, half, part, piece = three_levels(rows, cores)
        shapes = ((batches, piece), (lines, part), (cores, half))
        found = [pltpu.VMEM((*shape, C_OUT), bf16) for shape in shapes]
        for count in (batches, lines, 1):
            found += [pltpu.SemaphoreType.DMA((count,))] * 2
        return found

    def copies(self, level):
        sent, got = self.sems[2 * level], self.sems[2 * level + 1]
        if level == 0:
            slot = self.gathered.at[self.batch]
            peers_here = self.batch_peers()
        elif level == 1:
            slot = self.joined.at[self.line]
            peers_here = self.line_peers()
        else:
            slot = self.full.at[self.core]
            return [remote(slot, slot, sent.at[0], got.at[0], self.core_peer())]
        return [remote(slot, slot, sent.at[d], got.at[d], device) for d, _, device in peers_here]

    def start(self, level, share=None):
        if level == 0:
            self.gathered[self.batch] = share
        if level == 1:
            self.joined[self.line] = self.gathered[...].reshape(self.part, C_OUT)
        if level == 2:
            self.full[self.core] = self.joined[...].reshape(self.half, C_OUT)
        for copy in self.copies(level):
            copy.start()

    def end(self, level):
        for copy in self.copies(level):
            copy.wait()


def conv_back(
    cg_ref, left_ref, right_ref, taps_ref, h_ref, m_ref, st_ref, norm_ref, xq_ref, kron_ref, own_ref,
    grad_ref,
    hg_ref, out_ref, sum_ref, gg_ref,
    fills, ext, sums, fg, kept, raw, xg, gg, *buffers,
):
    step = pl.program_id(0)
    pairs = pl.num_programs(0) // 2
    scatter = Scatter(grad_ref, buffers[6:])
    stats = st_ref[...]
    norm = norm_ref[...]
    mean, rstd, scale, shift = first_moments(stats, norm)

    @pl.when(step == 0)
    def _():
        greet()
        sums[...] = jnp.zeros_like(sums)
        gg[...] = jnp.zeros_like(gg)

    half_scale, half_shift = 0.5 * scale, 0.5 * shift

    def extend():
        kept[step] = h_ref[0]
        for q in range(2):
            for lane in range(2):
                at = slice(lane * HALF, (lane + 1) * HALF)
                fills[q, lane, pl.ds(7, UNITS, stride=GROUP), :] = left_ref[
                    0, q, 0:UNITS, at
                ].astype(f32)
                fills[q, lane, pl.ds(0, UNITS, stride=GROUP), :] = right_ref[
                    0, q, 0:UNITS, at
                ].astype(f32)
        for q in range(4):
            ext[q + 2] = cg_ref[0, q]
            for start in range(0, JOINTS, CUT):
                rows = slice(start * 2 * GROUP, (start + CUT) * 2 * GROUP)
                tiles = cg_ref[0, q, rows, :].astype(f32).reshape(-1, GROUP, C_OUT)
                fill = jnp.concatenate([fills[q % 2, lane, rows, :] for lane in range(2)], axis=1)
                fill = fill.reshape(-1, GROUP, C_OUT)
                moved = insert_and_roll(tiles, fill, 7 if q >= 2 else 0)
                at = q - 2 if q >= 2 else q + 6
                ext[at, rows, :] = moved.reshape(-1, C_OUT).astype(bf16)

    def convolve(c):
        p, q = c % 2, c // 2
        total = None
        for i in range(5 - p):
            part = dot_nt(ext[4 - i + q], taps_ref[2 * i + p])
            total = part if total is None else total + part
        raw[c] = total

    def activate_back(c):
        mask = 0.5 * m_ref[0, c]
        mask = jnp.concatenate([mask, mask], axis=1)[None]
        for start in range(0, JOINTS, CUT):
            rows = slice(start * 2 * GROUP, (start + CUT) * 2 * GROUP)
            hidden = kept[step - 1, c, rows, :].astype(f32)
            half = hidden * half_scale + half_shift
            turn = jnp.tanh(half)
            slope = (1.0 + turn) * (1.0 + (half - half * turn))
            slope = (slope.reshape(CUT, 2 * GROUP, C_OUT) * mask).reshape(-1, C_OUT)
            grad = raw[c, rows, :] * slope
            fg[step - 1, c, rows, :] = grad
            sums[0] += fold(grad)
            sums[1] += fold(grad * hidden)

    order = (0, 2, 4, 6, 1, 3, 5, 7)

    @pl.when(step == 0)
    def _():
        extend()
        for c in order:
            convolve(c)

    @pl.when((step > 0) & (step < pairs))
    def _():
        extend()
        for c in order:
            activate_back(c)
            convolve(c)

    @pl.when(step == pairs)
    def _():
        for c in order:
            activate_back(c)

    @pl.when(step > pairs)
    def _():
        pair = step - pairs - 1
        count_in = stats[4:5]
        back_sum = out_ref[0:1]
        back_norm = rstd * (out_ref[1:2] - mean * back_sum)
        lead = norm[0:1] * rstd
        slope = lead * rstd * back_norm / count_in
        offset = lead * back_sum / count_in - slope * mean
        for c in range(PHASES):
            mask = m_ref[0, c]
            shifts = jnp.concatenate([mask, mask], axis=1)[None] * offset
            for start in range(0, JOINTS, CUT):
                rows = slice(start * 2 * GROUP, (start + CUT) * 2 * GROUP)
                hidden = kept[pair, c, rows, :].astype(f32)
                taken = hidden.reshape(CUT, 2 * GROUP, C_OUT) * slope + shifts
                taken = taken.reshape(-1, C_OUT)
                hg_ref[0, c, rows, :] = (fg[pair, c, rows, :] * lead - taken).astype(bf16)
            seen = xq_ref[0, c, 0:HALF_ROWS, :].astype(f32).reshape(JOINTS, GROUP, 2 * C_IN)
            parts = [seen[:, :, side * C_IN : (side + 1) * C_IN] for side in range(2)]
            xg[c] = mix_rows(parts, own_ref[...], kron_ref, xq_ref.at[0, c])
        gg[...] += dot_tn(
            xg[...].reshape(PHASES * ROWS, SUBSETS * C_IN),
            hg_ref[0].reshape(PHASES * ROWS, C_OUT),
        )

    @pl.when(step == 0)
    def _():
        await_greetings()
        scatter.start(0)

    for level, at in ((0, 1), (1, pairs - 2)):

        @pl.when(step == at)
        def _(level=level):
            scatter.end(level)
            scatter.start(level + 1)

    @pl.when(step == pairs)
    def _():
        rows = [jnp.sum(sums[k], axis=0, keepdims=True) for k in range(2)]
        rows.append(jnp.zeros((6, C_OUT), f32))
        out_ref[...] = sum_all(jnp.concatenate(rows, axis=0), buffers[0:6])

    @pl.when(step == 2 * pairs)
    def _():
        gg_ref[0 : SUBSETS * C_IN, :] = gg[...].astype(bf16)
        rest = gg_ref.shape[0] - SUBSETS * C_IN
        if rest:
            gg_ref[SUBSETS * C_IN :, :] = jnp.zeros((rest, C_OUT), bf16)
        scatter.end(2)
        sum_ref[...] = scatter.out[...]


def graph_back(
    hg_ref, xq_ref, sg_ref, wgt_ref, wst_ref, kront_ref, own_ref, piece_ref, grad_ref,
    ig_ref, taps_sum_ref, sum_ref, edge_ref,
    spread, staged, eg, own_grad, *buffers,
):
    step = pl.program_id(0)
    pairs = pl.num_programs(0) // 2
    total = Total(buffers[0:6])
    gather_taps = Gather(taps_sum_ref.shape[0], buffers[6:15])
    scatter = Scatter(grad_ref, buffers[15:27], 1)
    gather = Gather(grad_ref.shape[0], buffers[27:36], 1)

    @pl.when(step == 0)
    def _():
        greet()
        eg[...] = jnp.zeros_like(eg)
        own_grad[...] = jnp.zeros_like(own_grad)

    def side_by_side(values):
        return jnp.concatenate([values[:, 0:GROUP], values[:, GROUP : 2 * GROUP]], axis=2)

    own = own_ref[...]
    own = jnp.concatenate([own, own], axis=2)

    def spread_out(first):
        rest = jnp.zeros((C_OUT - HALF_ROWS, C_OUT), f32)
        found = None
        owned = None
        for c in range(first, first + 4):
            if c % 2 == 0:
                pair_back = dot(hg_ref[0, c : c + 2].reshape(2 * ROWS, C_OUT), wgt_ref[...])
                pair_back = pair_back.reshape(2, JOINTS, 2 * GROUP, SUBSETS * C_IN)
            back = pair_back[c % 2]
            for k in range(SUBSETS):
                both = side_by_side(back[:, :, k * C_IN : (k + 1) * C_IN])
                if k == 0:
                    seen = xq_ref[0, c, 0:HALF_ROWS, :].astype(f32)
                    part = seen.reshape(JOINTS, GROUP, 2 * C_IN) * both
                    owned = part if owned is None else owned + part
                both = jnp.concatenate([both.reshape(HALF_ROWS, 2 * C_IN), rest], axis=0)
                spread[step, c, k] = both.astype(bf16)
        for c in range(first, first + 4):
            both = spread[step, c, 1:3].reshape(2 * C_OUT, C_OUT)
            part = dot_nt(both, xq_ref[0, c])
            found = part if found is None else found + part
        eg[...] += found
        own_grad[...] += owned

    def mix_back(first):
        pair = step - pairs
        for c in range(first, first + 4):
            mixed = dot(kront_ref[...], spread[pair, c, 1:3].reshape(2 * C_OUT, C_OUT))
            direct = spread[pair, c, 0, 0:HALF_ROWS, :].astype(f32)
            result = mixed.reshape(JOINTS, GROUP, 2 * C_IN)
            result = result + direct.reshape(JOINTS, GROUP, 2 * C_IN) * own
            if c % 4 == 0:
                short = dot(sg_ref[0, c // 2 : c // 2 + 2].reshape(2 * ROWS, C_OUT), wst_ref[...])
                short = short.reshape(2, JOINTS, 2 * GROUP, C_IN)
            if c % 2 == 0:
                result = result + side_by_side(short[c % 4 // 2])
            staged[c] = result

    def put_natural():
        for side in range(2):
            lanes = slice(side * C_IN, (side + 1) * C_IN)
            for start in range(0, JOINTS, CUT):
                rows = [staged[c, start : start + CUT, :, lanes] for c in range(PHASES)]
                rows = jnp.swapaxes(jnp.stack(rows, axis=1), 1, 2)
                rows = rows.reshape(CUT, GROUP * PHASES, C_IN)
                ig_ref[side, start : start + CUT] = rows.astype(bf16)

    def pack_edges():
        lines = lax.broadcasted_iota(jnp.int32, (C_OUT, C_OUT), 0)
        spots = lax.broadcasted_iota(jnp.int32, (C_OUT, C_OUT), 1)
        same = lines % GROUP == spots % GROUP
        row = lax.broadcasted_iota(jnp.int32, (32, C_OUT), 0)
        col = lax.broadcasted_iota(jnp.int32, (32, C_OUT), 1)
        down = (row == col // GROUP).astype(f32)
        sums = jnp.sum(own_grad[...], axis=1)
        sums = jnp.sum(sums, axis=1, keepdims=True)
        row = lax.broadcasted_iota(jnp.int32, (JOINTS, 128), 0)
        col = lax.broadcasted_iota(jnp.int32, (JOINTS, 128), 1)
        packed = jnp.where(row == col, jnp.broadcast_to(sums, (JOINTS, 128)), 0.0)
        packed = jnp.concatenate([packed, jnp.zeros((32 - JOINTS, 128), f32)], axis=0)
        row = lax.broadcasted_iota(jnp.int32, (C_OUT, 128), 0)
        col = lax.broadcasted_iota(jnp.int32, (C_OUT, 128), 1)
        for k in range(2):
            kept = jnp.where(same, eg[k * C_OUT : (k + 1) * C_OUT, :], 0.0)
            narrow = lax.dot_general(
                down, kept, (((1,), (1,)), ((), ())),
                preferred_element_type=f32, precision=lax.Precision.HIGHEST,
            )
            place = (row // GROUP + 32 * (k + 1) == col).astype(f32)
            packed = packed + jnp.dot(
                narrow, place, preferred_element_type=f32, precision=lax.Precision.HIGHEST
            )
        return packed

    def begin():
        await_greetings()
        scatter.start(1)
        gather_taps.start(0, piece_ref[...])

    def second():
        scatter.end(1)
        scatter.start(2)

    def taps_second():
        gather_taps.end(0)
        gather_taps.start(1)

    def third():
        scatter.end(2)
        gather.start(0, scatter.out[...])
        total.start(0, pack_edges())

    def fourth():
        total.start(1, total.end(0))

    def fifth():
        gather.end(0)
        gather.start(1)

    def taps_third():
        gather_taps.end(1)
        gather_taps.start(2)

    def finish():
        edge_ref[...] = total.end(1)
        gather_taps.end(2)
        taps_sum_ref[...] = gather_taps.full[...].reshape(taps_sum_ref.shape)
        gather.end(1)
        sum_ref[...] = gather.joined[...].reshape(sum_ref.shape)

    schedule = {
        (3, 1): second,
        (4, 0): taps_second,
        (pairs - 1, 1): third,
        (pairs + 1, 1): fourth,
        (pairs + 2, 1): fifth,
        (pairs + 3, 0): taps_third,
        (2 * pairs - 1, 1): finish,
    }

    def advance(half):
        for (at, part), act in schedule.items():
            if part == half:
                pl.when(step == at)(act)

    pl.when(step == 2)(begin)

    @pl.when(step < pairs)
    def _():
        spread_out(0)

    @pl.when(step >= pairs)
    def _():
        mix_back(0)

    advance(0)

    @pl.when(step < pairs)
    def _():
        spread_out(4)

    @pl.when(step >= pairs)
    def _():
        mix_back(4)
        put_natural()

    advance(1)


def update(
    grads_ref, graph_grad_ref, edge_grad_ref, gm_ref, st_ref, cs_ref, bk_ref, fs_ref, ig_ref, o_ref,
    *refs,
):
    groups = [refs[4 * k : 4 * k + 4] for k in range(5)]
    out_ig, out_o, out_norm = refs[20:23]
    outs = [refs[23 + 4 * k : 27 + 4 * k] for k in range(5)]
    squares, norm_grad = refs[43:45]
    step = pl.program_id(0)
    taps_rows = TAPS * C_OUT

    def edge_grad(k):
        values = edge_grad_ref[...]
        if k:
            values = pltpu.roll(values, 128 - 32 * k, 1)
        return values[0:JOINTS, 0:JOINTS] * gm_ref[k]

    def apply(group, out, at, gradient, rate, decay):
        factor = squares[0:1, 0:1]
        new = adam_update(*[ref[at] for ref in group], gradient, factor, rate, decay)
        for ref, value in zip(out, new):
            ref[at] = value

    @pl.when(step == 0)
    def _():
        stats = st_ref[...]
        norm = groups[4][0][...]
        mean, rstd, _, _ = first_moments(stats, norm)
        first_sum = fs_ref[0:1]
        first_norm = rstd * (fs_ref[1:2] - mean * first_sum)
        back_sum, back_conv, back_short = back_totals(
            bk_ref[...], second_moments(stats, cs_ref[...])
        )
        norm_grad[...] = jnp.concatenate(
            [first_norm, first_sum, back_conv, back_sum, back_short, back_sum], axis=0
        )
        total = jnp.zeros((GROUP, C_OUT), f32)
        for start in range(0, taps_rows + C_IN, C_IN):
            rows = grads_ref[start : start + C_IN, :].astype(f32)
            total = total + fold(rows * rows)
        for start in range(0, SUBSETS * C_IN, C_IN):
            rows = graph_grad_ref[start : start + C_IN, :].astype(f32)
            total = total + fold(rows * rows)
        whole = jnp.sum(total) + jnp.sum(norm_grad[...] * norm_grad[...])
        for k in range(SUBSETS):
            values = edge_grad(k)
            whole = whole + jnp.sum(values * values)
        size = jnp.sqrt(jnp.full((GROUP, 128), whole, f32))
        squares[...] = jnp.minimum(1.0, clip_limit / (size + 1e-06))
        out_norm[0] = jnp.max(size)
        every = (slice(None), slice(None))
        apply(groups[4], outs[4], every, norm_grad[...], rate_small, 0.0)
        for k in range(SUBSETS):
            apply(groups[3], outs[3], k, edge_grad(k), rate_small, 0.0)

    for k in range(3):
        row = (3 * (step // 2) + k) * C_OUT
        lane = (step % 2) * C_IN
        at = (pl.ds(pl.multiple_of(row, C_OUT), C_OUT), pl.ds(pl.multiple_of(lane, C_IN), C_IN))
        apply(groups[1], outs[1], k, grads_ref[at].T.astype(f32), rate_matrix, decay_matrix)
    rows = graph_grad_ref[pl.ds(pl.multiple_of(step * 64, 64), 64), :].astype(f32)
    every = (slice(None), slice(None))
    apply(groups[0], outs[0], every, rows, rate_matrix, decay_matrix)

    @pl.when(step == 0)
    def _():
        rows = grads_ref[taps_rows : taps_rows + C_IN, :].astype(f32)
        every = (slice(None), slice(None))
        apply(groups[2], outs[2], every, rows, rate_matrix, decay_matrix)

    out_ig[...] = ig_ref[...]
    out_o[...] = o_ref[...]


def whole_spec(shape):
    return pl.BlockSpec(shape, lambda i: (0,) * len(shape))


def lead_spec(shape):
    return pl.BlockSpec(shape, lambda i: (i,) + (0,) * (len(shape) - 1))


def spec(block, index):
    return pl.BlockSpec(block, index)


def by_step(block):
    return spec(block, lambda i: (i,) + (0,) * (len(block) - 1))


def call(body, steps, ins, outs, scratch, name, **more):
    def to_spec(where, shape):
        if where is None:
            return whole_spec(shape)
        return where if isinstance(where, pl.BlockSpec) else by_step(where)

    return pl.pallas_call(
        body,
        grid=(steps,),
        in_specs=[to_spec(where, array.shape) for array, where in ins],
        out_specs=[to_spec(where, shape) for shape, _, where in outs],
        out_shape=[jax.ShapeDtypeStruct(shape, kind) for shape, kind, _ in outs],
        scratch_shapes=scratch,
        compiler_params=params(**more),
        name=name,
    )(*[array for array, _ in ins])


def shards(
    inputs, cotangent, lengths, frame_mask, subsets,
    graph_weight, graph_moment, graph_square, graph_average,
    temporal_weight, temporal_moment, temporal_square, temporal_average,
    shortcut_weight, shortcut_moment, shortcut_square, shortcut_average,
    edge_weight, edge_moment, edge_square, edge_average,
    norm_params, norm_moment, norm_square, norm_average,
):
    clips = inputs.shape[0]
    frames = inputs.shape[1]
    pairs = clips // 2
    natural = jnp.transpose(inputs, (0, 2, 1, 3))
    cot = jnp.transpose(cotangent, (0, 2, 1, 3))

    x_block = (2, JOINTS, frames, C_IN)
    mask_block = (1, PHASES, 2 * GROUP, 128)
    wide_block = (1, PHASES, ROWS, C_OUT)
    out_block = (1, 4, ROWS, C_OUT)
    xe_block = (1, 4, ROWS, C_IN)
    a_block = (1, 2, 8, ROWS, C_OUT)
    rim_block = (1, 2, 64, C_OUT)
    xq_block = (1, PHASES, C_OUT, C_OUT)
    cot_block = (2, JOINTS, frames // 2, C_OUT)
    edge_block = (1, JOINTS, 2 * GROUP, C_IN)
    end_block = (clips, JOINTS, 2 * GROUP, C_IN)
    small = (8, C_OUT)
    dma = pltpu.SemaphoreType.DMA

    def full(block):
        return (pairs,) + block[1:]

    def by_pair(block, pair):
        return spec(block, lambda i: (jnp.clip(pair(i), 0, pairs - 1),) + (0,) * (len(block) - 1))

    def early(block):
        return by_pair(block, lambda i: i)

    def behind(block):
        return by_pair(block, lambda i: i - 1)

    def late(block):
        return by_pair(block, lambda i: i - pairs)

    def later(block):
        return by_pair(block, lambda i: i - pairs - 1)

    given = (
        lengths, frame_mask, subsets, edge_weight, graph_weight, shortcut_weight, temporal_weight
    )
    taps_block = (TAPS // 3, C_OUT, C_OUT)
    shapes = [
        ((clips * frames, 128), f32),
        ((clips * GROUP, 128), f32),
        ((2 * HALF_ROWS, C_OUT), bf16),
        ((HALF_ROWS, 2 * C_OUT), bf16),
        ((JOINTS, GROUP, C_IN), f32),
        ((SUBSETS, JOINTS, JOINTS), f32),
        ((SUBSETS * C_IN, C_OUT), bf16),
        ((C_OUT, SUBSETS * C_IN), bf16),
        ((C_IN, C_OUT), bf16),
        ((C_OUT, C_IN), bf16),
        ((TAPS, C_OUT, C_OUT), bf16),
    ]
    masks, edge_masks, kron, kront, own, graph_mask, wg, wgt, ws, wst, taps = pl.pallas_call(
        prepare,
        grid=(3,),
        in_specs=[pl.BlockSpec(memory_space=pltpu.SMEM)]
        + [whole_spec(array.shape) for array in given[1:-1]]
        + [by_step(taps_block)],
        out_specs=[whole_spec(shape) for shape, _ in shapes[:-1]] + [by_step(taps_block)],
        out_shape=[jax.ShapeDtypeStruct(shape, kind) for shape, kind in shapes],
        compiler_params=pltpu.CompilerParams(vmem_limit_bytes=60 * 2**20),
        name="prepare",
    )(*given)
    masks = masks.reshape(pairs, PHASES, 2 * GROUP, 128)

    xq, xe, hidden, stats, rims, rim_mask = call(
        graph_forward,
        pairs + 1,
        [
            (natural, early(x_block)),
            (natural, pl.BlockSpec(memory_space=pl.ANY)),
            (masks, early(mask_block)),
            (edge_masks, None),
            (kron, None),
            (own, None),
            (wg, None),
            (ws, None),
        ],
        [
            (full(xq_block), bf16, early(xq_block)),
            (full(xe_block), bf16, early(xe_block)),
            (full(wide_block), bf16, behind(wide_block)),
            (small, f32, None),
            (full(edge_block), bf16, None),
            (edge_masks.shape, f32, None),
        ],
        [
            pltpu.VMEM((PHASES, 2, JOINTS, GROUP, C_IN), f32),
            pltpu.VMEM((PHASES, ROWS, SUBSETS * C_IN), bf16),
            pltpu.VMEM((4, ROWS, C_IN), bf16),
            pltpu.VMEM(end_block, bf16),
            pltpu.VMEM(end_block, bf16),
            dma((2,)),
            pltpu.VMEM((4, GROUP, C_OUT), f32),
            pltpu.VMEM((2, 2 * GROUP, 128), f32),
            pltpu.VMEM(full(edge_block), bf16),
            pltpu.VMEM(full(edge_block), bf16),
            pltpu.VMEM(full(edge_block), bf16),
            pltpu.VMEM(edge_masks.shape, f32),
            pltpu.VMEM(edge_masks.shape, f32),
        ]
        + [dma((2,))] * 4
        + sum_scratch(),
        "graph_forward",
        collective_id=1,
        has_side_effects=True,
    )

    active, conv, conv_stats = call(
        conv_forward,
        pairs,
        [
            (hidden, wide_block),
            (rims, edge_block),
            (masks, mask_block),
            (rim_mask, (2 * GROUP, 128)),
            (stats, None),
            (norm_params, None),
            (kron, None),
            (own, None),
            (wg, None),
            (taps, None),
        ],
        [
            (full(a_block), bf16, a_block),
            (full(out_block), f32, out_block),
            (small, f32, None),
        ],
        [
            pltpu.VMEM((C_OUT, C_OUT), bf16),
            pltpu.VMEM((2, ROWS, HALF), f32),
            pltpu.VMEM((4, 2, ROWS, HALF), f32),
            pltpu.VMEM((2, GROUP, C_OUT), f32),
        ]
        + sum_scratch(),
        "conv_forward",
        collective_id=2,
        has_side_effects=True,
    )

    def both_ways(block):
        return by_pair(block, lambda i: jnp.where(i < pairs, i, i - pairs))

    grad_rows = padded(TAPS * C_OUT + C_IN)
    outputs, conv_grad, short_grad, left_rim, right_rim, grads, back = call(
        middle,
        2 * pairs + 1,
        [
            (conv, early(out_block)),
            (xe, both_ways(xe_block)),
            (cot, early(cot_block)),
            (active, later(a_block)),
            (masks, both_ways(mask_block)),
            (stats, None),
            (conv_stats, None),
            (norm_params, None),
            (ws, None),
        ],
        [
            (cot.shape, bf16, early(cot_block)),
            (full(out_block), bf16, late(out_block)),
            (full(out_block), bf16, late(out_block)),
            (full(rim_block), bf16, None),
            (full(rim_block), bf16, None),
            ((grad_rows, C_OUT), bf16, None),
            (small, f32, None),
        ],
        [
            pltpu.VMEM((2, 2, JOINTS, frames // 2, HALF), f32),
            pltpu.VMEM((2, 2, JOINTS, frames // 2, HALF), f32),
            pltpu.VMEM((3, GROUP, C_OUT), f32),
            pltpu.VMEM(full(out_block), f32),
            pltpu.VMEM(full(out_block), f32),
            pltpu.VMEM((C_OUT, DEPTH), bf16),
            pltpu.VMEM((2, ROWS, HALF), f32),
            pltpu.VMEM((TAPS, C_OUT, C_OUT), f32),
            pltpu.VMEM((C_IN, C_OUT), f32),
        ]
        + [pltpu.VMEM(full(rim_block), bf16)] * 4
        + [dma((pairs,))] * 4
        + sum_scratch(),
        "middle",
        collective_id=3,
        has_side_effects=True,
    )

    graph_rows = padded(SUBSETS * C_IN)
    hidden_grad, first_sums, grad_piece, graph_grad = call(
        conv_back,
        2 * pairs + 1,
        [
            (conv_grad, early(out_block)),
            (left_rim, early(rim_block)),
            (right_rim, early(rim_block)),
            (taps, None),
            (hidden, early(wide_block)),
            (masks, by_pair(mask_block, lambda i: jnp.where(i <= pairs, i - 1, i - pairs - 1))),
            (stats, None),
            (norm_params, None),
            (xq, later(xq_block)),
            (kron, None),
            (own, None),
            (grads, None),
        ],
        [
            (full(wide_block), bf16, later(wide_block)),
            (small, f32, None),
            ((grad_rows // lax.axis_size(("tm", "batch")), C_OUT), bf16, None),
            ((graph_rows, C_OUT), bf16, None),
        ],
        [
            pltpu.VMEM((2, 2, ROWS, HALF), f32),
            pltpu.VMEM((8, ROWS, C_OUT), bf16),
            pltpu.VMEM((2, GROUP, C_OUT), f32),
            pltpu.VMEM(full(wide_block), f32),
            pltpu.VMEM(full(wide_block), bf16),
            pltpu.VMEM((PHASES, ROWS, C_OUT), f32),
            pltpu.VMEM((PHASES, ROWS, SUBSETS * C_IN), bf16),
            pltpu.VMEM((SUBSETS * C_IN, C_OUT), f32),
        ]
        + sum_scratch()
        + Scatter.scratch(grad_rows),
        "conv_back",
        collective_id=4,
        has_side_effects=True,
    )

    input_grad, grad_sums, graph_sum, edge_sum = call(
        graph_back,
        2 * pairs,
        [
            (hidden_grad, early(wide_block)),
            (xq, early(xq_block)),
            (short_grad, late(out_block)),
            (wgt, None),
            (wst, None),
            (kront, None),
            (own, None),
            (grad_piece, None),
            (graph_grad, None),
        ],
        [
            (natural.shape, bf16, late(x_block)),
            ((grad_rows, C_OUT), bf16, None),
            ((graph_rows, C_OUT), bf16, None),
            ((32, 128), f32, None),
        ],
        [
            pltpu.VMEM((pairs, PHASES, SUBSETS, C_OUT, C_OUT), bf16),
            pltpu.VMEM((PHASES, JOINTS, GROUP, 2 * C_IN), f32),
            pltpu.VMEM((2 * C_OUT, C_OUT), f32),
            pltpu.VMEM((JOINTS, GROUP, 2 * C_IN), f32),
        ]
        + sum_scratch((32, 128))
        + Gather.scratch(grad_rows)
        + Scatter.scratch(graph_rows, 1)
        + Gather.scratch(graph_rows, 1),
        "graph_back",
        collective_id=5,
        has_side_effects=True,
    )

    tap_spec = spec((TAPS // 3, C_IN, C_OUT), lambda i: (i // 2, i % 2, 0))
    graph_spec = spec((64, C_OUT), lambda i: (i % 2, i // 2))
    states = [
        (graph_weight, graph_moment, graph_square, graph_average),
        (temporal_weight, temporal_moment, temporal_square, temporal_average),
        (shortcut_weight, shortcut_moment, shortcut_square, shortcut_average),
        (edge_weight, edge_moment, edge_square, edge_average),
        (norm_params, norm_moment, norm_square, norm_average),
    ]
    places = [graph_spec, tap_spec, None, None, None]
    state_ins = [(array, place) for group, place in zip(states, places) for array in group]
    clip_spec = spec((clips // 6, JOINTS, frames, C_IN), lambda i: (i, 0, 0, 0))
    out_spec = spec((clips // 6, JOINTS, frames // 2, C_OUT), lambda i: (i, 0, 0, 0))
    new = call(
        update,
        6,
        [
            (grad_sums, None),
            (graph_sum, None),
            (edge_sum, None),
            (graph_mask, None),
            (stats, None),
            (conv_stats, None),
            (back, None),
            (first_sums, None),
            (input_grad, clip_spec),
            (outputs, out_spec),
        ]
        + state_ins,
        [(natural.shape, bf16, clip_spec), (cot.shape, bf16, out_spec), ((1,), f32, pl.BlockSpec(memory_space=pltpu.SMEM))]
        + [(array.shape, f32, place) for array, place in state_ins],
        [pltpu.VMEM((GROUP, 128), f32), pltpu.VMEM((6, C_OUT), f32)],
        "update",
    )
    return (
        jnp.transpose(new[1], (0, 2, 1, 3)),
        jnp.transpose(new[0], (0, 2, 1, 3)),
        new[2],
        *new[3:],
    )


def solution(mesh):
    rows = P("batch", "tm", None, None)
    in_specs = (rows, rows, P("batch"), P("batch", "tm")) + (P(),) * 21
    out_specs = (rows, rows) + (P(),) * 21
    return jax.shard_map(shards, mesh=mesh, in_specs=in_specs, out_specs=out_specs, check_vma=False)
```
